32 devices in a mesh: batch: 8 (over z, y), blk: 4 (over x, core).
Axes of the slice: x: 2, y: 2, z: 4, core: 2. Of those that a mesh axis runs over, the one named last changes fastest.
Arguments:
- inputs: bfloat16 [64, 512, 768], P('batch', 'blk'), may hold values from -6 to 6
- w_qkv: bfloat16 [768, 2304], P(('batch', 'blk')), may hold values from -0.21875 to 0.21875
- bias_query: bfloat16 [768], P(('batch', 'blk')), may hold values from -1.75 to 1.75
- bias_value: bfloat16 [768], P(('batch', 'blk')), may hold values from -1.75 to 1.75
- w_out: bfloat16 [768, 768], P(('batch', 'blk')), may hold values from -1.75 to 1.75
- bias_out: bfloat16 [768], P(('batch', 'blk')), may hold values from -1.75 to 1.75
- gain_first: bfloat16 [768], P(('batch', 'blk')), may hold values from 0.5 to 1.5
- shift_first: bfloat16 [768], P(('batch', 'blk')), may hold values from -1.75 to 1.75
- w_up: bfloat16 [768, 3072], P(('batch', 'blk')), may hold values from -0.21875 to 0.21875
- bias_up: bfloat16 [3072], P(('batch', 'blk')), may hold values from -1.75 to 1.75
- w_down: bfloat16 [3072, 768], P(('batch', 'blk')), may hold values from -0.109375 to 0.109375
- bias_down: bfloat16 [768], P(('batch', 'blk')), may hold values from -1.75 to 1.75
- gain_second: bfloat16 [768], P(('batch', 'blk')), may hold values from 0.5 to 1.5
- shift_second: bfloat16 [768], P(('batch', 'blk')), may hold values from -1.75 to 1.75
- dam_mask: int32 [12, 512, 512], P(None, 'blk'), may hold values from 0 to 1, as said below
- positions: int32 [64, 128], P('batch'), may hold values from -1 to 511, as said below
- counts: int32 [64], P('batch'), may hold values from 16 to 128, as said below
- cot_values: bfloat16 [64, 128, 768], P('batch'), may hold values from -6 to 6
Outputs:
- activations: bfloat16 [64, 512, 768], P('batch', 'blk')
- input_grad: float32 [64, 512, 768], P('batch', 'blk')
- grad_w_qkv: float32 [768, 2304], P(('batch', 'blk'))
- grad_bias_query: float32 [768], P(('batch', 'blk'))
- grad_bias_value: float32 [768], P(('batch', 'blk'))
- grad_w_out: float32 [768, 768], P(('batch', 'blk'))
- grad_bias_out: float32 [768], P(('batch', 'blk'))
- grad_gain_first: float32 [768], P(('batch', 'blk'))
- grad_shift_first: float32 [768], P(('batch', 'blk'))
- grad_w_up: float32 [768, 3072], P(('batch', 'blk'))
- grad_bias_up: float32 [3072], P(('batch', 'blk'))
- grad_w_down: float32 [3072, 768], P(('batch', 'blk'))
- grad_bias_down: float32 [768], P(('batch', 'blk'))
- grad_gain_second: float32 [768], P(('batch', 'blk'))
- grad_shift_second: float32 [768], P(('batch', 'blk'))
The draws below stay inside these ranges and needn't reach their ends.
Inputs may be any that keep to these rules, and one draw needn't show every extreme that they name: `dam_mask`: every head's mask is 1 on its diagonal. The first counts[s] entries of row s are distinct positions of sequence s; the remaining entries are -1. `counts`: some sequence has exactly 128 masked positions in every draw.
All inputs are finite; a program needn't handle non-finite values.
Results may differ from the reference program's by a relative error of at most 0.014.
Values may be sent and summed in bfloat16 or wider, within the bound.
No kernel may reach another device: no remote copies, remote signals or barrier semaphores. Data moves between devices by JAX's collectives and lax.ppermute only.
A program may use at most 192 MiB of HBM per device.

```python
import math
from functools import partial
import jax
import jax.numpy as jnp
from jax import lax

D = 768
H = 12
HD = 64
FF = 3072
SEQ = 512
MAXP = 128
QB = 128
SEQS = 64


def masked_lists(key):
    key_count, key_pick, key_order = jax.random.split(key, 3)
    least_count = MAXP // 8
    draws = jax.random.randint(key_count, (SEQS,), 0, 64)
    count_all = least_count + draws * draws * draws * (MAXP - least_count) // 250047
    chosen = jax.random.randint(key_pick, (), 0, SEQS)
    count_all = jnp.where(jnp.arange(SEQS) == chosen, MAXP, count_all).astype(jnp.int32)
    order_keys = jax.random.randint(key_order, (SEQS, SEQ), 0, 1 << 20) * SEQ + jnp.arange(SEQ)[None, :]
    ordered = jnp.argsort(order_keys, axis=1, stable=True)[:, :MAXP].astype(jnp.int32)
    slot_index = jnp.arange(MAXP)[None, :]
    listed = jnp.where(slot_index < count_all[:, None], ordered, -1).astype(jnp.int32)
    return (listed, count_all)


def draw_positions(key, part):
    return masked_lists(key)[0]


def draw_counts(key, part):
    return masked_lists(key)[1]


def draw_dam_mask(key, part):
    key = jax.random.fold_in(key, 11)
    key_tiles, key_full, key_density, key_cells = jax.random.split(key, 4)
    tiles = SEQ // QB
    tile_on = jax.random.randint(key_tiles, (H, tiles, tiles), 0, 10) < 6
    full_head = jax.random.randint(key_full, (), 0, H)
    tile_on = tile_on | (jnp.arange(H) == full_head)[:, None, None] | jnp.eye(tiles, dtype=bool)[None]
    density = jax.random.randint(key_density, (H, 1, 1), 30, 95)
    cells = jax.random.randint(key_cells, (H, SEQ, SEQ), 0, 100) < density
    spread = jnp.repeat(jnp.repeat(tile_on, QB, axis=1), QB, axis=2)
    return (spread & cells | jnp.eye(SEQ, dtype=bool)[None]).astype(jnp.int32)


def steps_of(stream_key, extent, cuts, low, top_value):
    loudness = 1.0
    for position, blocks in cuts:
        heights = jax.random.uniform(jax.random.fold_in(jax.random.fold_in(stream_key, 6), position), (blocks,), jnp.float32, low / len(cuts), top_value / len(cuts))
        loudness = loudness * jnp.repeat(jnp.exp(heights), extent[position] // blocks).reshape((-1,) + (1,) * (len(extent) - 1 - position))
    return loudness


def normal_values(key, extent, width, bound, cuts=(), kind=jnp.bfloat16):
    level = steps_of(key, extent, cuts, -0.22, 0.18) if cuts else 1.0
    array = jax.random.normal(key, extent, jnp.float32) * width * level
    return jnp.minimum(jnp.maximum(array, -bound), bound).astype(kind)


def setup_inputs(seed: int = 0) -> dict:
    arg_keys = jax.random.split(jax.random.key(seed), 19)
    inputs = normal_values(arg_keys[0], (SEQS, SEQ, D), 1.0, 6.0, ((0, 8), (1, 4)))
    w_qkv = normal_values(arg_keys[1], (D, 3 * D), D ** -0.5, 0.21875, ((0, 32),))
    bias_query = normal_values(arg_keys[2], (D,), 0.3, 1.75, ((0, 32),))
    bias_value = normal_values(arg_keys[3], (D,), 0.3, 1.75, ((0, 32),))
    w_out = normal_values(arg_keys[4], (D, D), (D // 64) ** -0.5, 1.75, ((0, 32),))
    bias_out = normal_values(arg_keys[5], (D,), 0.3, 1.75, ((0, 32),))
    gain_first = jnp.clip(1.0 + 0.1 * jax.random.normal(arg_keys[6], (D,), jnp.float32), 0.5, 1.5).astype(jnp.bfloat16)
    shift_first = normal_values(arg_keys[7], (D,), 0.3, 1.75, ((0, 32),))
    w_up = normal_values(arg_keys[8], (D, FF), D ** -0.5, 0.21875, ((0, 32),))
    bias_up = normal_values(arg_keys[9], (FF,), 0.3, 1.75, ((0, 32),))
    w_down = normal_values(arg_keys[10], (FF, D), FF ** -0.5, 0.109375, ((0, 32),))
    bias_down = normal_values(arg_keys[11], (D,), 0.3, 1.75, ((0, 32),))
    gain_second = jnp.clip(1.0 + 0.1 * jax.random.normal(arg_keys[12], (D,), jnp.float32), 0.5, 1.5).astype(jnp.bfloat16)
    shift_second = normal_values(arg_keys[13], (D,), 0.3, 1.75, ((0, 32),))
    dam_mask = draw_dam_mask(jax.random.fold_in(arg_keys[18], 71), 0)
    positions = draw_positions(jax.random.fold_in(arg_keys[18], 71), 0)
    counts = draw_counts(jax.random.fold_in(arg_keys[18], 71), 0)
    cot_values = normal_values(arg_keys[17], (SEQS, MAXP, D), 1.0, 6.0, ((0, 8),))
    return dict(inputs=inputs, w_qkv=w_qkv, bias_query=bias_query, bias_value=bias_value, w_out=w_out, bias_out=bias_out, gain_first=gain_first, shift_first=shift_first, w_up=w_up, bias_up=bias_up, w_down=w_down, bias_down=bias_down, gain_second=gain_second, shift_second=shift_second, dam_mask=dam_mask, positions=positions, counts=counts, cot_values=cot_values)


@jax.custom_vjp
def low(v):
    return lax.optimization_barrier(v.astype(jnp.bfloat16)).astype(jnp.float32)

@jax.custom_vjp
def low_back(v):
    return v

def low_keep(v):
    return (low(v), None)

def low_pass(kept, grad):
    return (grad,)

def back_keep(v):
    return (v, None)

def back_low(kept, grad):
    return (low(grad),)
low.defvjp(low_keep, low_pass)
low_back.defvjp(back_keep, back_low)
norm_eps = 1e-06
masked_score = -1e+30

def matmul(left, right):
    return jnp.dot(left, right, precision=lax.Precision.HIGHEST)

def layer_norm(token_rows, gain, shift):
    center = lax.optimization_barrier(jnp.mean(token_rows, axis=-1, keepdims=True))
    centered = token_rows - center
    spread = lax.optimization_barrier(jnp.mean(centered * centered, axis=-1, keepdims=True))
    return centered * lax.rsqrt(spread + norm_eps) * gain + shift

def attend(triple, allowed):
    queries, keys_all, values_all = triple
    scores = jnp.einsum('qhd,khd->hqk', queries, keys_all, precision=lax.Precision.HIGHEST)
    scores = low_back(scores * HD ** (-0.5))
    scores = jnp.where(allowed, scores, masked_score)
    row_top = lax.optimization_barrier(jnp.max(scores, axis=-1, keepdims=True))
    weights = jnp.exp(scores - row_top)
    probabilities = low(weights / lax.optimization_barrier(jnp.sum(weights, axis=-1, keepdims=True)))
    attended = jnp.einsum('hqk,khd->qhd', probabilities, values_all, precision=lax.Precision.HIGHEST)
    return attended.reshape(SEQ, D)

def block_forward(inputs, params, allowed):
    w_qkv, bias_query, bias_value, w_out, bias_out, gain_first, shift_first, w_up, bias_up, w_down, bias_down, gain_second, shift_second = params
    groups = inputs.shape[0]
    token_rows = inputs.reshape(groups * SEQ, D)
    joined = matmul(token_rows, w_qkv)
    queries = low(low_back(joined[:, :D] + bias_query))
    keys_all = low(low_back(joined[:, D:2 * D]))
    values_all = low(low_back(joined[:, 2 * D:] + bias_value))

    def heads_of(tensor):
        return tensor.reshape(groups, SEQ, H, HD)
    attended = lax.map(jax.checkpoint(partial(attend, allowed=allowed)), (heads_of(queries), heads_of(keys_all), heads_of(values_all)))
    attended = low(low_back(attended.reshape(groups * SEQ, D)))
    branch = low_back(matmul(attended, w_out) + bias_out)
    hidden = layer_norm(token_rows + branch, gain_first, shift_first)
    gate_in = low_back(matmul(low(hidden), w_up) + bias_up)
    active = low(jax.nn.gelu(gate_in, approximate=False))
    second = low_back(matmul(active, w_down) + bias_down)
    result = layer_norm(hidden + second, gain_second, shift_second)
    return result.reshape(groups, SEQ, D)

def reference(inputs, w_qkv, bias_query, bias_value, w_out, bias_out, gain_first, shift_first, w_up, bias_up, w_down, bias_down, gain_second, shift_second, dam_mask, positions, counts, cot_values):
    params = tuple((tensor.astype(jnp.float32) for tensor in (w_qkv, bias_query, bias_value, w_out, bias_out, gain_first, shift_first, w_up, bias_up, w_down, bias_down, gain_second, shift_second)))
    allowed = dam_mask > 0
    group = math.gcd(SEQS, max(1, 4096 // SEQ))
    rounds = SEQS // group
    input_groups = inputs.astype(jnp.float32).reshape(rounds, group, SEQ, D)
    position_groups = positions.reshape(rounds, group, MAXP)
    count_groups = counts.reshape(rounds, group)
    value_groups = cot_values.astype(jnp.float32).reshape(rounds, group, MAXP, D)

    def one_group(totals, pieces):
        input_part, position_part, count_part, value_part = pieces
        slots = jnp.arange(MAXP, dtype=jnp.int32)[None, :] < count_part[:, None]
        targets = jnp.where(slots, position_part, SEQ).astype(jnp.int32)
        sequence_index = jnp.broadcast_to(jnp.arange(group, dtype=jnp.int32)[:, None], (group, MAXP))
        upstream = jnp.zeros((group, SEQ, D), jnp.float32).at[sequence_index, targets].add(value_part, mode='drop')

        def forward_part(input_rows, weights_all):
            return block_forward(input_rows, weights_all, allowed)
        result, pullback = jax.vjp(forward_part, input_part, params)
        grad_input, grad_params = pullback(upstream)
        totals = jax.tree.map(jnp.add, totals, grad_params)
        return (totals, (result.astype(jnp.bfloat16), grad_input))
    zeros = tuple((jnp.zeros_like(tensor) for tensor in params))
    totals, (results, grad_inputs) = lax.scan(one_group, zeros, (input_groups, position_groups, count_groups, value_groups))
    return (results.reshape(SEQS, SEQ, D), grad_inputs.reshape(SEQS, SEQ, D), totals[0], totals[1], totals[2], totals[3], totals[4], totals[5], totals[6], totals[7], totals[8], totals[9], totals[10], totals[11], totals[12])
```

```python
from functools import partial

import jax
import jax.numpy as jnp
from jax import lax
from jax.sharding import PartitionSpec as P

norm_eps = 1e-06
masked_score = -1e30
f32 = jnp.float32
bf16 = jnp.bfloat16
both = ("batch", "blk")


def matmul(left, right):
    return jnp.dot(left, right, preferred_element_type=f32)


def matmul_left_t(left, right):
    return jnp.einsum("ti,tj->ij", left, right, preferred_element_type=f32)


def matmul_right_t(left, right):
    return jnp.einsum("tj,ij->ti", left, right, preferred_element_type=f32)


def norm_forward(token_rows, gain, shift):
    center = jnp.mean(token_rows, axis=-1, keepdims=True)
    centered = token_rows - center
    spread = jnp.mean(centered * centered, axis=-1, keepdims=True)
    inverse = lax.rsqrt(spread + norm_eps)
    normed = centered * inverse
    return (normed * gain + shift, normed, inverse)


def norm_backward(upstream, normed, inverse, gain):
    grad_gain = jnp.sum(upstream * normed, axis=0)
    grad_shift = jnp.sum(upstream, axis=0)
    scaled = upstream * gain
    inner = jnp.mean(scaled, axis=-1, keepdims=True)
    projected = jnp.mean(scaled * normed, axis=-1, keepdims=True)
    return (inverse * (scaled - inner - normed * projected), grad_gain, grad_shift)


class Grid:
    def __init__(self, mesh):
        batch, blk = mesh.shape["batch"], mesh.shape["blk"]
        self.sizes = {"z": batch // 2, "y": 2, "x": blk // 2, "c": 2}
        self.strides = {"c": 1, "x": 2, "y": blk, "z": 2 * blk}
        self.total = batch * blk
        self.blk = blk

    def digit(self, name):
        index = lax.axis_index("batch") * self.blk + lax.axis_index("blk")
        return (index // self.strides[name]) % self.sizes[name]

    def swap(self, array, name, delta=1):
        size, stride = self.sizes[name], self.strides[name]
        pairs = []
        for index in range(self.total):
            here = (index // stride) % size
            pairs.append((index, index + ((here ^ delta) - here) * stride))
        return lax.ppermute(array, both, pairs)

    def swap_blk(self, array, delta):
        pairs = [(index, index ^ delta) for index in range(self.total)]
        return lax.ppermute(array, both, pairs)


def place(parts, index):
    if len(parts) == 1:
        return parts[0][None]
    rows = []
    for target in range(len(parts)):
        row = parts[0]
        for delta in range(1, len(parts)):
            row = jnp.where(index == target ^ delta, parts[delta], row)
        rows.append(row)
    return jnp.stack(rows)


def pick(array, index):
    return lax.dynamic_index_in_dim(array, index, axis=0, keepdims=False)


def gather_rows(grid, shard):
    rows, cols = shard.shape
    half = cols // 2
    core = grid.digit("c")
    halves = jnp.stack([shard[:, :half], shard[:, half:]])
    mine, other = pick(halves, core), pick(halves, 1 - core)
    held = place([mine, grid.swap(other, "c")], core)
    for name in ("x", "z", "y"):
        parts = [held] + [grid.swap(held, name, d) for d in range(1, grid.sizes[name])]
        held = place(parts, grid.digit(name))
        if name == "y":
            held = jnp.moveaxis(held, 0, 1)
        held = held.reshape((-1,) + held.shape[2:]) if name == "x" else held
    held = held.reshape(grid.total * rows, half)
    back = grid.swap(held, "c")
    return jnp.concatenate(
        [jnp.where(core == 0, held, back), jnp.where(core == 0, back, held)], axis=1
    )


def add_low(*parts):
    total = parts[0].astype(f32)
    for part in parts[1:]:
        total = total + part.astype(f32)
    return total


def scatter_rows(grid, array):
    total_rows, cols = array.shape
    half = cols // 2
    rows = total_rows // grid.total
    core = grid.digit("c")
    low, high = array[:, :half], array[:, half:]
    kept = jnp.where(core == 0, low, high)
    sent = jnp.where(core == 0, high, low)
    held = add_low(kept, grid.swap(sent, "c")).astype(bf16)
    zs, ys, xs = grid.sizes["z"], grid.sizes["y"], grid.sizes["x"]
    held = held.reshape(zs, ys, xs * 2 * rows, half)
    where_y = grid.digit("y")
    kept = lax.dynamic_index_in_dim(held, where_y, axis=1, keepdims=False)
    sent = lax.dynamic_index_in_dim(held, 1 - where_y, axis=1, keepdims=False)
    held = add_low(kept, grid.swap(sent, "y")).astype(bf16)
    where_z = grid.digit("z")
    parts = [pick(held, where_z)]
    for delta in range(1, zs):
        parts.append(grid.swap(pick(held, where_z ^ delta), "z", delta))
    held = add_low(*parts).astype(bf16).reshape(xs, 2, rows, half)
    where_x = grid.digit("x")
    parts = [pick(held, where_x)]
    for delta in range(1, xs):
        parts.append(grid.swap(pick(held, where_x ^ delta), "x", delta))
    held = add_low(*parts).astype(bf16)
    mine = pick(held, core)
    back = grid.swap(pick(held, 1 - core), "c")
    return jnp.concatenate(
        [jnp.where(core == 0, mine, back), jnp.where(core == 0, back, mine)], axis=1
    ).astype(f32)


def split_heads(tensor, head_count):
    return tensor.reshape(tensor.shape[0], head_count, tensor.shape[1] // head_count)


def scores_of(queries, keys_all, addend, head_count):
    head_dim = queries.shape[1] // head_count
    scores = jnp.einsum(
        "qhd,khd->hqk",
        split_heads(queries, head_count),
        split_heads(keys_all, head_count),
        preferred_element_type=f32,
    ) * head_dim ** (-0.5)
    return scores + addend.astype(f32)


def attend_forward(triple, addend, head_count):
    queries, keys_all, values_all = triple
    scores = scores_of(queries, keys_all, addend, head_count)
    row_top = jnp.max(scores, axis=-1, keepdims=True)
    weights = jnp.exp(scores - row_top)
    totals = jnp.sum(weights, axis=-1, keepdims=True)
    probabilities = (weights / totals).astype(bf16)
    attended = jnp.einsum(
        "hqk,khd->qhd",
        probabilities,
        split_heads(values_all, head_count),
        preferred_element_type=f32,
    )
    return (attended.reshape(queries.shape[0], queries.shape[1]), row_top + jnp.log(totals))


def attend_backward(pieces, addend, head_count):
    queries, keys_all, values_all, log_totals, upstream = pieces
    head_dim = queries.shape[1] // head_count
    score_scale = head_dim ** (-0.5)
    scores = scores_of(queries, keys_all, addend, head_count)
    exact = jnp.exp(scores - log_totals)
    up_heads = split_heads(upstream, head_count)
    grad_probs = jnp.einsum(
        "qhd,khd->hqk", up_heads, split_heads(values_all, head_count), preferred_element_type=f32
    )
    inner = jnp.sum(grad_probs * exact, axis=-1, keepdims=True)
    grad_scores = (exact * (grad_probs - inner)).astype(bf16)
    grad_values = jnp.einsum("hqk,qhd->khd", exact.astype(bf16), up_heads, preferred_element_type=f32)
    grad_queries = (
        jnp.einsum(
            "hqk,khd->qhd", grad_scores, split_heads(keys_all, head_count), preferred_element_type=f32
        )
        * score_scale
    )
    grad_keys = (
        jnp.einsum(
            "hqk,qhd->khd", grad_scores, split_heads(queries, head_count), preferred_element_type=f32
        )
        * score_scale
    )
    width = queries.shape[1]
    return jnp.concatenate(
        [g.reshape(g.shape[0], width).astype(bf16) for g in (grad_queries, grad_keys, grad_values)],
        axis=1,
    )


def local(
    grid,
    inputs,
    w_qkv,
    bias_query,
    bias_value,
    w_out,
    bias_out,
    gain_first,
    shift_first,
    w_up,
    bias_up,
    w_down,
    bias_down,
    gain_second,
    shift_second,
    dam_mask,
    positions,
    counts,
    cot_values,
):
    groups, block_rows, width = inputs.shape
    head_count = dam_mask.shape[0]
    blk = grid.blk
    seqs = groups // blk
    length = blk * block_rows
    token_count = seqs * length
    here = lax.axis_index("blk")
    rows = w_qkv.shape[0]
    up_per = bias_up.shape[0] // rows

    by_home = inputs.reshape(blk, seqs, block_rows, width)
    parts = [pick(by_home, here)]
    for delta in range(1, blk):
        parts.append(grid.swap_blk(pick(by_home, here ^ delta), delta))

    pad_cols = 256
    vectors = (
        bias_query,
        bias_value,
        bias_out,
        gain_first,
        shift_first,
        bias_down,
        gain_second,
        shift_second,
    )
    columns = jnp.concatenate([jnp.stack(vectors, axis=1), bias_up.reshape(rows, up_per)], axis=1)
    columns = jnp.pad(columns, ((0, 0), (0, pad_cols - columns.shape[1])))
    first_group = gather_rows(grid, jnp.concatenate([w_qkv, columns], axis=1))

    addend = jnp.where(dam_mask > 0, 0.0, masked_score).astype(bf16)
    mask_parts = [addend, grid.swap(addend, "c")]
    far = grid.swap(addend, "x") if grid.sizes["x"] > 1 else None
    if far is not None:
        mask_parts += [far, grid.swap(far, "c")]
    second_group = gather_rows(grid, jnp.concatenate([w_out, w_up], axis=1))
    down_full = gather_rows(grid, w_down)

    qkv_full = first_group[:, : 3 * width]
    gathered = first_group[:, 3 * width :]
    vector_rows = gathered[:, : len(vectors)].T.astype(f32)
    (
        query_bias,
        value_bias,
        out_bias,
        gain_one,
        shift_one,
        down_bias,
        gain_two,
        shift_two,
    ) = [vector_rows[i] for i in range(len(vectors))]
    up_bias = gathered[:, len(vectors) : len(vectors) + up_per].reshape(-1).astype(f32)
    out_full = second_group[:, :width]
    up_full = second_group[:, width:]

    token_rows = place(parts, here).transpose(1, 0, 2, 3).reshape(token_count, width)
    addend_all = place(mask_parts, here).transpose(1, 0, 2, 3).reshape(head_count, length, length)

    joined = matmul(token_rows, qkv_full)
    queries = (joined[:, :width] + query_bias).astype(bf16).reshape(seqs, length, width)
    keys = joined[:, width : 2 * width].astype(bf16).reshape(seqs, length, width)
    values = (joined[:, 2 * width :] + value_bias).astype(bf16).reshape(seqs, length, width)
    attended, log_totals = lax.map(
        partial(attend_forward, addend=addend_all, head_count=head_count), (queries, keys, values)
    )
    attended = attended.reshape(token_count, width).astype(bf16)
    branch = matmul(attended, out_full) + out_bias
    first_sum = token_rows.astype(f32) + branch
    hidden, normed_first, inverse_first = norm_forward(first_sum, gain_one, shift_one)
    hidden_low = hidden.astype(bf16)
    gate_in = matmul(hidden_low, up_full) + up_bias
    active = jax.nn.gelu(gate_in, approximate=False).astype(bf16)
    second = matmul(active, down_full) + down_bias
    result, normed_second, inverse_second = norm_forward(hidden + second, gain_two, shift_two)

    def home(array):
        by_place = array.astype(bf16).reshape(seqs, blk, block_rows, width)
        got = [lax.dynamic_index_in_dim(by_place, here, axis=1, keepdims=False)]
        for delta in range(1, blk):
            sent = lax.dynamic_index_in_dim(by_place, here ^ delta, axis=1, keepdims=False)
            got.append(grid.swap_blk(sent, delta))
        return place(got, here).reshape(groups, block_rows, width)

    activations = home(result)

    my_positions = pick(positions.reshape(blk, seqs, -1), here)
    my_counts = pick(counts.reshape(blk, seqs), here)
    my_values = pick(cot_values.reshape((blk, seqs) + cot_values.shape[1:]), here)
    live = jnp.arange(positions.shape[1], dtype=jnp.int32)[None, :] < my_counts[:, None]
    picks = (
        my_positions[:, :, None] == jnp.arange(length, dtype=jnp.int32)[None, None, :]
    ) & live[:, :, None]
    upstream = jnp.einsum(
        "gpr,gpd->grd", picks.astype(bf16), my_values, preferred_element_type=f32
    ).reshape(token_count, width)
    grad_second_sum, grad_gain_second, grad_shift_second = norm_backward(
        upstream, normed_second, inverse_second, gain_two
    )
    grad_down_in = grad_second_sum.astype(bf16)
    grad_bias_down = jnp.sum(grad_down_in.astype(f32), axis=0)
    share_w_down = scatter_rows(grid, matmul_left_t(active, grad_down_in).astype(bf16))
    grad_active = matmul_right_t(grad_down_in, down_full)
    unused, gelu_pull = jax.vjp(partial(jax.nn.gelu, approximate=False), gate_in)
    grad_gate = gelu_pull(grad_active)[0].astype(bf16)
    grad_bias_up = jnp.sum(grad_gate.astype(f32), axis=0)
    grad_w_up = matmul_left_t(hidden_low, grad_gate).astype(bf16)
    grad_hidden = grad_second_sum + matmul_right_t(grad_gate, up_full)
    grad_first_sum, grad_gain_first, grad_shift_first = norm_backward(
        grad_hidden, normed_first, inverse_first, gain_one
    )
    grad_branch = grad_first_sum.astype(bf16)
    grad_bias_out = jnp.sum(grad_branch.astype(f32), axis=0)
    grad_w_out = matmul_left_t(attended, grad_branch).astype(bf16)
    share_second = scatter_rows(grid, jnp.concatenate([grad_w_out, grad_w_up], axis=1))
    grad_attended = matmul_right_t(grad_branch, out_full).astype(bf16).reshape(seqs, length, width)
    grad_joined = lax.map(
        partial(attend_backward, addend=addend_all, head_count=head_count),
        (queries, keys, values, log_totals, grad_attended),
    ).reshape(token_count, 3 * width)
    grad_bias_query = jnp.sum(grad_joined[:, :width].astype(f32), axis=0)
    grad_bias_value = jnp.sum(grad_joined[:, 2 * width :].astype(f32), axis=0)
    grad_w_qkv = matmul_left_t(token_rows, grad_joined).astype(bf16)
    vector_grads = (
        grad_bias_query,
        grad_bias_value,
        grad_bias_out,
        grad_gain_first,
        grad_shift_first,
        grad_bias_down,
        grad_gain_second,
        grad_shift_second,
    )
    columns = jnp.concatenate(
        [jnp.stack(vector_grads, axis=1), grad_bias_up.reshape(width, up_per)], axis=1
    )
    columns = jnp.pad(columns, ((0, 0), (0, pad_cols - columns.shape[1]))).astype(bf16)
    share_first = scatter_rows(grid, jnp.concatenate([grad_w_qkv, columns], axis=1))
    grad_inputs = home(grad_first_sum + matmul_right_t(grad_joined, qkv_full)).astype(f32)

    share_vectors = [share_first[:, 3 * width + i] for i in range(len(vectors))]
    share_bias_up = share_first[
        :, 3 * width + len(vectors) : 3 * width + len(vectors) + up_per
    ].reshape(-1)
    (
        share_bias_query,
        share_bias_value,
        share_bias_out,
        share_gain_first,
        share_shift_first,
        share_bias_down,
        share_gain_second,
        share_shift_second,
    ) = share_vectors
    return (
        activations,
        grad_inputs,
        share_first[:, : 3 * width],
        share_bias_query,
        share_bias_value,
        share_second[:, :width],
        share_bias_out,
        share_gain_first,
        share_shift_first,
        share_second[:, width:],
        share_bias_up,
        share_w_down,
        share_bias_down,
        share_gain_second,
        share_shift_second,
    )


def solution(mesh):
    sharded = P(both)
    rows = P(both, None)
    whole = P("batch", "blk", None)
    return jax.shard_map(
        partial(local, Grid(mesh)),
        mesh=mesh,
        in_specs=(
            whole,
            rows,
            sharded,
            sharded,
            rows,
            sharded,
            sharded,
            sharded,
            rows,
            sharded,
            rows,
            sharded,
            sharded,
            sharded,
            P(None, "blk", None),
            P("batch", None),
            P("batch"),
            P("batch", None, None),
        ),
        out_specs=(
            whole,
            whole,
            rows,
            sharded,
            sharded,
            rows,
            sharded,
            sharded,
            sharded,
            rows,
            sharded,
            rows,
            sharded,
            sharded,
            sharded,
        ),
        check_vma=False,
    )
```

```python
import math
from functools import partial

import jax
import jax.numpy as jnp
from jax import lax
from jax.experimental import pallas as pl
from jax.experimental.pallas import tpu as pltpu
from jax.sharding import PartitionSpec as P

norm_eps = 1e-06
masked_score = -1e30
f32 = jnp.float32
bf16 = jnp.bfloat16
both = ("batch", "blk")
log2e = math.log2(math.e)
roomy = pltpu.CompilerParams(vmem_limit_bytes=48 << 20)
vector_names = (
    "bias_query",
    "bias_value",
    "bias_out",
    "gain_first",
    "shift_first",
    "bias_down",
    "gain_second",
    "shift_second",
)
row_of = {name: index for index, name in enumerate(vector_names)}


def dot(left, right):
    return jnp.dot(left, right, preferred_element_type=f32)


def dot_right_t(left, right):
    return lax.dot_general(left, right, (((1,), (1,)), ((), ())), preferred_element_type=f32)


def dot_left_t(left, right):
    return lax.dot_general(left, right, (((0,), (0,)), ((), ())), preferred_element_type=f32)


def norm_stats(rows):
    center = jnp.mean(rows, axis=-1, keepdims=True)
    centered = rows - center
    inverse = lax.rsqrt(jnp.mean(centered * centered, axis=-1, keepdims=True) + norm_eps)
    return centered * inverse, inverse


def norm_pull(upstream, normed, inverse, gain):
    scaled = upstream * gain
    inner = jnp.mean(scaled, axis=-1, keepdims=True)
    projected = jnp.mean(scaled * normed, axis=-1, keepdims=True)
    return inverse * (scaled - inner - normed * projected)


def vector(ref, name):
    index = row_of[name]
    return ref[index : index + 1, :]


def add_sums(sums_ref, rows):
    total = jnp.concatenate(
        [jnp.sum(row, axis=0, keepdims=True) for row in rows]
        + [jnp.zeros((sums_ref.shape[0] - len(rows), sums_ref.shape[1]), f32)],
        axis=0,
    )

    @pl.when(pl.program_id(0) == 0)
    def _():
        sums_ref[...] = total

    @pl.when(pl.program_id(0) > 0)
    def _():
        sums_ref[...] += total


def piece_rows(here, piece, rows):
    return pl.ds(pl.multiple_of((here ^ piece) * rows, rows), rows)


def stack_pieces(ref, places):
    return jnp.concatenate([ref[place_, :] for place_ in places], axis=0)


def attend_kernel(head_dim, here_ref, q_ref, k_ref, v_ref, *rest):
    pieces, (o_ref, lse_ref) = rest[:-2], rest[-2:]
    here = here_ref[0]
    pair, seq = pl.program_id(0), pl.program_id(1)
    length, wide = q_ref.shape
    per = wide // head_dim
    rows = pieces[0].shape[1]
    lanes = lax.broadcasted_iota(jnp.int32, (1, wide), 1)
    log_lanes = lax.broadcasted_iota(jnp.int32, (1, lse_ref.shape[1]), 1)
    keys, values = k_ref[...], v_ref[...]
    for first in range(0, len(pieces), 2):
        span = range(first, min(first + 2, len(pieces)))
        places = [piece_rows(here, piece, rows) for piece in span]
        queries = stack_pieces(q_ref, places)
        out, logs = None, []
        for head in range(per):
            mine = lanes // head_dim == head
            scores = dot_right_t(jnp.where(mine, queries, 0), keys) * (head_dim**-0.5 * log2e)
            addend = jnp.concatenate([pieces[piece][head] for piece in span], axis=0)
            scores = scores + addend.astype(f32)
            top = jnp.max(scores, axis=1, keepdims=True)
            weights = jnp.exp2(scores - top)
            total = jnp.sum(weights, axis=1, keepdims=True)
            part = dot(weights.astype(bf16), values) * (1.0 / total)
            out = part if out is None else jnp.where(mine, part, out)
            logs.append(top + jnp.log2(total))
        for index, place_ in enumerate(places):
            here_rows = slice(index * rows, (index + 1) * rows)
            o_ref[place_, :] = out[here_rows].astype(bf16)
            start = seq * length + (here ^ span[index]) * rows
            log_place = pl.ds(pl.multiple_of(start, rows), rows)
            kept = lse_ref[log_place, :]
            for head in range(per):
                kept = jnp.where(log_lanes == pair * per + head, logs[head][here_rows], kept)
            lse_ref[log_place, :] = kept


def attend_back_kernel(head_dim, here_ref, q_ref, k_ref, v_ref, o_ref, g_ref, lse_ref, *rest):
    pieces, (dq_ref, dk_ref, dv_ref) = rest[:-3], rest[-3:]
    here = here_ref[0]
    pair, seq = pl.program_id(0), pl.program_id(1)
    length, wide = q_ref.shape
    per = wide // head_dim
    rows = pieces[0].shape[1]
    lanes = lax.broadcasted_iota(jnp.int32, (1, wide), 1)
    log_lanes = lax.broadcasted_iota(jnp.int32, (1, lse_ref.shape[1]), 1)
    keys, values = k_ref[...], v_ref[...]
    back = head_dim**-0.5
    dk = jnp.zeros(keys.shape, f32)
    dv = jnp.zeros(keys.shape, f32)
    for first in range(0, len(pieces), 2):
        span = range(first, min(first + 2, len(pieces)))
        places = [piece_rows(here, piece, rows) for piece in span]
        queries, ups = stack_pieces(q_ref, places), stack_pieces(g_ref, places)
        products = ups.astype(f32) * stack_pieces(o_ref, places).astype(f32)
        starts = [seq * length + (here ^ piece) * rows for piece in span]
        logs = stack_pieces(lse_ref, [pl.ds(pl.multiple_of(at, rows), rows) for at in starts])
        dq = None
        for head in range(per):
            mine = lanes // head_dim == head
            q_mine, g_mine = jnp.where(mine, queries, 0), jnp.where(mine, ups, 0)
            inner = jnp.sum(jnp.where(mine, products, 0.0), axis=1, keepdims=True)
            log = jnp.sum(
                jnp.where(log_lanes == pair * per + head, logs, 0.0), axis=1, keepdims=True
            )
            scores = dot_right_t(q_mine, keys) * (back * log2e)
            addend = jnp.concatenate([pieces[piece][head] for piece in span], axis=0)
            exact = jnp.exp2(scores + addend.astype(f32) - log)
            grads = (exact * (dot_right_t(g_mine, values) - inner)).astype(bf16)
            dv = dv + dot_left_t(exact.astype(bf16), g_mine)
            dk = dk + dot_left_t(grads, q_mine)
            part = dot(grads, keys)
            dq = part if dq is None else jnp.where(mine, part, dq)
        for index, place_ in enumerate(places):
            dq_ref[place_, :] = (dq[index * rows : (index + 1) * rows] * back).astype(bf16)
    dk_ref[...] = (dk * back).astype(bf16)
    dv_ref[...] = dv.astype(bf16)


def attention_call(kernel, here, per_head, logs, mask_parts, outs, seqs, head_count, cost):
    tokens = per_head[0][0].shape[0]
    rows, length = mask_parts[0].shape[1:]
    width = per_head[-1][0].shape[1] if len(per_head) > 3 else per_head[0][0].shape[1] // 3
    head_dim = width // head_count
    wide = 2 * head_dim

    def block(first):
        return pl.BlockSpec((length, wide), lambda p, s, h: (s, first + p))

    log_block = pl.BlockSpec((tokens, 128), lambda p, s, h: (0, 0))
    mask_block = pl.BlockSpec((2, rows, length), lambda p, s, h: (p, 0, 0))
    log_shape = jax.ShapeDtypeStruct((tokens, 128), f32)
    shapes = [jax.ShapeDtypeStruct((tokens, width), bf16)] * outs
    out_specs = [block(0)] * outs
    if logs is None:
        shapes.append(log_shape)
        out_specs.append(log_block)
    return pl.pallas_call(
        partial(kernel, head_dim),
        out_shape=shapes,
        grid_spec=pltpu.PrefetchScalarGridSpec(
            num_scalar_prefetch=1,
            grid=(width // wide, seqs),
            in_specs=[block(first) for unused, first in per_head]
            + ([] if logs is None else [log_block])
            + [mask_block] * len(mask_parts),
            out_specs=out_specs,
        ),
        compiler_params=roomy,
        cost_estimate=cost,
    )(here, *[array for array, unused in per_head], *([] if logs is None else [logs]), *mask_parts)


def attend(here, joined, mask_parts, seqs, head_count):
    tokens, width = joined.shape[0], joined.shape[1] // 3
    blocks = head_count // 2
    cells = tokens * mask_parts[0].shape[2] * head_count
    return attention_call(
        attend_kernel,
        here,
        [(joined, 0), (joined, blocks), (joined, 2 * blocks)],
        None,
        mask_parts,
        1,
        seqs,
        head_count,
        pl.CostEstimate(flops=cells * 3000, bytes_accessed=tokens * width * 16, transcendentals=cells),
    )


def attend_back(here, joined, attended, upstream, logs, mask_parts, seqs, head_count):
    tokens, width = attended.shape
    blocks = head_count // 2
    cells = tokens * mask_parts[0].shape[2] * head_count
    return attention_call(
        attend_back_kernel,
        here,
        [(joined, 0), (joined, blocks), (joined, 2 * blocks), (attended, 0), (upstream, 0)],
        logs,
        mask_parts,
        3,
        seqs,
        head_count,
        pl.CostEstimate(flops=cells * 4500, bytes_accessed=tokens * width * 24, transcendentals=cells),
    )


def out_kernel(att_ref, w_ref, x_ref, vec_ref, first_ref, low_ref):
    first = x_ref[...].astype(f32) + (dot(att_ref[...], w_ref[...]) + vector(vec_ref, "bias_out"))
    first_ref[...] = first
    gain, shift = vector(vec_ref, "gain_first"), vector(vec_ref, "shift_first")
    low_ref[...] = (norm_stats(first)[0] * gain + shift).astype(bf16)


def whole_block(array):
    return pl.BlockSpec(array.shape, lambda *unused: (0,) * array.ndim)


def out_projection(attended, w_out, token_rows, vectors, block):
    tokens, width = attended.shape
    row = pl.BlockSpec((block, width), lambda i: (i, 0))
    return pl.pallas_call(
        out_kernel,
        out_shape=(
            jax.ShapeDtypeStruct((tokens, width), f32),
            jax.ShapeDtypeStruct((tokens, width), bf16),
        ),
        grid=(tokens // block,),
        in_specs=[row, whole_block(w_out), row, whole_block(vectors)],
        out_specs=(row, row),
        compiler_params=roomy,
        cost_estimate=pl.CostEstimate(
            flops=4 * tokens * width * width, bytes_accessed=tokens * width * 10, transcendentals=0
        ),
    )(attended, w_out, token_rows, vectors)


def up_kernel(chunk, h_ref, w_ref, b_ref, act_ref, der_ref):
    weights, bias = w_ref[...], b_ref[...]
    for first in range(0, h_ref.shape[0], chunk):
        place_ = slice(first, first + chunk)
        gate = dot(h_ref[place_, :], weights) + bias
        share = 0.5 + 0.5 * lax.erf(gate * math.sqrt(0.5))
        bell = jnp.exp2((-0.5 * log2e) * (gate * gate)) * (1.0 / math.sqrt(2.0 * math.pi))
        act_ref[place_, :] = (gate * share).astype(bf16)
        der_ref[place_, :] = (share + gate * bell).astype(bf16)


def up_projection(hidden_low, w_up, bias, block):
    tokens, width = hidden_low.shape
    cols = w_up.shape[1]
    out = pl.BlockSpec((tokens, block), lambda j: (0, j))
    shape = jax.ShapeDtypeStruct((tokens, cols), bf16)
    return pl.pallas_call(
        partial(up_kernel, 128),
        out_shape=(shape, shape),
        grid=(cols // block,),
        in_specs=[
            whole_block(hidden_low),
            pl.BlockSpec((width, block), lambda j: (0, j)),
            pl.BlockSpec((1, block), lambda j: (0, j)),
        ],
        out_specs=(out, out),
        compiler_params=roomy,
        cost_estimate=pl.CostEstimate(
            flops=5 * tokens * width * cols,
            bytes_accessed=tokens * cols * 4,
            transcendentals=2 * tokens * cols,
        ),
    )(hidden_low, w_up, bias)


def down_kernel(
    steps_per_seq,
    here_ref,
    pos_ref,
    cot_ref,
    act_ref,
    der_ref,
    first_ref,
    w_ref,
    vec_ref,
    out_ref,
    gss_ref,
    gdi_ref,
    gate_ref,
    sums_ref,
    up_sum_ref,
):
    step = pl.program_id(0)
    block = act_ref.shape[0]
    normed_one = norm_stats(first_ref[...])[0]
    hidden = normed_one * vector(vec_ref, "gain_first") + vector(vec_ref, "shift_first")
    second = hidden + (dot(act_ref[...], w_ref[...]) + vector(vec_ref, "bias_down"))
    normed, inverse = norm_stats(second)
    gain = vector(vec_ref, "gain_second")
    out_ref[...] = (normed * gain + vector(vec_ref, "shift_second")).astype(bf16)
    slots = pos_ref.shape[-1]
    token = lax.broadcasted_iota(jnp.int32, (block, slots), 0) + (step % steps_per_seq) * block
    picks = jnp.where(token == pos_ref[0], 1.0, 0.0).astype(bf16)
    upstream = dot(picks, cot_ref[0])
    grad = norm_pull(upstream, normed, inverse, gain)
    gss_ref[...] = grad
    low = grad.astype(bf16)
    gdi_ref[...] = low
    add_sums(sums_ref, [low.astype(f32), upstream * normed, upstream])
    grad_gate = (dot_right_t(low, w_ref[...]) * der_ref[...].astype(f32)).astype(bf16)
    gate_ref[...] = grad_gate
    add_sums(up_sum_ref, [grad_gate.astype(f32)])


def down_projection(here, active, slope, first_sum, w_down, vectors, marks, cot_values, seqs, block):
    tokens, cols = active.shape
    width = w_down.shape[1]
    steps = tokens // seqs // block
    slots = marks.shape[-1]
    row = pl.BlockSpec((block, width), lambda i, h: (i, 0))
    wide = pl.BlockSpec((block, cols), lambda i, h: (i, 0))
    sums = jax.ShapeDtypeStruct((8, width), f32)
    up_sums = jax.ShapeDtypeStruct((8, cols), f32)
    return pl.pallas_call(
        partial(down_kernel, steps),
        out_shape=(
            jax.ShapeDtypeStruct((tokens, width), bf16),
            jax.ShapeDtypeStruct((tokens, width), f32),
            jax.ShapeDtypeStruct((tokens, width), bf16),
            jax.ShapeDtypeStruct((tokens, cols), bf16),
            sums,
            up_sums,
        ),
        grid_spec=pltpu.PrefetchScalarGridSpec(
            num_scalar_prefetch=1,
            grid=(tokens // block,),
            in_specs=[
                pl.BlockSpec((1, 1, slots), lambda i, h: (i // steps, 0, 0)),
                pl.BlockSpec((1, slots, width), lambda i, h: (h[0] * seqs + i // steps, 0, 0)),
                wide,
                wide,
                row,
                whole_block(w_down),
                whole_block(vectors),
            ],
            out_specs=(row, row, row, wide, whole_block(sums), whole_block(up_sums)),
        ),
        compiler_params=roomy,
        cost_estimate=pl.CostEstimate(
            flops=6 * tokens * width * cols, bytes_accessed=tokens * cols * 8, transcendentals=0
        ),
    )(here, marks, cot_values, active, slope, first_sum, w_down, vectors)


def first_back_kernel(
    gate_ref, gss_ref, first_ref, w_up_ref, w_out_ref, vec_ref, gfs_ref, branch_ref, att_ref, sums_ref
):
    grad_hidden = gss_ref[...] + dot_right_t(gate_ref[...], w_up_ref[...])
    normed, inverse = norm_stats(first_ref[...])
    grad = norm_pull(grad_hidden, normed, inverse, vector(vec_ref, "gain_first"))
    gfs_ref[...] = grad
    low = grad.astype(bf16)
    branch_ref[...] = low
    att_ref[...] = dot_right_t(low, w_out_ref[...]).astype(bf16)
    add_sums(sums_ref, [low.astype(f32), grad_hidden * normed, grad_hidden])


def first_back(grad_gate, grad_second_sum, first_sum, w_up, w_out, vectors, block):
    tokens, cols = grad_gate.shape
    width = w_out.shape[0]
    row = pl.BlockSpec((block, width), lambda i: (i, 0))
    sums = jax.ShapeDtypeStruct((8, width), f32)
    low = jax.ShapeDtypeStruct((tokens, width), bf16)
    return pl.pallas_call(
        first_back_kernel,
        out_shape=(jax.ShapeDtypeStruct((tokens, width), f32), low, low, sums),
        grid=(tokens // block,),
        in_specs=[
            pl.BlockSpec((block, cols), lambda i: (i, 0)),
            row,
            row,
            whole_block(w_up),
            whole_block(w_out),
            whole_block(vectors),
        ],
        out_specs=(row, row, row, whole_block(sums)),
        compiler_params=roomy,
        cost_estimate=pl.CostEstimate(
            flops=4 * tokens * width * cols, bytes_accessed=tokens * cols * 4, transcendentals=0
        ),
    )(grad_gate, grad_second_sum, first_sum, w_up, w_out, vectors)


def matmul(left, right):
    return jnp.dot(left, right, preferred_element_type=f32)


def matmul_left_t(left, right):
    return jnp.einsum("ti,tj->ij", left, right, preferred_element_type=f32)


def matmul_right_t(left, right):
    return jnp.einsum("tj,ij->ti", left, right, preferred_element_type=f32)


class Grid:
    def __init__(self, mesh):
        batch, blk = mesh.shape["batch"], mesh.shape["blk"]
        self.sizes = {"z": batch // 2, "y": 2, "x": blk // 2, "c": 2}
        self.strides = {"c": 1, "x": 2, "y": blk, "z": 2 * blk}
        self.total = batch * blk
        self.blk = blk

    def digit(self, name):
        index = lax.axis_index("batch") * self.blk + lax.axis_index("blk")
        return (index // self.strides[name]) % self.sizes[name]

    def swap(self, array, name, delta=1):
        size, stride = self.sizes[name], self.strides[name]
        pairs = []
        for index in range(self.total):
            here = (index // stride) % size
            pairs.append((index, index + ((here ^ delta) - here) * stride))
        return lax.ppermute(array, both, pairs)

    def swap_blk(self, array, delta):
        pairs = [(index, index ^ delta) for index in range(self.total)]
        return lax.ppermute(array, both, pairs)


def place(parts, index):
    if len(parts) == 1:
        return parts[0][None]
    rows = []
    for target in range(len(parts)):
        row = parts[0]
        for delta in range(1, len(parts)):
            row = jnp.where(index == target ^ delta, parts[delta], row)
        rows.append(row)
    return jnp.stack(rows)


def pick(array, index):
    return lax.dynamic_index_in_dim(array, index, axis=0, keepdims=False)


def gather_rows(grid, shard):
    rows, cols = shard.shape
    half = cols // 2
    core = grid.digit("c")
    halves = jnp.stack([shard[:, :half], shard[:, half:]])
    mine, other = pick(halves, core), pick(halves, 1 - core)
    held = place([mine, grid.swap(other, "c")], core)
    for name in ("x", "z", "y"):
        parts = [held] + [grid.swap(held, name, d) for d in range(1, grid.sizes[name])]
        held = place(parts, grid.digit(name))
        if name == "y":
            held = jnp.moveaxis(held, 0, 1)
        held = held.reshape((-1,) + held.shape[2:]) if name == "x" else held
    held = held.reshape(grid.total * rows, half)
    back = grid.swap(held, "c")
    return jnp.concatenate(
        [jnp.where(core == 0, held, back), jnp.where(core == 0, back, held)], axis=1
    )


def add_low(*parts):
    total = parts[0].astype(f32)
    for part in parts[1:]:
        total = total + part.astype(f32)
    return total


def scatter_rows(grid, array):
    total_rows, cols = array.shape
    half = cols // 2
    rows = total_rows // grid.total
    core = grid.digit("c")
    low, high = array[:, :half], array[:, half:]
    kept = jnp.where(core == 0, low, high)
    sent = jnp.where(core == 0, high, low)
    held = add_low(kept, grid.swap(sent, "c")).astype(bf16)
    zs, ys, xs = grid.sizes["z"], grid.sizes["y"], grid.sizes["x"]
    held = held.reshape(zs, ys, xs * 2 * rows, half)
    where_y = grid.digit("y")
    kept = lax.dynamic_index_in_dim(held, where_y, axis=1, keepdims=False)
    sent = lax.dynamic_index_in_dim(held, 1 - where_y, axis=1, keepdims=False)
    held = add_low(kept, grid.swap(sent, "y")).astype(bf16)
    where_z = grid.digit("z")
    parts = [pick(held, where_z)]
    for delta in range(1, zs):
        parts.append(grid.swap(pick(held, where_z ^ delta), "z", delta))
    held = add_low(*parts).astype(bf16).reshape(xs, 2, rows, half)
    where_x = grid.digit("x")
    parts = [pick(held, where_x)]
    for delta in range(1, xs):
        parts.append(grid.swap(pick(held, where_x ^ delta), "x", delta))
    held = add_low(*parts).astype(bf16)
    mine = pick(held, core)
    back = grid.swap(pick(held, 1 - core), "c")
    return jnp.concatenate(
        [jnp.where(core == 0, mine, back), jnp.where(core == 0, back, mine)], axis=1
    ).astype(f32)


def local(
    grid,
    inputs,
    w_qkv,
    bias_query,
    bias_value,
    w_out,
    bias_out,
    gain_first,
    shift_first,
    w_up,
    bias_up,
    w_down,
    bias_down,
    gain_second,
    shift_second,
    dam_mask,
    positions,
    counts,
    cot_values,
):
    groups, block_rows, width = inputs.shape
    head_count = dam_mask.shape[0]
    blk = grid.blk
    seqs = groups // blk
    length = blk * block_rows
    token_count = seqs * length
    here = lax.axis_index("blk")
    rows = w_qkv.shape[0]
    up_per = bias_up.shape[0] // rows

    by_home = inputs.reshape(blk, seqs, block_rows, width)
    parts = [pick(by_home, here)]
    for delta in range(1, blk):
        parts.append(grid.swap_blk(pick(by_home, here ^ delta), delta))

    pad_cols = 256
    vectors = (
        bias_query,
        bias_value,
        bias_out,
        gain_first,
        shift_first,
        bias_down,
        gain_second,
        shift_second,
    )
    columns = jnp.concatenate([jnp.stack(vectors, axis=1), bias_up.reshape(rows, up_per)], axis=1)
    columns = jnp.pad(columns, ((0, 0), (0, pad_cols - columns.shape[1])))
    first_group = gather_rows(grid, jnp.concatenate([w_qkv, columns], axis=1))

    addend = jnp.where(dam_mask > 0, 0.0, masked_score).astype(bf16)
    mask_parts = [addend, grid.swap(addend, "c")]
    far = grid.swap(addend, "x") if grid.sizes["x"] > 1 else None
    if far is not None:
        mask_parts += [far, grid.swap(far, "c")]
    second_group = gather_rows(grid, jnp.concatenate([w_out, w_up], axis=1))
    down_full = gather_rows(grid, w_down)

    qkv_full = first_group[:, : 3 * width]
    gathered = first_group[:, 3 * width :]
    vector_rows = gathered[:, : len(vectors)].T.astype(f32)
    up_bias = gathered[:, len(vectors) : len(vectors) + up_per].reshape(1, -1).astype(f32)
    out_full = second_group[:, :width]
    up_full = second_group[:, width:]

    token_rows = place(parts, here).transpose(1, 0, 2, 3).reshape(token_count, width)
    joined_bias = jnp.concatenate(
        [vector_rows[0], jnp.zeros((width,), f32), vector_rows[1]], axis=0
    )
    joined = (matmul(token_rows, qkv_full) + joined_bias).astype(bf16)
    here_1 = here.reshape(1).astype(jnp.int32)
    attended, logs = attend(here_1, joined, mask_parts, seqs, head_count)
    block = min(256, length)
    first_sum, hidden_low = out_projection(attended, out_full, token_rows, vector_rows, block)
    active, slope = up_projection(hidden_low, up_full, up_bias, min(512, up_full.shape[1]))

    my_positions = pick(positions.reshape(blk, seqs, -1), here)
    my_counts = pick(counts.reshape(blk, seqs), here)
    live = jnp.arange(positions.shape[1], dtype=jnp.int32)[None, :] < my_counts[:, None]
    marks = jnp.where(live, my_positions, -1)[:, None, :]
    result, grad_second_sum, grad_down_in, grad_gate, second_sums, up_sums = down_projection(
        here_1, active, slope, first_sum, down_full, vector_rows, marks, cot_values, seqs, block
    )
    grad_bias_down, grad_gain_second, grad_shift_second = second_sums[:3]
    grad_bias_up = up_sums[0]

    def home(array):
        by_place = array.astype(bf16).reshape(seqs, blk, block_rows, width)
        got = [lax.dynamic_index_in_dim(by_place, here, axis=1, keepdims=False)]
        for delta in range(1, blk):
            sent = lax.dynamic_index_in_dim(by_place, here ^ delta, axis=1, keepdims=False)
            got.append(grid.swap_blk(sent, delta))
        return place(got, here).reshape(groups, block_rows, width)

    activations = home(result)

    share_w_down = scatter_rows(grid, matmul_left_t(active, grad_down_in).astype(bf16))
    grad_w_up = matmul_left_t(hidden_low, grad_gate).astype(bf16)
    grad_first_sum, grad_branch, grad_attended, first_sums = first_back(
        grad_gate, grad_second_sum, first_sum, up_full, out_full, vector_rows, block
    )
    grad_bias_out, grad_gain_first, grad_shift_first = first_sums[:3]
    grad_w_out = matmul_left_t(attended, grad_branch).astype(bf16)
    share_second = scatter_rows(grid, jnp.concatenate([grad_w_out, grad_w_up], axis=1))
    grad_joined = jnp.concatenate(
        attend_back(
            here_1, joined, attended, grad_attended, logs, mask_parts, seqs, head_count
        ),
        axis=1,
    )
    grad_bias_query = jnp.sum(grad_joined[:, :width].astype(f32), axis=0)
    grad_bias_value = jnp.sum(grad_joined[:, 2 * width :].astype(f32), axis=0)
    grad_w_qkv = matmul_left_t(token_rows, grad_joined).astype(bf16)
    vector_grads = (
        grad_bias_query,
        grad_bias_value,
        grad_bias_out,
        grad_gain_first,
        grad_shift_first,
        grad_bias_down,
        grad_gain_second,
        grad_shift_second,
    )
    columns = jnp.concatenate(
        [jnp.stack(vector_grads, axis=1), grad_bias_up.reshape(width, up_per)], axis=1
    )
    columns = jnp.pad(columns, ((0, 0), (0, pad_cols - columns.shape[1]))).astype(bf16)
    share_first = scatter_rows(grid, jnp.concatenate([grad_w_qkv, columns], axis=1))
    grad_inputs = home(grad_first_sum + matmul_right_t(grad_joined, qkv_full)).astype(f32)

    share_vectors = [share_first[:, 3 * width + i] for i in range(len(vectors))]
    share_bias_up = share_first[
        :, 3 * width + len(vectors) : 3 * width + len(vectors) + up_per
    ].reshape(-1)
    (
        share_bias_query,
        share_bias_value,
        share_bias_out,
        share_gain_first,
        share_shift_first,
        share_bias_down,
        share_gain_second,
        share_shift_second,
    ) = share_vectors
    return (
        activations,
        grad_inputs,
        share_first[:, : 3 * width],
        share_bias_query,
        share_bias_value,
        share_second[:, :width],
        share_bias_out,
        share_gain_first,
        share_shift_first,
        share_second[:, width:],
        share_bias_up,
        share_w_down,
        share_bias_down,
        share_gain_second,
        share_shift_second,
    )


def solution(mesh):
    sharded = P(both)
    rows = P(both, None)
    whole = P("batch", "blk", None)
    return jax.shard_map(
        partial(local, Grid(mesh)),
        mesh=mesh,
        in_specs=(
            whole,
            rows,
            sharded,
            sharded,
            rows,
            sharded,
            sharded,
            sharded,
            rows,
            sharded,
            rows,
            sharded,
            sharded,
            sharded,
            P(None, "blk", None),
            P("batch", None),
            P("batch"),
            P("batch", None, None),
        ),
        out_specs=(
            whole,
            whole,
            rows,
            sharded,
            sharded,
            rows,
            sharded,
            sharded,
            sharded,
            rows,
            sharded,
            rows,
            sharded,
            sharded,
            sharded,
        ),
        check_vma=False,
    )
```

```python
import math
from functools import partial

import jax
import jax.numpy as jnp
from jax import lax
from jax.experimental import pallas as pl
from jax.experimental.pallas import tpu as pltpu
from jax.sharding import PartitionSpec as P

norm_eps = 1e-06
masked_score = -1e30
f32 = jnp.float32
bf16 = jnp.bfloat16
both = ("batch", "blk")
log2e = math.log2(math.e)
long, brief, least = 10**11, 100000000000, 100000000000
roomy = pltpu.CompilerParams(vmem_limit_bytes=48 << 20)
vector_names = (
    "bias_query",
    "bias_value",
    "bias_out",
    "gain_first",
    "shift_first",
    "bias_down",
    "gain_second",
    "shift_second",
)
row_of = {name: index for index, name in enumerate(vector_names)}


def dot(left, right):
    return jnp.dot(left, right, preferred_element_type=f32)


def dot_right_t(left, right):
    return lax.dot_general(left, right, (((1,), (1,)), ((), ())), preferred_element_type=f32)


def dot_left_t(left, right):
    return lax.dot_general(left, right, (((0,), (0,)), ((), ())), preferred_element_type=f32)


def norm_stats(rows):
    center = jnp.mean(rows, axis=-1, keepdims=True)
    centered = rows - center
    inverse = lax.rsqrt(jnp.mean(centered * centered, axis=-1, keepdims=True) + norm_eps)
    return centered * inverse, inverse


def norm_pull(upstream, normed, inverse, gain):
    scaled = upstream * gain
    inner = jnp.mean(scaled, axis=-1, keepdims=True)
    projected = jnp.mean(scaled * normed, axis=-1, keepdims=True)
    return inverse * (scaled - inner - normed * projected)


def vector(ref, name):
    index = row_of[name]
    return ref[index : index + 1, :]


def add_sums(sums_ref, rows):
    total = jnp.concatenate(
        [jnp.sum(row, axis=0, keepdims=True) for row in rows]
        + [jnp.zeros((sums_ref.shape[0] - len(rows), sums_ref.shape[1]), f32)],
        axis=0,
    )

    @pl.when(pl.program_id(0) == 0)
    def _():
        sums_ref[...] = total

    @pl.when(pl.program_id(0) > 0)
    def _():
        sums_ref[...] += total


def piece_rows(here, piece, rows):
    return pl.ds(pl.multiple_of((here ^ piece) * rows, rows), rows)


def stack_pieces(ref, places, cols):
    return jnp.concatenate([ref[0, place_, cols] for place_ in places], axis=0)


def any_block():
    return pl.BlockSpec(memory_space=pl.ANY)


def whole_block(array):
    return pl.BlockSpec(array.shape, lambda *unused: (0,) * len(array.shape))


def pair_order(core, first, second, wide):
    blocks = []
    for start in range(0, first.shape[-1], wide):
        left, right = first[:, start : start + wide], second[:, start : start + wide]
        blocks += [jnp.where(core == 0, left, right), jnp.where(core == 0, right, left)]
    return jnp.concatenate(blocks, axis=1)


def pair_split(core, array, wide):
    outs = []
    for turn in range(2):
        outs.append(
            jnp.concatenate(
                [
                    jnp.where(
                        core == turn,
                        array[:, start : start + wide],
                        array[:, start + wide : start + 2 * wide],
                    )
                    for start in range(0, array.shape[1], 2 * wide)
                ],
                axis=1,
            )
        )
    return outs


def half_split(core, array):
    half = array.shape[1] // 2
    left, right = array[:, :half], array[:, half:]
    return jnp.where(core == 0, left, right), jnp.where(core == 0, right, left)


class Run:
    def __init__(self, ids):
        self.ids, self.token = ids, None


id_of = {"here": 0, "c": 1, "y": 2, "z": 3, "x": 4}
token_shape = jax.ShapeDtypeStruct((8, 128), f32)


def after(run, arrays, *ties):
    shapes = [jax.ShapeDtypeStruct(array.shape, array.dtype) for array in arrays]

    def body(*refs):
        refs[-1][...] = jnp.zeros(token_shape.shape, f32)

    *arrays, run.token = pl.pallas_call(
        body,
        out_shape=shapes + [token_shape],
        in_specs=[any_block()] * (len(arrays) + len(ties)),
        out_specs=[any_block()] * len(arrays) + [pl.BlockSpec(memory_space=pltpu.VMEM)],
        input_output_aliases={index: index for index in range(len(arrays))},
    )(*arrays, *ties)
    return arrays


def kernel_call(
    kernel, run, arrays, ties, grid, in_specs, out_specs, out_shape, scratch=(), cost=long
):
    several = isinstance(out_shape, (list, tuple))
    out_specs, out_shape = [
        list(value) if several else [value] for value in (out_specs, out_shape)
    ]
    count, outs = 1 + len(arrays), len(out_shape)

    def body(*refs):
        inputs, refs = refs[:count], refs[count + len(ties) :]
        refs[outs][...] = jnp.zeros(token_shape.shape, f32)
        kernel(*inputs, *refs[:outs], *refs[outs + 1 :])

    *results, run.token = pl.pallas_call(
        body,
        out_shape=out_shape + [token_shape],
        grid_spec=pltpu.PrefetchScalarGridSpec(
            num_scalar_prefetch=1,
            grid=grid,
            in_specs=list(in_specs) + [any_block()] * len(ties),
            out_specs=out_specs + [whole_block(token_shape)],
            scratch_shapes=scratch,
        ),
        compiler_params=roomy,
        cost_estimate=pl.CostEstimate(flops=cost, bytes_accessed=1024, transcendentals=0),
    )(run.ids, *arrays, *ties)
    return results if several else results[0]


def place_kernel(digit, count, ids, *refs):
    parts, (out, sems) = refs[:count], refs[count:]
    copies = [
        pltpu.make_async_copy(part, out.at[ids[digit] ^ delta], sems.at[delta])
        for delta, part in enumerate(parts)
    ]
    for copy in copies:
        copy.start()
    for copy in copies:
        copy.wait()


def place_parts(run, parts, digit, ties=()):
    count = len(parts)
    return kernel_call(
        partial(place_kernel, id_of[digit], count),
        run,
        parts,
        ties,
        (1,),
        [whole_block(part) for part in parts],
        any_block(),
        jax.ShapeDtypeStruct((count, *parts[0].shape), parts[0].dtype),
        [pltpu.SemaphoreType.DMA((count,))],
        cost=least,
    )


def widen_kernel(digit, count, ids, *refs):
    for delta in range(count):
        refs[count][ids[digit] ^ delta] = refs[delta][...].astype(f32)


def widen_parts(run, parts, digit, ties=()):
    count = len(parts)
    shape = jax.ShapeDtypeStruct((count, *parts[0].shape), f32)
    return kernel_call(
        partial(widen_kernel, id_of[digit], count),
        run,
        parts,
        ties,
        (1,),
        [whole_block(part) for part in parts],
        whole_block(shape),
        shape,
    )


class Loader:
    def __init__(self, ids, sems, digit="y"):
        self.core, self.digit = ids[id_of["c"]], ids[id_of[digit]]
        self.sems, self.copies = sems, []

    def put(self, source, target):
        copy = pltpu.make_async_copy(source, target, self.sems.at[len(self.copies)])
        copy.start()
        self.copies.append(copy)

    def rows(self, pieces, start, size, target):
        for turn, piece in enumerate(pieces):
            self.put(piece.at[:, :, pl.ds(start, size)], target.at[:, self.digit ^ turn])

    def columns(self, both_cores, start, size, target):
        for other, pieces in enumerate(both_cores):
            lanes = pl.ds(pl.multiple_of((self.core ^ other) * size, 128), size)
            for turn, piece in enumerate(pieces):
                self.put(
                    piece.at[:, :, pl.ds(start, size)], target.at[:, self.digit ^ turn, :, lanes]
                )

    def wait(self):
        for copy in self.copies:
            copy.wait()


def flat(ref, first=None, count=None):
    value = ref[...] if first is None else ref[pl.ds(first, count)]
    return value.reshape(-1, value.shape[-1])


def place_shape(piece, cols):
    return pltpu.VMEM((piece.shape[0], 2, piece.shape[1], cols), bf16)


def split_kernel(ids, qkv_ref, vec_ref, out_ref, up_ref, down_ref, *outs):
    core = ids[1]
    width = down_ref.shape[1]
    lanes = lax.broadcasted_iota(jnp.int32, (vec_ref.shape[0], 128), 1)
    eye = lanes == lax.broadcasted_iota(jnp.int32, lanes.shape, 0)
    columns = dot_left_t(vec_ref[...], jnp.where(eye, 1.0, 0.0).astype(bf16)).astype(bf16)
    for turn in range(2):
        first, second, down = outs[3 * turn : 3 * turn + 3]
        pairs = []
        for start in range(0, width, 256):
            for part in range(3):
                left = qkv_ref[:, part * width + start : part * width + start + 128]
                right = qkv_ref[:, part * width + start + 128 : part * width + start + 256]
                pairs.append(jnp.where(core == turn, left, right))
        first[...] = jnp.concatenate(pairs + [columns], axis=1)
        second[...] = jnp.concatenate(
            [half_split(core, ref[...])[turn] for ref in (out_ref, up_ref)], axis=1
        )
        down[...] = half_split(core, down_ref[...])[turn]


def split_weights(ids, w_qkv, vectors, w_out, w_up, w_down, ties=()):
    rows, cols = w_qkv.shape
    arrays = [w_qkv, vectors, w_out, w_up, w_down]
    shapes = [
        jax.ShapeDtypeStruct((rows, cols // 2 + 128), bf16),
        jax.ShapeDtypeStruct((rows, (w_out.shape[1] + w_up.shape[1]) // 2), bf16),
        jax.ShapeDtypeStruct((w_down.shape[0], w_down.shape[1] // 2), bf16),
    ] * 2
    outs = kernel_call(
        split_kernel,
        ids,
        arrays,
        ties,
        (1,),
        [whole_block(array) for array in arrays],
        [whole_block(shape) for shape in shapes],
        shapes,
        cost=least,
    )
    return list(zip(outs[:3], outs[3:]))


def load_qkv(load, chunks, targets):
    for turn, target in enumerate(targets):
        cols, split = target.shape[-1], chunks[0][0].shape[-1]
        for start, size, chunk in ((0, split, chunks[0]), (split, cols - split, chunks[1])):
            load.rows(
                chunk[2 * turn : 2 * turn + 2], 0, size, target.at[:, :, :, pl.ds(start, size)]
            )


def qkv_kernel(blk, ids, *refs):
    parts, refs = refs[:blk], refs[blk:]
    chunks, refs = (refs[:4], refs[4:8]), refs[8:]
    x_ref, vec_ref, out_ref, w_ref, w_far_ref, v_ref, sems = refs
    here, core = ids[0], ids[1]
    step = pl.program_id(0)
    cols = out_ref.shape[2]

    @pl.when(step == 0)
    def _():
        load = Loader(ids, sems)
        for piece, part in enumerate(parts):
            load.put(part, x_ref.at[:, here ^ piece])
        load_qkv(load, chunks, (w_ref, w_far_ref))
        used = cols - chunks[0][0].shape[-1]
        load.rows(chunks[1][:2], used, 128, v_ref)
        load.wait()
        vec_ref[...] = flat(v_ref).astype(f32).T[: vec_ref.shape[0]]

    per_seq = x_ref.shape[1] // 2
    rows = x_ref[step // per_seq, pl.ds(2 * (step % per_seq), 2)].reshape(-1, x_ref.shape[-1])
    for turn, weights in enumerate((w_ref, w_far_ref)):
        bias = []
        for start in range(0, vec_ref.shape[1], 256):
            for name in ("bias_query", None, "bias_value"):
                if name is None:
                    bias.append(jnp.zeros((1, 128), f32))
                    continue
                row = vector(vec_ref, name)
                bias.append(
                    jnp.where(
                        core == turn, row[:, start : start + 128], row[:, start + 128 : start + 256]
                    )
                )
        total = dot(rows, flat(weights)) + jnp.concatenate(bias, axis=1)
        out_ref[turn] = total.astype(bf16)


def qkv_projection(ids, parts, pieces, cols, ties=()):
    blk = len(parts)
    seqs, block_rows, width = parts[0].shape
    tokens = seqs * blk * block_rows
    block = 2 * block_rows
    piece = pieces[0][0][0]
    shape = place_shape(piece, cols)
    x_shape = jax.ShapeDtypeStruct((seqs, blk, block_rows, width), bf16)
    v_shape = jax.ShapeDtypeStruct((16, width), f32)
    return kernel_call(
        partial(qkv_kernel, blk),
        ids,
        [*parts, *[piece for chunk in pieces for pair in chunk for piece in pair]],
        ties,
        (tokens // block,),
        [any_block()] * (blk + 8),
        (
            whole_block(x_shape),
            whole_block(v_shape),
            pl.BlockSpec((2, block, cols), lambda i, ids: (0, i, 0)),
        ),
        (x_shape, v_shape, jax.ShapeDtypeStruct((2, tokens, cols), bf16)),
        [shape, shape, place_shape(piece, 128), pltpu.SemaphoreType.DMA((blk + 10,))],
        cost=brief,
    )


def attend_kernel(head_dim, ids, qkv_ref, *rest):
    pieces, (o_ref, lse_ref) = rest[:-2], rest[-2:]
    here = ids[0]
    pair, seq = pl.program_id(1), pl.program_id(2)
    length, wide = o_ref.shape[1:]
    per = wide // head_dim
    rows = pieces[0].shape[1]
    lanes = lax.broadcasted_iota(jnp.int32, (1, wide), 1)
    log_lanes = lax.broadcasted_iota(jnp.int32, (1, lse_ref.shape[2]), 1)
    keys, values = qkv_ref[0, :, wide : 2 * wide], qkv_ref[0, :, 2 * wide :]
    for first in range(0, len(pieces), 2):
        span = range(first, min(first + 2, len(pieces)))
        places = [piece_rows(here, piece, rows) for piece in span]
        queries = stack_pieces(qkv_ref, places, slice(0, wide))
        out, logs = None, []
        for head in range(per):
            mine = lanes // head_dim == head
            scores = dot_right_t(jnp.where(mine, queries, 0), keys) * (head_dim**-0.5 * log2e)
            addend = jnp.concatenate([pieces[piece][head] for piece in span], axis=0)
            scores = scores + addend.astype(f32)
            top = jnp.max(scores, axis=1, keepdims=True)
            weights = jnp.exp2(scores - top)
            total = jnp.sum(weights, axis=1, keepdims=True)
            part = dot(weights.astype(bf16), values) * (1.0 / total)
            out = part if out is None else jnp.where(mine, part, out)
            logs.append(top + jnp.log2(total))
        for index, place_ in enumerate(places):
            here_rows = slice(index * rows, (index + 1) * rows)
            o_ref[0, place_, :] = out[here_rows].astype(bf16)
            start = seq * length + (here ^ span[index]) * rows
            log_place = pl.ds(pl.multiple_of(start, rows), rows)
            kept = lse_ref[0, log_place, :]
            for head in range(per):
                kept = jnp.where(log_lanes == pair * per + head, logs[head][here_rows], kept)
            lse_ref[0, log_place, :] = kept


def attend_back_kernel(head_dim, ids, qkv_ref, o_ref, g_ref, lse_ref, *rest):
    pieces, (out_ref, sums_ref) = rest[:-2], rest[-2:]
    here = ids[0]
    pair, seq = pl.program_id(1), pl.program_id(2)
    length, wide = o_ref.shape[1:]
    per = wide // head_dim
    rows = pieces[0].shape[1]
    lanes = lax.broadcasted_iota(jnp.int32, (1, wide), 1)
    log_lanes = lax.broadcasted_iota(jnp.int32, (1, lse_ref.shape[2]), 1)
    keys, values = qkv_ref[0, :, wide : 2 * wide], qkv_ref[0, :, 2 * wide :]
    everything = slice(None)
    back = head_dim**-0.5
    dk = jnp.zeros(keys.shape, f32)
    dv = jnp.zeros(keys.shape, f32)
    for first in range(0, len(pieces), 2):
        span = range(first, min(first + 2, len(pieces)))
        places = [piece_rows(here, piece, rows) for piece in span]
        queries = stack_pieces(qkv_ref, places, slice(0, wide))
        ups = stack_pieces(g_ref, places, everything)
        products = ups.astype(f32) * stack_pieces(o_ref, places, everything).astype(f32)
        starts = [seq * length + (here ^ piece) * rows for piece in span]
        log_places = [pl.ds(pl.multiple_of(at, rows), rows) for at in starts]
        logs = stack_pieces(lse_ref, log_places, everything)
        dq = None
        for head in range(per):
            mine = lanes // head_dim == head
            q_mine, g_mine = jnp.where(mine, queries, 0), jnp.where(mine, ups, 0)
            inner = jnp.sum(jnp.where(mine, products, 0.0), axis=1, keepdims=True)
            log = jnp.sum(
                jnp.where(log_lanes == pair * per + head, logs, 0.0), axis=1, keepdims=True
            )
            scores = dot_right_t(q_mine, keys) * (back * log2e)
            addend = jnp.concatenate([pieces[piece][head] for piece in span], axis=0)
            exact = jnp.exp2(scores + addend.astype(f32) - log)
            grads = (exact * (dot_right_t(g_mine, values) - inner)).astype(bf16)
            dv = dv + dot_left_t(exact.astype(bf16), g_mine)
            dk = dk + dot_left_t(grads, q_mine)
            part = dot(grads, keys)
            dq = part if dq is None else jnp.where(mine, part, dq)
        for index, place_ in enumerate(places):
            out_ref[0, place_, :wide] = (dq[index * rows : (index + 1) * rows] * back).astype(bf16)
    out_ref[0, :, wide : 2 * wide] = (dk * back).astype(bf16)
    out_ref[0, :, 2 * wide :] = dv.astype(bf16)
    sums = dot(jnp.ones((sums_ref.shape[2], length), bf16), out_ref[0])

    @pl.when(seq == 0)
    def _():
        sums_ref[0, 0] = sums

    @pl.when(seq > 0)
    def _():
        sums_ref[0, 0] += sums


def attention_specs(joined, mask_parts):
    rows, length = mask_parts[0].shape[1:]

    def block(cols):
        return pl.BlockSpec((1, length, cols), lambda r, p, s, ids: (r, s, p))

    logs = pl.BlockSpec((1, joined.shape[1], 128), lambda r, p, s, ids: (r, 0, 0))
    mask = pl.BlockSpec((2, rows, length), lambda r, p, s, ids: (2 * p + (ids[1] ^ r), 0, 0))
    return block, logs, [mask] * len(mask_parts)


def attend(ids, joined, mask_parts, seqs, head_dim, ties=()):
    tokens, cols = joined.shape[1:]
    block, logs, masks = attention_specs(joined, mask_parts)
    width = cols // 3
    return kernel_call(
        partial(attend_kernel, head_dim),
        ids,
        [joined, *mask_parts],
        ties,
        (2, width // 128, seqs),
        [block(384)] + masks,
        (block(128), logs),
        (
            jax.ShapeDtypeStruct((2, tokens, width), bf16),
            jax.ShapeDtypeStruct((2, tokens, 128), f32),
        ),
        cost=brief,
    )


def attend_back(
    ids, joined, attended, upstream, logs, mask_parts, seqs, head_dim, ties=()
):
    tokens, cols = joined.shape[1:]
    count = cols // 384
    block, log_block, masks = attention_specs(joined, mask_parts)
    return kernel_call(
        partial(attend_back_kernel, head_dim),
        ids,
        [joined, attended, upstream, logs, *mask_parts],
        ties,
        (2, count, seqs),
        [block(384), block(128), block(128), log_block] + masks,
        (
            block(384),
            pl.BlockSpec((1, 1, 8, 384), lambda r, p, s, ids: (r, p, 0, 0)),
        ),
        (
            jax.ShapeDtypeStruct((2, tokens, cols), bf16),
            jax.ShapeDtypeStruct((2, count, 8, 384), f32),
        ),
    )


def out_kernel(ids, att_ref, x_ref, vec_ref, *refs):
    pieces, (first_ref, low_ref, w_ref, sems) = (refs[:2], refs[2:4]), refs[4:]

    @pl.when(pl.program_id(0) == 0)
    def _():
        load = Loader(ids, sems)
        load.columns(pieces, 0, w_ref.shape[-1] // 2, w_ref)
        load.wait()

    attended = pair_order(ids[1], att_ref[0], att_ref[1], 128)
    first = x_ref[...].astype(f32) + (dot(attended, flat(w_ref)) + vector(vec_ref, "bias_out"))
    first_ref[...] = first
    gain, shift = vector(vec_ref, "gain_first"), vector(vec_ref, "shift_first")
    low_ref[...] = (norm_stats(first)[0] * gain + shift).astype(bf16)


def out_projection(ids, attended, pieces, token_rows, vectors, block, ties=()):
    tokens, width = token_rows.shape
    row = pl.BlockSpec((block, width), lambda i, ids: (i, 0))
    return kernel_call(
        out_kernel,
        ids,
        [attended, token_rows, vectors, *pieces[0], *pieces[1]],
        ties,
        (tokens // block,),
        [
            pl.BlockSpec((2, block, width // 2), lambda i, ids: (0, i, 0)),
            row,
            whole_block(vectors),
        ]
        + [any_block()] * 4,
        (row, row),
        (jax.ShapeDtypeStruct((tokens, width), f32), jax.ShapeDtypeStruct((tokens, width), bf16)),
        [place_shape(pieces[0][0], width), pltpu.SemaphoreType.DMA((4,))],
        cost=brief,
    )


def up_kernel(chunk, steps, ids, h_ref, b_ref, *refs):
    pieces, (act_ref, der_ref, w_ref, w_far_ref, sems) = (refs[:2], refs[2:4]), refs[4:]
    step = pl.program_id(0)
    block = act_ref.shape[1]
    cols = w_ref.shape[-1]

    @pl.when(step == 0)
    def _():
        load = Loader(ids, sems)
        start = pieces[0][0].shape[-1] - cols
        load.rows(pieces[0], start, cols, w_ref)
        load.rows(pieces[1], start, cols, w_far_ref)
        load.wait()

    def run(ref):
        lanes = pl.ds(pl.multiple_of((step % steps) * block, block), block)
        weights = ref[:, :, :, lanes].reshape(-1, block)
        bias = b_ref[0]
        for first in range(0, h_ref.shape[0], chunk):
            place_ = slice(first, first + chunk)
            gate = dot(h_ref[place_, :], weights) + bias
            share = 0.5 + 0.5 * lax.erf(gate * math.sqrt(0.5))
            bell = jnp.exp2((-0.5 * log2e) * (gate * gate)) * (1.0 / math.sqrt(2.0 * math.pi))
            act_ref[place_, :] = (gate * share).astype(bf16)
            der_ref[place_, :] = (share + gate * bell).astype(bf16)

    pl.when(step < steps)(lambda: run(w_ref))
    pl.when(step >= steps)(lambda: run(w_far_ref))


def up_projection(ids, hidden_low, pieces, bias, ties=()):
    tokens, width = hidden_low.shape
    half = bias.shape[2]
    block = width
    steps = half // block
    out = pl.BlockSpec((tokens, block), lambda j, ids: (0, (ids[1] ^ (j // steps)) * steps + j % steps))
    shape = jax.ShapeDtypeStruct((tokens, 2 * half), bf16)
    scratch = place_shape(pieces[0][0], half)
    return kernel_call(
        partial(up_kernel, 128, steps),
        ids,
        [hidden_low, bias, *pieces[0], *pieces[1]],
        ties,
        (2 * steps,),
        [
            whole_block(hidden_low),
            pl.BlockSpec((1, 1, block), lambda j, ids: (ids[1] ^ (j // steps), 0, j % steps)),
        ]
        + [any_block()] * 4,
        (out, out),
        (shape, shape),
        [scratch, scratch, pltpu.SemaphoreType.DMA((4,))],
        cost=brief,
    )


def down_kernel(blk, ids, *refs):
    pos_ref, cot_ref, act_ref, der_ref, first_ref, vec_ref = refs[:6]
    mine, other = refs[6:8], refs[8:10]
    outs, refs = refs[10 : 10 + blk], refs[10 + blk :]
    gss_ref, gdi_ref, gate_ref, sums_ref, up_ref, w_ref, sems = refs
    step = pl.program_id(0)
    here = ids[0]
    seqs, rows, width = first_ref.shape

    @pl.when(step == 0)
    def _():
        load = Loader(ids, sems)
        load.columns((mine, other), 0, width // 2, w_ref)
        load.wait()

    weights = flat(w_ref)
    cols = act_ref.shape[-1]
    normed_one = norm_stats(first_ref[...].reshape(-1, width))[0]
    hidden = normed_one * vector(vec_ref, "gain_first") + vector(vec_ref, "shift_first")
    product = dot(act_ref[...].reshape(-1, cols), weights)
    second = hidden + (product + vector(vec_ref, "bias_down"))
    normed, inverse = norm_stats(second)
    gain = vector(vec_ref, "gain_second")
    result = (normed * gain + vector(vec_ref, "shift_second")).astype(bf16)
    for piece, out in enumerate(outs):

        @pl.when(step == piece)
        def _():
            out[...] = result.reshape(out.shape)

    slots = pos_ref.shape[-1]
    token = lax.broadcasted_iota(jnp.int32, (rows, slots), 0) + (here ^ step) * rows
    upstream = jnp.concatenate(
        [
            dot(jnp.where(token == pos_ref[seq], 1.0, 0.0).astype(bf16), cot_ref[seq])
            for seq in range(seqs)
        ],
        axis=0,
    )
    grad = norm_pull(upstream, normed, inverse, gain)
    gss_ref[...] = grad.reshape(gss_ref.shape)
    low = grad.astype(bf16)
    gdi_ref[...] = low.reshape(gdi_ref.shape)
    add_sums(sums_ref, [low.astype(f32), upstream * normed, upstream])
    grad_gate = dot_right_t(low, weights) * der_ref[...].reshape(-1, cols).astype(f32)
    grad_gate = grad_gate.astype(bf16)
    gate_ref[...] = grad_gate.reshape(gate_ref.shape)
    add_sums(up_ref, [grad_gate.astype(f32)])


def down_projection(
    ids, active, slope, first_sum, pieces, vectors, marks, cot_values, seqs, blk, ties=()
):
    tokens, cols = active.shape
    width = first_sum.shape[1]
    length = tokens // seqs
    rows = length // blk

    def block(size):
        return pl.BlockSpec((seqs, rows, size), lambda d, ids: (0, ids[0] ^ d, 0))

    def shape(size, dtype):
        return jax.ShapeDtypeStruct((seqs, length, size), dtype)

    piece = jax.ShapeDtypeStruct((seqs, rows, width), bf16)
    sums = jax.ShapeDtypeStruct((8, width), f32)
    up_sums = jax.ShapeDtypeStruct((8, cols), f32)
    slots = marks.shape[-1]
    by_seq = [array.reshape(seqs, length, -1) for array in (active, slope, first_sum)]
    outs = kernel_call(
        partial(down_kernel, blk),
        ids,
        [marks, cot_values, *by_seq, vectors, *pieces[0], *pieces[1]],
        ties,
        (blk,),
        [
            whole_block(marks),
            pl.BlockSpec((seqs, slots, width), lambda d, ids: (ids[0], 0, 0)),
            block(cols),
            block(cols),
            block(width),
            whole_block(vectors),
        ]
        + [any_block()] * 4,
        [whole_block(piece)] * blk
        + [block(width), block(width), block(cols), whole_block(sums), whole_block(up_sums)],
        [piece] * blk + [shape(width, f32), shape(width, bf16), shape(cols, bf16), sums, up_sums],
        [place_shape(pieces[0][0], width), pltpu.SemaphoreType.DMA((4,))],
    )
    rest = outs[blk:]
    return outs[:blk], [array.reshape(tokens, -1) for array in rest[:3]], rest[3:]


def first_back_kernel(ids, gate_ref, gss_ref, first_ref, vec_ref, *refs):
    pieces, refs = (refs[:2], refs[2:4]), refs[4:]
    gfs_ref, branch_ref, att_ref, sums_ref, w_ref, w_out_ref, sems = refs
    width = gss_ref.shape[1]

    @pl.when(pl.program_id(0) == 0)
    def _():
        load = Loader(ids, sems)
        load.columns(pieces, width // 2, w_ref.shape[-1] // 2, w_ref)
        load.columns(pieces, 0, width // 2, w_out_ref)
        load.wait()

    grad_hidden = gss_ref[...] + dot_right_t(gate_ref[...], flat(w_ref))
    normed, inverse = norm_stats(first_ref[...])
    grad = norm_pull(grad_hidden, normed, inverse, vector(vec_ref, "gain_first"))
    gfs_ref[...] = grad
    low = grad.astype(bf16)
    branch_ref[...] = low
    grad_att = dot_right_t(low, flat(w_out_ref)).astype(bf16)
    att_ref[0], att_ref[1] = pair_split(ids[1], grad_att, 128)
    add_sums(sums_ref, [low.astype(f32), grad_hidden * normed, grad_hidden])


def first_back(ids, grad_gate, grad_second_sum, first_sum, pieces, vectors, block, ties=()):
    tokens, cols = grad_gate.shape
    width = first_sum.shape[1]

    def row(size):
        return pl.BlockSpec((block, size), lambda i, ids: (i, 0))

    def shape(size, dtype):
        return jax.ShapeDtypeStruct((tokens, size), dtype)

    sums = jax.ShapeDtypeStruct((8, width), f32)
    piece = pieces[0][0]
    return kernel_call(
        first_back_kernel,
        ids,
        [grad_gate, grad_second_sum, first_sum, vectors, *pieces[0], *pieces[1]],
        ties,
        (tokens // block,),
        [row(cols), row(width), row(width), whole_block(vectors)] + [any_block()] * 4,
        (
            row(width),
            row(width),
            pl.BlockSpec((2, block, width // 2), lambda i, ids: (0, i, 0)),
            whole_block(sums),
        ),
        (
            shape(width, f32),
            shape(width, bf16),
            jax.ShapeDtypeStruct((2, tokens, width // 2), bf16),
            sums,
        ),
        [place_shape(piece, cols), place_shape(piece, width), pltpu.SemaphoreType.DMA((8,))],
    )


def beside(array, devices, per):
    groups = array.reshape(devices, per, -1, array.shape[-1])
    return jnp.concatenate(
        [groups[:, index].reshape(-1, array.shape[-1]) for index in range(per)], axis=1
    )


def down_grad_kernel(devices, per, ids, act_ref, g_ref, keep_ref, send_ref):
    halves = half_split(ids[1], dot_left_t(act_ref[...], g_ref[...]))
    for half, out in zip(halves, (keep_ref, send_ref)):
        out[...] = (beside(half, devices, per) if per > 1 else half).astype(bf16)


def down_grad(ids, active, grad_down_in, devices, ties=()):
    tokens, cols = active.shape
    width = grad_down_in.shape[1]
    per, block = cols // width, width
    inside = (width // devices) % 8 == 0
    groups = per if inside else 1
    out = pl.BlockSpec((block // groups, groups * width // 2), lambda i, ids: (i, 0))
    shape = jax.ShapeDtypeStruct((cols // groups, groups * width // 2), bf16)
    halves = kernel_call(
        partial(down_grad_kernel, devices // per, groups),
        ids,
        [active, grad_down_in],
        ties,
        (cols // block,),
        [pl.BlockSpec((tokens, block), lambda i, ids: (0, i)), whole_block(grad_down_in)],
        (out, out),
        (shape, shape),
    )
    return halves if inside else [beside(half, devices, per) for half in halves]


def up_grad_kernel(ids, h_ref, g_ref, g_far_ref, keep_ref, send_ref):
    keep_ref[...] = dot_left_t(h_ref[...], g_ref[...]).astype(bf16)
    send_ref[...] = dot_left_t(h_ref[...], g_far_ref[...]).astype(bf16)


def up_grad(ids, hidden_low, grad_gate, block, ties=()):
    tokens, width = hidden_low.shape
    cols = grad_gate.shape[1] // 2
    steps = cols // block
    shape = jax.ShapeDtypeStruct((width, cols), bf16)
    out = pl.BlockSpec((width, block), lambda j, ids: (0, j))
    return kernel_call(
        up_grad_kernel,
        ids,
        [hidden_low, grad_gate, grad_gate],
        ties,
        (steps,),
        [
            whole_block(hidden_low),
            pl.BlockSpec((tokens, block), lambda j, ids: (0, ids[1] * steps + j)),
            pl.BlockSpec((tokens, block), lambda j, ids: (0, (1 - ids[1]) * steps + j)),
        ],
        (out, out),
        (shape, shape),
    )


def left_grad_kernel(
    ids,
    x_ref,
    g_ref,
    att_ref,
    branch_ref,
    sums_ref,
    first_ref,
    second_ref,
    up_ref,
    keep_ref,
    send_ref,
):
    core, step = ids[1], pl.program_id(0)
    attended = pair_order(core, att_ref[0], att_ref[1], 128)
    out_grads = half_split(core, dot_left_t(attended, branch_ref[...]))
    sums = [sums_ref[turn, step][:1] for turn in range(2)]
    rows = [
        pair_order(core, sums[0][:, at : at + 128], sums[1][:, at : at + 128], 128)
        for at in (0, 256)
    ]
    rows += [first_ref[:3], second_ref[:3], up_ref[...]]
    used = sum(row.shape[0] for row in rows)
    rows = jnp.concatenate(rows + [jnp.zeros((16 - used, rows[0].shape[1]), f32)], axis=0)
    lanes = lax.broadcasted_iota(jnp.int32, (16, 128), 1)
    eye = lanes == lax.broadcasted_iota(jnp.int32, lanes.shape, 0)
    columns = dot_left_t(rows.astype(bf16), jnp.where(eye, 1.0, 0.0).astype(bf16))
    for turn, out in enumerate((keep_ref, send_ref)):
        grad = dot_left_t(x_ref[...], g_ref[turn])
        out[...] = jnp.concatenate([grad, out_grads[turn], columns], axis=1).astype(bf16)


def left_grad(ids, left, grads, attended, grad_branch, sums, totals, ties=()):
    tokens, width = left.shape
    cols = grads.shape[2] + width // 2 + 128
    shape = jax.ShapeDtypeStruct((width, cols), bf16)
    out = pl.BlockSpec((256, cols), lambda i, ids: (i, 0))
    return kernel_call(
        left_grad_kernel,
        ids,
        [left, grads, attended, grad_branch, sums, *totals],
        ties,
        (width // 256,),
        [
            pl.BlockSpec((tokens, 256), lambda i, ids: (0, i)),
            whole_block(grads),
            pl.BlockSpec((2, tokens, 128), lambda i, ids: (0, 0, i)),
            whole_block(grad_branch),
            whole_block(sums),
        ]
        + [pl.BlockSpec((array.shape[0], 256), lambda i, ids: (0, i)) for array in totals],
        (out, out),
        (shape, shape),
    )


def input_grad_kernel(blk, ids, g_ref, gfs_ref, *refs):
    chunks, refs = (refs[:4], refs[4:8]), refs[8:]
    outs, (w_ref, w_far_ref, sems) = refs[:blk], refs[blk:]
    step = pl.program_id(0)

    @pl.when(step == 0)
    def _():
        load = Loader(ids, sems)
        load_qkv(load, chunks, (w_ref, w_far_ref))
        load.wait()

    width = gfs_ref.shape[-1]
    total = gfs_ref[...].reshape(-1, width)
    for turn, weights in enumerate((w_ref, w_far_ref)):
        total = total + dot_right_t(g_ref[turn].reshape(-1, g_ref.shape[-1]), flat(weights))
    for piece, out in enumerate(outs):

        @pl.when(step == piece)
        def _():
            out[...] = total.astype(bf16).reshape(out.shape)


def input_grad(ids, grads, grad_first_sum, pieces, seqs, blk, ties=()):
    tokens, width = grad_first_sum.shape
    length = tokens // seqs
    rows = length // blk
    cols = grads.shape[2]
    piece = jax.ShapeDtypeStruct((seqs, rows, width), bf16)
    shape = place_shape(pieces[0][0][0], cols)
    pieces = [piece for chunk in pieces for pair in chunk for piece in pair]
    return kernel_call(
        partial(input_grad_kernel, blk),
        ids,
        [
            grads.reshape(2, seqs, length, cols),
            grad_first_sum.reshape(seqs, length, width),
            *pieces,
        ],
        ties,
        (blk,),
        [
            pl.BlockSpec((2, seqs, rows, cols), lambda d, ids: (0, 0, ids[0] ^ d, 0)),
            pl.BlockSpec((seqs, rows, width), lambda d, ids: (0, ids[0] ^ d, 0)),
        ]
        + [any_block()] * len(pieces),
        [whole_block(piece)] * blk,
        [piece] * blk,
        [shape, shape, pltpu.SemaphoreType.DMA((len(pieces),))],
    )


class Grid:
    def __init__(self, mesh):
        batch, blk = mesh.shape["batch"], mesh.shape["blk"]
        self.sizes = {"z": batch // 2, "y": 2, "x": blk // 2, "c": 2}
        self.strides = {"c": 1, "x": 2, "y": blk, "z": 2 * blk}
        self.total = batch * blk
        self.blk = blk

    def digit(self, name):
        index = lax.axis_index("batch") * self.blk + lax.axis_index("blk")
        return (index // self.strides[name]) % self.sizes[name]

    def swap(self, array, name, delta=1):
        size, stride = self.sizes[name], self.strides[name]
        pairs = []
        for index in range(self.total):
            here = (index // stride) % size
            pairs.append((index, index + ((here ^ delta) - here) * stride))
        return lax.ppermute(array, both, pairs)

    def swap_blk(self, array, delta):
        pairs = [(index, index ^ delta) for index in range(self.total)]
        return lax.ppermute(array, both, pairs)


def place(parts, index):
    if len(parts) == 1:
        return parts[0][None]
    rows = []
    for target in range(len(parts)):
        row = parts[0]
        for delta in range(1, len(parts)):
            row = jnp.where(index == target ^ delta, parts[delta], row)
        rows.append(row)
    return jnp.stack(rows)


def pick(array, index):
    return lax.dynamic_index_in_dim(array, index, axis=0, keepdims=False)


def gather_core(grid, mine, other):
    cols = mine.shape[1]
    return place([mine, grid.swap(other, "c")], grid.digit("c")).reshape(-1, cols)


def gather_step(grid, run, held, name, *ties):
    parts = [grid.swap(held, name, d) for d in range(1, grid.sizes[name])]
    return place_parts(run, [held, *parts], name, ties)


def gather_last(grid, held, name):
    far = grid.swap(held, name)
    if held.shape[1] % 16 == 0:
        return [held, far]
    where = grid.digit(name)
    whole = jnp.moveaxis(place([held, far], where), 0, 1).reshape(4, 2, -1, held.shape[2])
    return [lax.dynamic_index_in_dim(whole, where ^ d, 1, keepdims=False) for d in range(2)]


def gather_pieces(grid, run, held, *ties):
    near, far = held
    if ties:
        (far,) = after(run, [far], *ties)
    return [[near, far], [grid.swap(near, "c"), grid.swap(far, "c")]]


def add_low(*parts):
    total = parts[0].astype(f32)
    for part in parts[1:]:
        total = total + part.astype(f32)
    return total


def fold_kernel(count, groups, ids, *refs):
    outs = refs[len(refs) - count :]
    refs = list(refs[: len(refs) - count])
    for out in outs:
        sums = []
        for terms in groups:
            picked, refs = refs[:terms], refs[terms:]
            total = picked[0][...].astype(f32)
            for ref in picked[1:]:
                total = total + ref[...].astype(f32)
            sums.append(total.astype(out.dtype))
        out[...] = jnp.concatenate(sums, axis=-1).reshape(out.shape)


def fold(ids, which, groups, ties):
    outer, count, rows, unused = groups[0][0].shape
    steps = 2 if outer % 2 == 0 else 1
    part = outer // steps

    def term_block(cols, delta):
        return pl.BlockSpec((part, 1, rows, cols), lambda i, ids: (i, ids[which] ^ delta, 0, 0))

    terms = [term for group in groups for term in group]
    cols = sum(group[0].shape[3] for group in groups)
    shape = jax.ShapeDtypeStruct((outer, rows, cols), bf16)
    return kernel_call(
        partial(fold_kernel, count, [len(group) for group in groups]),
        ids,
        [term for delta in range(count) for term in terms],
        ties,
        (steps,),
        [term_block(term.shape[3], delta) for delta in range(count) for term in terms],
        [pl.BlockSpec((part, rows, cols), lambda i, ids: (i, 0, 0))] * count,
        [shape] * count,
    )


class Scatter:
    def __init__(self, grid, ids, pairs, order):
        self.grid, self.ids, self.order = grid, ids, list(order)
        sizes = grid.sizes
        self.left = [("z", sizes["z"]), ("y", sizes["y"]), ("x", sizes["x"])]
        self.last = 2 * (pairs[0][0].shape[0] // grid.total)
        self.groups = [[keep, grid.swap(send, "c")] for keep, send in pairs]

    def shaped(self, *shape):
        return [[term.reshape(*shape, term.shape[-1]) for term in group] for group in self.groups]

    def step(self, ties=()):
        name = self.order.pop(0)
        index = [left for left, unused in self.left].index(name)
        count = self.left[index][1]
        outer = math.prod(size for unused, size in self.left[:index])
        inner = math.prod(size for unused, size in self.left[index + 1 :]) * self.last
        sums = fold(self.ids, id_of[name], self.shaped(outer, count, inner), ties)
        self.left.pop(index)
        sent = [self.grid.swap(sums[delta], name, delta) for delta in range(1, count)]
        self.groups = [[sums[0], *sent]]

    def end(self, ties=()):
        mine, other = fold(self.ids, id_of["c"], self.shaped(1, 2, self.last // 2), ties)
        mine, other = [array.reshape(array.shape[1:]) for array in (mine, other)]
        return mine.astype(f32), self.grid.swap(other, "c").astype(f32)


def in_order(core, mine, other):
    return jnp.where(core == 0, mine, other), jnp.where(core == 0, other, mine)


def local(
    grid,
    inputs,
    w_qkv,
    bias_query,
    bias_value,
    w_out,
    bias_out,
    gain_first,
    shift_first,
    w_up,
    bias_up,
    w_down,
    bias_down,
    gain_second,
    shift_second,
    dam_mask,
    positions,
    counts,
    cot_values,
):
    groups, block_rows, width = inputs.shape
    head_count = dam_mask.shape[0]
    head_dim = width // head_count
    blk = grid.blk
    seqs = groups // blk
    length = blk * block_rows
    tokens = seqs * length
    here, core = lax.axis_index("blk"), grid.digit("c")
    ids = Run(jnp.stack([here, core] + [grid.digit(name) for name in "yzx"]).astype(jnp.int32))
    rows = w_qkv.shape[0]
    up_per = bias_up.shape[0] // rows
    half = width // 2
    pairs = width // 256

    vectors = (
        bias_query,
        bias_value,
        bias_out,
        gain_first,
        shift_first,
        bias_down,
        gain_second,
        shift_second,
    )
    stacked = jnp.concatenate(
        [
            jnp.stack(vectors),
            bias_up.reshape(rows, up_per).T,
            jnp.zeros((16 - len(vectors) - up_per, rows), bf16),
        ]
    )
    halves = split_weights(ids, w_qkv, stacked, w_out, w_up, w_down)
    first_near, second_near, down_near = [gather_core(grid, *pair) for pair in halves]

    def over_x(held):
        return gather_step(grid, ids, held, "x").reshape(-1, held.shape[1])

    first_near = over_x(first_near)
    event = ids.token
    split = first_near.shape[1] // 2

    by_home = inputs.reshape(blk, seqs, block_rows, width)
    parts = [pick(by_home, here ^ delta) for delta in range(blk)]
    parts[2:] = after(ids, parts[2:], event)
    parts[1:] = [grid.swap_blk(parts[delta], delta) for delta in range(1, blk)]
    second_near = over_x(second_near)
    ties = [ids.token, *parts[2:]]
    down_near = over_x(down_near)
    ties.append(ids.token)
    addend = jnp.where(dam_mask > 0, 0.0, masked_score).astype(bf16)
    (addend,) = after(ids, [addend], event)
    mask_parts = [addend, grid.swap(addend, "c")]
    first_z = gather_step(grid, ids, first_near[:, :split], "z")
    (rest,) = after(ids, [first_near[:, split:]], ids.token)
    first_y = gather_last(grid, first_z, "y")
    rest_z = gather_step(grid, ids, rest, "z", *ties)
    (second_near,) = after(ids, [second_near], ids.token)
    rest_y = gather_last(grid, rest_z, "y")
    first_pieces = [gather_pieces(grid, ids, held) for held in (first_y, rest_y)]
    event = [ids.token]
    if grid.sizes["x"] > 1:
        (far,) = after(ids, [grid.swap(addend, "x")], *event)
        mask_parts += [far, grid.swap(far, "c")]
        event.append(ids.token)
    second_z = gather_step(grid, ids, second_near, "z", *event)
    (down_near,) = after(ids, [down_near], ids.token)
    second_y = gather_last(grid, second_z, "y")
    token_rows, vector_rows, joined = qkv_projection(ids, parts, first_pieces, 3 * half, ties=[ids.token])
    token_rows = token_rows.reshape(tokens, width)
    first_row = len(vectors)
    up_bias = vector_rows[first_row : first_row + up_per].T.reshape(2, 1, -1)

    attended, logs = attend(ids, joined, mask_parts, seqs, head_dim, ties=[ids.token])
    down_z = gather_step(grid, ids, down_near, "z", ids.token)
    down_y = gather_last(grid, down_z, "y")
    second_pieces = gather_pieces(grid, ids, second_y, ids.token)
    first_sum, hidden_low = out_projection(
        ids, attended, second_pieces, token_rows, vector_rows, 2 * block_rows
    )
    active, slope = up_projection(ids, hidden_low, second_pieces, up_bias)
    down_pieces = gather_pieces(grid, ids, down_y, ids.token)

    my_positions = pick(positions.reshape(blk, seqs, -1), here)
    my_counts = pick(counts.reshape(blk, seqs), here)
    live = jnp.arange(positions.shape[1], dtype=jnp.int32)[None, :] < my_counts[:, None]
    marks = jnp.where(live, my_positions, -1)[:, None, :]
    result, (grad_second_sum, grad_down_in, grad_gate), (second_sums, up_sums) = down_projection(
        ids, active, slope, first_sum, down_pieces, vector_rows, marks, cot_values, seqs, blk
    )

    def home(pieces):
        return [pieces[0]] + [grid.swap_blk(pieces[delta], delta) for delta in range(1, blk)]

    result = home(result)
    down_halves = down_grad(ids, active, grad_down_in, grid.total)
    up_halves = up_grad(ids, hidden_low, grad_gate, width, ties=[ids.token])
    ffn_sum = Scatter(grid, ids, [up_halves, down_halves], "yzx")
    ffn_sum.step([ids.token])
    grad_first_sum, grad_branch, grad_attended, first_sums = first_back(
        ids,
        grad_gate,
        grad_second_sum,
        first_sum,
        second_pieces,
        vector_rows,
        2 * block_rows,
        ties=[ids.token],
    )
    result = after(ids, result, ids.token)
    grads, grad_sums = attend_back(
        ids,
        joined,
        attended,
        grad_attended,
        logs,
        mask_parts,
        seqs,
        head_dim,
        ties=[ids.token],
    )
    ffn_sum.step([ids.token])
    up_rows = up_sums[0].reshape(width, up_per).T
    totals = [first_sums, second_sums, up_rows]
    halves = left_grad(
        ids, token_rows, grads, attended, grad_branch, grad_sums, totals, ties=[ids.token]
    )
    att_sum = Scatter(grid, ids, [halves], "xyz")
    att_sum.step([ids.token])
    sent = input_grad(ids, grads, grad_first_sum, first_pieces, seqs, blk, ties=[ids.token])
    grad_inputs = home(sent)
    att_sum.step([ids.token])
    ffn_sum.step([ids.token])
    activations = place_parts(ids, result, "here", [ids.token])
    activations = activations.reshape(groups, block_rows, width)
    att_sum.step([ids.token])
    share_ffn = ffn_sum.end([ids.token])
    grad_inputs = widen_parts(ids, grad_inputs, "here", [ids.token])
    grad_inputs = grad_inputs.reshape(groups, block_rows, width)
    share_att = att_sum.end([ids.token])

    cols = grads.shape[2]
    by_core = jnp.stack(in_order(core, *[share[:, :cols] for share in share_att]), axis=0)
    by_core = by_core.reshape(2, rows, pairs, 3, 128)
    share_qkv = by_core.transpose(1, 3, 2, 0, 4).reshape(rows, 3 * width)
    share_out = jnp.concatenate(
        in_order(core, *[share[:, cols : cols + half] for share in share_att]), axis=1
    )
    up_cols = up_halves[0].shape[1]
    share_up = [share[:, :up_cols] for share in share_ffn]
    share_down = [
        share[:, up_cols:].reshape(rows, up_per, half).transpose(1, 0, 2).reshape(-1, half)
        for share in share_ffn
    ]
    shares = share_att[0][:, cols + half :]
    share_vectors = [shares[:, index] for index in range(len(vectors))]
    share_bias_up = shares[:, len(vectors) : len(vectors) + up_per].reshape(-1)
    (
        share_bias_query,
        share_bias_value,
        share_bias_out,
        share_gain_first,
        share_shift_first,
        share_bias_down,
        share_gain_second,
        share_shift_second,
    ) = share_vectors
    return (
        activations,
        grad_inputs,
        share_qkv,
        share_bias_query,
        share_bias_value,
        share_out,
        share_bias_out,
        share_gain_first,
        share_shift_first,
        jnp.concatenate(in_order(core, *share_up), axis=1),
        share_bias_up,
        jnp.concatenate(in_order(core, *share_down), axis=1),
        share_bias_down,
        share_gain_second,
        share_shift_second,
    )


def solution(mesh):
    sharded = P(both)
    rows = P(both, None)
    whole = P("batch", "blk", None)
    return jax.shard_map(
        partial(local, Grid(mesh)),
        mesh=mesh,
        in_specs=(
            whole,
            rows,
            sharded,
            sharded,
            rows,
            sharded,
            sharded,
            sharded,
            rows,
            sharded,
            rows,
            sharded,
            sharded,
            sharded,
            P(None, "blk", None),
            P("batch", None),
            P("batch"),
            P("batch", None, None),
        ),
        out_specs=(
            whole,
            whole,
            rows,
            sharded,
            sharded,
            rows,
            sharded,
            sharded,
            sharded,
            rows,
            sharded,
            rows,
            sharded,
            sharded,
            sharded,
        ),
        check_vma=False,
    )
```

```python
import math
from functools import partial

import jax
import jax.numpy as jnp
from jax import lax
from jax.experimental import pallas as pl
from jax.experimental.pallas import tpu as pltpu
from jax.sharding import PartitionSpec as P

norm_eps = 1e-06
masked_score = -1e30
f32 = jnp.float32
bf16 = jnp.bfloat16
both = ("batch", "blk")
log2e = math.log2(math.e)
long, brief, least = 10**11, 100000000000, 100000000000
roomy = pltpu.CompilerParams(vmem_limit_bytes=48 << 20)
vector_names = (
    "bias_query",
    "bias_value",
    "bias_out",
    "gain_first",
    "shift_first",
    "bias_down",
    "gain_second",
    "shift_second",
)
row_of = {name: index for index, name in enumerate(vector_names)}


def dot(left, right):
    return jnp.dot(left, right, preferred_element_type=f32)


def dot_right_t(left, right):
    return lax.dot_general(left, right, (((1,), (1,)), ((), ())), preferred_element_type=f32)


def dot_left_t(left, right):
    return lax.dot_general(left, right, (((0,), (0,)), ((), ())), preferred_element_type=f32)


def norm_stats(rows):
    center = jnp.mean(rows, axis=-1, keepdims=True)
    centered = rows - center
    inverse = lax.rsqrt(jnp.mean(centered * centered, axis=-1, keepdims=True) + norm_eps)
    return centered * inverse, inverse


def norm_pull(upstream, normed, inverse, gain):
    scaled = upstream * gain
    inner = jnp.mean(scaled, axis=-1, keepdims=True)
    projected = jnp.mean(scaled * normed, axis=-1, keepdims=True)
    return inverse * (scaled - inner - normed * projected)


def vector(ref, name):
    index = row_of[name]
    return ref[index : index + 1, :]


def add_sums(sums_ref, rows):
    total = jnp.concatenate(
        [jnp.sum(row, axis=0, keepdims=True) for row in rows]
        + [jnp.zeros((sums_ref.shape[0] - len(rows), sums_ref.shape[1]), f32)],
        axis=0,
    )

    @pl.when(pl.program_id(0) == 0)
    def _():
        sums_ref[...] = total

    @pl.when(pl.program_id(0) > 0)
    def _():
        sums_ref[...] += total


def piece_rows(here, piece, rows):
    return pl.ds(pl.multiple_of((here ^ piece) * rows, rows), rows)


def stack_pieces(ref, places, cols):
    return jnp.concatenate([ref[0, place_, cols] for place_ in places], axis=0)


def any_block():
    return pl.BlockSpec(memory_space=pl.ANY)


def whole_block(array):
    return pl.BlockSpec(array.shape, lambda *unused: (0,) * len(array.shape))


def pair_order(core, first, second, wide):
    blocks = []
    for start in range(0, first.shape[-1], wide):
        left, right = first[:, start : start + wide], second[:, start : start + wide]
        blocks += [jnp.where(core == 0, left, right), jnp.where(core == 0, right, left)]
    return jnp.concatenate(blocks, axis=1)


def pair_split(core, array, wide):
    outs = []
    for turn in range(2):
        outs.append(
            jnp.concatenate(
                [
                    jnp.where(
                        core == turn,
                        array[:, start : start + wide],
                        array[:, start + wide : start + 2 * wide],
                    )
                    for start in range(0, array.shape[1], 2 * wide)
                ],
                axis=1,
            )
        )
    return outs


def half_split(core, array):
    half = array.shape[1] // 2
    left, right = array[:, :half], array[:, half:]
    return jnp.where(core == 0, left, right), jnp.where(core == 0, right, left)


class Run:
    def __init__(self, ids):
        self.ids, self.token = ids, None


id_of = {"here": 0, "c": 1, "y": 2, "z": 3, "x": 4}
token_shape = jax.ShapeDtypeStruct((8, 128), f32)


def after(run, arrays, *ties):
    shapes = [jax.ShapeDtypeStruct(array.shape, array.dtype) for array in arrays]

    def body(*refs):
        refs[-1][...] = jnp.zeros(token_shape.shape, f32)

    *arrays, run.token = pl.pallas_call(
        body,
        out_shape=shapes + [token_shape],
        in_specs=[any_block()] * (len(arrays) + len(ties)),
        out_specs=[any_block()] * len(arrays) + [pl.BlockSpec(memory_space=pltpu.VMEM)],
        input_output_aliases={index: index for index in range(len(arrays))},
    )(*arrays, *ties)
    return arrays


def kernel_call(
    kernel, run, arrays, ties, grid, in_specs, out_specs, out_shape, scratch=(), cost=long
):
    several = isinstance(out_shape, (list, tuple))
    out_specs, out_shape = [
        list(value) if several else [value] for value in (out_specs, out_shape)
    ]
    count, outs = 1 + len(arrays), len(out_shape)

    def body(*refs):
        inputs, refs = refs[:count], refs[count + len(ties) :]
        refs[outs][...] = jnp.zeros(token_shape.shape, f32)
        kernel(*inputs, *refs[:outs], *refs[outs + 1 :])

    *results, run.token = pl.pallas_call(
        body,
        out_shape=out_shape + [token_shape],
        grid_spec=pltpu.PrefetchScalarGridSpec(
            num_scalar_prefetch=1,
            grid=grid,
            in_specs=list(in_specs) + [any_block()] * len(ties),
            out_specs=out_specs + [whole_block(token_shape)],
            scratch_shapes=scratch,
        ),
        compiler_params=roomy,
        cost_estimate=pl.CostEstimate(flops=cost, bytes_accessed=1024, transcendentals=0),
    )(run.ids, *arrays, *ties)
    return results if several else results[0]


def place_kernel(digit, count, ids, *refs):
    parts, (out, sems) = refs[:count], refs[count:]
    copies = [
        pltpu.make_async_copy(part, out.at[ids[digit] ^ delta], sems.at[delta])
        for delta, part in enumerate(parts)
    ]
    for copy in copies:
        copy.start()
    for copy in copies:
        copy.wait()


def place_parts(run, parts, digit, ties=()):
    count = len(parts)
    return kernel_call(
        partial(place_kernel, id_of[digit], count),
        run,
        parts,
        ties,
        (1,),
        [whole_block(part) for part in parts],
        any_block(),
        jax.ShapeDtypeStruct((count, *parts[0].shape), parts[0].dtype),
        [pltpu.SemaphoreType.DMA((count,))],
        cost=least,
    )


def widen_kernel(digit, count, ids, *refs):
    for delta in range(count):
        refs[count][ids[digit] ^ delta] = refs[delta][...].astype(f32)


def widen_parts(run, parts, digit, ties=()):
    count = len(parts)
    shape = jax.ShapeDtypeStruct((count, *parts[0].shape), f32)
    return kernel_call(
        partial(widen_kernel, id_of[digit], count),
        run,
        parts,
        ties,
        (1,),
        [whole_block(part) for part in parts],
        whole_block(shape),
        shape,
    )


class Loader:
    def __init__(self, ids, sems, digit="y"):
        self.core, self.digit = ids[id_of["c"]], ids[id_of[digit]]
        self.sems, self.copies = sems, []

    def put(self, source, target):
        copy = pltpu.make_async_copy(source, target, self.sems.at[len(self.copies)])
        copy.start()
        self.copies.append(copy)

    def rows(self, pieces, start, size, target):
        for turn, piece in enumerate(pieces):
            self.put(piece.at[:, :, pl.ds(start, size)], target.at[:, self.digit ^ turn])

    def columns(self, both_cores, start, size, target):
        for other, pieces in enumerate(both_cores):
            lanes = pl.ds(pl.multiple_of((self.core ^ other) * size, 128), size)
            for turn, piece in enumerate(pieces):
                self.put(
                    piece.at[:, :, pl.ds(start, size)], target.at[:, self.digit ^ turn, :, lanes]
                )

    def wait(self):
        for copy in self.copies:
            copy.wait()


def flat(ref, first=None, count=None):
    value = ref[...] if first is None else ref[pl.ds(first, count)]
    return value.reshape(-1, value.shape[-1])


def place_shape(piece, cols):
    return pltpu.VMEM((piece.shape[0], 2, piece.shape[1], cols), bf16)


def split_kernel(ids, qkv_ref, vec_ref, out_ref, up_ref, down_ref, *outs):
    core = ids[1]
    width = down_ref.shape[1]
    lanes = lax.broadcasted_iota(jnp.int32, (vec_ref.shape[0], 128), 1)
    eye = lanes == lax.broadcasted_iota(jnp.int32, lanes.shape, 0)
    columns = dot_left_t(vec_ref[...], jnp.where(eye, 1.0, 0.0).astype(bf16)).astype(bf16)
    for turn in range(2):
        first, second, down = outs[3 * turn : 3 * turn + 3]
        pairs = []
        for start in range(0, width, 256):
            for part in range(3):
                left = qkv_ref[:, part * width + start : part * width + start + 128]
                right = qkv_ref[:, part * width + start + 128 : part * width + start + 256]
                pairs.append(jnp.where(core == turn, left, right))
        first[...] = jnp.concatenate(pairs + [columns], axis=1)
        second[...] = jnp.concatenate(
            [half_split(core, ref[...])[turn] for ref in (out_ref, up_ref)], axis=1
        )
        down[...] = half_split(core, down_ref[...])[turn]


def split_weights(ids, w_qkv, vectors, w_out, w_up, w_down, ties=()):
    rows, cols = w_qkv.shape
    arrays = [w_qkv, vectors, w_out, w_up, w_down]
    shapes = [
        jax.ShapeDtypeStruct((rows, cols // 2 + 128), bf16),
        jax.ShapeDtypeStruct((rows, (w_out.shape[1] + w_up.shape[1]) // 2), bf16),
        jax.ShapeDtypeStruct((w_down.shape[0], w_down.shape[1] // 2), bf16),
    ] * 2
    outs = kernel_call(
        split_kernel,
        ids,
        arrays,
        ties,
        (1,),
        [whole_block(array) for array in arrays],
        [whole_block(shape) for shape in shapes],
        shapes,
        cost=least,
    )
    return list(zip(outs[:3], outs[3:]))


def qkv_kernel(blk, ids, *refs):
    parts, refs = refs[:blk], refs[blk:]
    pieces, refs = (refs[:2], refs[2:4]), refs[4:]
    x_ref, vec_ref, out_ref, w_ref, w_far_ref, v_ref, sems = refs
    here, core = ids[0], ids[1]
    step = pl.program_id(0)
    cols = out_ref.shape[2]

    @pl.when(step == 0)
    def _():
        load = Loader(ids, sems)
        for piece, part in enumerate(parts):
            load.put(part, x_ref.at[:, here ^ piece])
        load.rows(pieces[0], 0, cols, w_ref)
        load.rows(pieces[1], 0, cols, w_far_ref)
        load.rows(pieces[0], cols, 128, v_ref)
        load.wait()
        vec_ref[...] = flat(v_ref).astype(f32).T[: vec_ref.shape[0]]

    per_seq = x_ref.shape[1] // 2
    rows = x_ref[step // per_seq, pl.ds(2 * (step % per_seq), 2)].reshape(-1, x_ref.shape[-1])
    for turn, weights in enumerate((w_ref, w_far_ref)):
        bias = []
        for start in range(0, vec_ref.shape[1], 256):
            for name in ("bias_query", None, "bias_value"):
                if name is None:
                    bias.append(jnp.zeros((1, 128), f32))
                    continue
                row = vector(vec_ref, name)
                bias.append(
                    jnp.where(
                        core == turn, row[:, start : start + 128], row[:, start + 128 : start + 256]
                    )
                )
        total = dot(rows, flat(weights)) + jnp.concatenate(bias, axis=1)
        out_ref[turn] = total.astype(bf16)


def qkv_projection(ids, parts, pieces, cols, ties=()):
    blk = len(parts)
    seqs, block_rows, width = parts[0].shape
    tokens = seqs * blk * block_rows
    block = 2 * block_rows
    piece = pieces[0][0]
    shape = place_shape(piece, cols)
    x_shape = jax.ShapeDtypeStruct((seqs, blk, block_rows, width), bf16)
    v_shape = jax.ShapeDtypeStruct((16, width), f32)
    return kernel_call(
        partial(qkv_kernel, blk),
        ids,
        [*parts, *pieces[0], *pieces[1]],
        ties,
        (tokens // block,),
        [any_block()] * (blk + 4),
        (
            whole_block(x_shape),
            whole_block(v_shape),
            pl.BlockSpec((2, block, cols), lambda i, ids: (0, i, 0)),
        ),
        (x_shape, v_shape, jax.ShapeDtypeStruct((2, tokens, cols), bf16)),
        [shape, shape, place_shape(piece, 128), pltpu.SemaphoreType.DMA((blk + 6,))],
        cost=brief,
    )


def attend_kernel(head_dim, ids, qkv_ref, *rest):
    pieces, (o_ref, lse_ref) = rest[:-2], rest[-2:]
    here = ids[0]
    pair, seq = pl.program_id(1), pl.program_id(2)
    length, wide = o_ref.shape[1:]
    per = wide // head_dim
    rows = pieces[0].shape[1]
    lanes = lax.broadcasted_iota(jnp.int32, (1, wide), 1)
    log_lanes = lax.broadcasted_iota(jnp.int32, (1, lse_ref.shape[2]), 1)
    keys, values = qkv_ref[0, :, wide : 2 * wide], qkv_ref[0, :, 2 * wide :]
    for first in range(0, len(pieces), 2):
        span = range(first, min(first + 2, len(pieces)))
        places = [piece_rows(here, piece, rows) for piece in span]
        queries = stack_pieces(qkv_ref, places, slice(0, wide))
        out, logs = None, []
        for head in range(per):
            mine = lanes // head_dim == head
            scores = dot_right_t(jnp.where(mine, queries, 0), keys) * (head_dim**-0.5 * log2e)
            addend = jnp.concatenate([pieces[piece][head] for piece in span], axis=0)
            scores = scores + addend.astype(f32)
            top = jnp.max(scores, axis=1, keepdims=True)
            weights = jnp.exp2(scores - top)
            total = jnp.sum(weights, axis=1, keepdims=True)
            part = dot(weights.astype(bf16), values) * (1.0 / total)
            out = part if out is None else jnp.where(mine, part, out)
            logs.append(top + jnp.log2(total))
        for index, place_ in enumerate(places):
            here_rows = slice(index * rows, (index + 1) * rows)
            o_ref[0, place_, :] = out[here_rows].astype(bf16)
            start = seq * length + (here ^ span[index]) * rows
            log_place = pl.ds(pl.multiple_of(start, rows), rows)
            kept = lse_ref[0, log_place, :]
            for head in range(per):
                kept = jnp.where(log_lanes == pair * per + head, logs[head][here_rows], kept)
            lse_ref[0, log_place, :] = kept


def attend_back_kernel(head_dim, ids, qkv_ref, o_ref, g_ref, lse_ref, *rest):
    pieces, (out_ref, sums_ref) = rest[:-2], rest[-2:]
    here = ids[0]
    pair, seq = pl.program_id(1), pl.program_id(2)
    length, wide = o_ref.shape[1:]
    per = wide // head_dim
    rows = pieces[0].shape[1]
    lanes = lax.broadcasted_iota(jnp.int32, (1, wide), 1)
    log_lanes = lax.broadcasted_iota(jnp.int32, (1, lse_ref.shape[2]), 1)
    keys, values = qkv_ref[0, :, wide : 2 * wide], qkv_ref[0, :, 2 * wide :]
    everything = slice(None)
    back = head_dim**-0.5
    dk = jnp.zeros(keys.shape, f32)
    dv = jnp.zeros(keys.shape, f32)
    for first in range(0, len(pieces), 2):
        span = range(first, min(first + 2, len(pieces)))
        places = [piece_rows(here, piece, rows) for piece in span]
        queries = stack_pieces(qkv_ref, places, slice(0, wide))
        ups = stack_pieces(g_ref, places, everything)
        products = ups.astype(f32) * stack_pieces(o_ref, places, everything).astype(f32)
        starts = [seq * length + (here ^ piece) * rows for piece in span]
        log_places = [pl.ds(pl.multiple_of(at, rows), rows) for at in starts]
        logs = stack_pieces(lse_ref, log_places, everything)
        dq = None
        for head in range(per):
            mine = lanes // head_dim == head
            q_mine, g_mine = jnp.where(mine, queries, 0), jnp.where(mine, ups, 0)
            inner = jnp.sum(jnp.where(mine, products, 0.0), axis=1, keepdims=True)
            log = jnp.sum(
                jnp.where(log_lanes == pair * per + head, logs, 0.0), axis=1, keepdims=True
            )
            scores = dot_right_t(q_mine, keys) * (back * log2e)
            addend = jnp.concatenate([pieces[piece][head] for piece in span], axis=0)
            exact = jnp.exp2(scores + addend.astype(f32) - log)
            grads = (exact * (dot_right_t(g_mine, values) - inner)).astype(bf16)
            dv = dv + dot_left_t(exact.astype(bf16), g_mine)
            dk = dk + dot_left_t(grads, q_mine)
            part = dot(grads, keys)
            dq = part if dq is None else jnp.where(mine, part, dq)
        for index, place_ in enumerate(places):
            out_ref[0, place_, :wide] = (dq[index * rows : (index + 1) * rows] * back).astype(bf16)
    out_ref[0, :, wide : 2 * wide] = (dk * back).astype(bf16)
    out_ref[0, :, 2 * wide :] = dv.astype(bf16)
    sums = dot(jnp.ones((sums_ref.shape[2], length), bf16), out_ref[0])

    @pl.when(seq == 0)
    def _():
        sums_ref[0, 0] = sums

    @pl.when(seq > 0)
    def _():
        sums_ref[0, 0] += sums


def attention_specs(joined, mask_parts, turn=0):
    rows, length = mask_parts[0].shape[1:]

    def block(cols):
        return pl.BlockSpec((1, length, cols), lambda r, p, s, ids: (turn + r, s, p))

    logs = pl.BlockSpec((1, joined.shape[1], 128), lambda r, p, s, ids: (turn + r, 0, 0))
    mask = pl.BlockSpec((2, rows, length), lambda r, p, s, ids: (2 * p + (ids[1] ^ (turn + r)), 0, 0))
    return block, logs, [mask] * len(mask_parts)


def attend(ids, joined, mask_parts, seqs, head_dim, ties=()):
    tokens, cols = joined.shape[1:]
    block, logs, masks = attention_specs(joined, mask_parts)
    width = cols // 3
    return kernel_call(
        partial(attend_kernel, head_dim),
        ids,
        [joined, *mask_parts],
        ties,
        (2, width // 128, seqs),
        [block(384)] + masks,
        (block(128), logs),
        (
            jax.ShapeDtypeStruct((2, tokens, width), bf16),
            jax.ShapeDtypeStruct((2, tokens, 128), f32),
        ),
        cost=brief,
    )


def attend_back(
    ids, joined, attended, upstream, logs, mask_parts, turn, seqs, head_dim, ties=()
):
    tokens, cols = joined.shape[1:]
    count = cols // 384
    length = tokens // seqs
    block, log_block, masks = attention_specs(joined, mask_parts, turn)
    return kernel_call(
        partial(attend_back_kernel, head_dim),
        ids,
        [joined, attended, upstream, logs, *mask_parts],
        ties,
        (1, count, seqs),
        [block(384), block(128), block(128), log_block] + masks,
        (
            pl.BlockSpec((1, length, 384), lambda r, p, s, ids: (0, s, p)),
            pl.BlockSpec((1, 1, 8, 384), lambda r, p, s, ids: (r, p, 0, 0)),
        ),
        (
            jax.ShapeDtypeStruct((1, tokens, cols), bf16),
            jax.ShapeDtypeStruct((1, count, 8, 384), f32),
        ),
    )


def out_kernel(ids, att_ref, x_ref, vec_ref, *refs):
    pieces, (first_ref, low_ref, w_ref, sems) = (refs[:2], refs[2:4]), refs[4:]

    @pl.when(pl.program_id(0) == 0)
    def _():
        load = Loader(ids, sems)
        load.columns(pieces, 0, w_ref.shape[-1] // 2, w_ref)
        load.wait()

    attended = pair_order(ids[1], att_ref[0], att_ref[1], 128)
    first = x_ref[...].astype(f32) + (dot(attended, flat(w_ref)) + vector(vec_ref, "bias_out"))
    first_ref[...] = first
    gain, shift = vector(vec_ref, "gain_first"), vector(vec_ref, "shift_first")
    low_ref[...] = (norm_stats(first)[0] * gain + shift).astype(bf16)


def out_projection(ids, attended, pieces, token_rows, vectors, block, ties=()):
    tokens, width = token_rows.shape
    row = pl.BlockSpec((block, width), lambda i, ids: (i, 0))
    return kernel_call(
        out_kernel,
        ids,
        [attended, token_rows, vectors, *pieces[0], *pieces[1]],
        ties,
        (tokens // block,),
        [
            pl.BlockSpec((2, block, width // 2), lambda i, ids: (0, i, 0)),
            row,
            whole_block(vectors),
        ]
        + [any_block()] * 4,
        (row, row),
        (jax.ShapeDtypeStruct((tokens, width), f32), jax.ShapeDtypeStruct((tokens, width), bf16)),
        [place_shape(pieces[0][0], width), pltpu.SemaphoreType.DMA((4,))],
        cost=brief,
    )


def up_kernel(chunk, steps, ids, h_ref, b_ref, *refs):
    pieces, (act_ref, der_ref, w_ref, w_far_ref, sems) = (refs[:2], refs[2:4]), refs[4:]
    step = pl.program_id(0)
    block = act_ref.shape[1]
    cols = w_ref.shape[-1]

    @pl.when(step == 0)
    def _():
        load = Loader(ids, sems)
        start = pieces[0][0].shape[-1] - cols
        load.rows(pieces[0], start, cols, w_ref)
        load.rows(pieces[1], start, cols, w_far_ref)
        load.wait()

    def run(ref):
        lanes = pl.ds(pl.multiple_of((step % steps) * block, block), block)
        weights = ref[:, :, :, lanes].reshape(-1, block)
        bias = b_ref[0]
        for first in range(0, h_ref.shape[0], chunk):
            place_ = slice(first, first + chunk)
            gate = dot(h_ref[place_, :], weights) + bias
            share = 0.5 + 0.5 * lax.erf(gate * math.sqrt(0.5))
            bell = jnp.exp2((-0.5 * log2e) * (gate * gate)) * (1.0 / math.sqrt(2.0 * math.pi))
            act_ref[place_, :] = (gate * share).astype(bf16)
            der_ref[place_, :] = (share + gate * bell).astype(bf16)

    pl.when(step < steps)(lambda: run(w_ref))
    pl.when(step >= steps)(lambda: run(w_far_ref))


def up_projection(ids, hidden_low, pieces, bias, ties=()):
    tokens, width = hidden_low.shape
    half = bias.shape[2]
    block = width
    steps = half // block
    out = pl.BlockSpec((tokens, block), lambda j, ids: (0, (ids[1] ^ (j // steps)) * steps + j % steps))
    shape = jax.ShapeDtypeStruct((tokens, 2 * half), bf16)
    scratch = place_shape(pieces[0][0], half)
    return kernel_call(
        partial(up_kernel, 128, steps),
        ids,
        [hidden_low, bias, *pieces[0], *pieces[1]],
        ties,
        (2 * steps,),
        [
            whole_block(hidden_low),
            pl.BlockSpec((1, 1, block), lambda j, ids: (ids[1] ^ (j // steps), 0, j % steps)),
        ]
        + [any_block()] * 4,
        (out, out),
        (shape, shape),
        [scratch, scratch, pltpu.SemaphoreType.DMA((4,))],
        cost=brief,
    )


def down_kernel(blk, ids, *refs):
    pos_ref, cot_ref, act_ref, der_ref, first_ref, vec_ref = refs[:6]
    mine, other = refs[6:8], refs[8:10]
    outs, refs = refs[10 : 10 + blk], refs[10 + blk :]
    gss_ref, gdi_ref, gate_ref, sums_ref, up_ref, w_ref, sems = refs
    step = pl.program_id(0)
    here = ids[0]
    seqs, rows, width = first_ref.shape

    @pl.when(step == 0)
    def _():
        load = Loader(ids, sems)
        load.columns((mine, other), 0, width // 2, w_ref)
        load.wait()

    weights = flat(w_ref)
    cols = act_ref.shape[-1]
    normed_one = norm_stats(first_ref[...].reshape(-1, width))[0]
    hidden = normed_one * vector(vec_ref, "gain_first") + vector(vec_ref, "shift_first")
    product = dot(act_ref[...].reshape(-1, cols), weights)
    second = hidden + (product + vector(vec_ref, "bias_down"))
    normed, inverse = norm_stats(second)
    gain = vector(vec_ref, "gain_second")
    result = (normed * gain + vector(vec_ref, "shift_second")).astype(bf16)
    for piece, out in enumerate(outs):

        @pl.when(step == piece)
        def _():
            out[...] = result.reshape(out.shape)

    slots = pos_ref.shape[-1]
    token = lax.broadcasted_iota(jnp.int32, (rows, slots), 0) + (here ^ step) * rows
    upstream = jnp.concatenate(
        [
            dot(jnp.where(token == pos_ref[seq], 1.0, 0.0).astype(bf16), cot_ref[seq])
            for seq in range(seqs)
        ],
        axis=0,
    )
    grad = norm_pull(upstream, normed, inverse, gain)
    gss_ref[...] = grad.reshape(gss_ref.shape)
    low = grad.astype(bf16)
    gdi_ref[...] = low.reshape(gdi_ref.shape)
    add_sums(sums_ref, [low.astype(f32), upstream * normed, upstream])
    grad_gate = dot_right_t(low, weights) * der_ref[...].reshape(-1, cols).astype(f32)
    grad_gate = grad_gate.astype(bf16)
    gate_ref[...] = grad_gate.reshape(gate_ref.shape)
    add_sums(up_ref, [grad_gate.astype(f32)])


def down_projection(
    ids, active, slope, first_sum, pieces, vectors, marks, cot_values, seqs, blk, ties=()
):
    tokens, cols = active.shape
    width = first_sum.shape[1]
    length = tokens // seqs
    rows = length // blk

    def block(size):
        return pl.BlockSpec((seqs, rows, size), lambda d, ids: (0, ids[0] ^ d, 0))

    def shape(size, dtype):
        return jax.ShapeDtypeStruct((seqs, length, size), dtype)

    piece = jax.ShapeDtypeStruct((seqs, rows, width), bf16)
    sums = jax.ShapeDtypeStruct((8, width), f32)
    up_sums = jax.ShapeDtypeStruct((8, cols), f32)
    slots = marks.shape[-1]
    by_seq = [array.reshape(seqs, length, -1) for array in (active, slope, first_sum)]
    outs = kernel_call(
        partial(down_kernel, blk),
        ids,
        [marks, cot_values, *by_seq, vectors, *pieces[0], *pieces[1]],
        ties,
        (blk,),
        [
            whole_block(marks),
            pl.BlockSpec((seqs, slots, width), lambda d, ids: (ids[0], 0, 0)),
            block(cols),
            block(cols),
            block(width),
            whole_block(vectors),
        ]
        + [any_block()] * 4,
        [whole_block(piece)] * blk
        + [block(width), block(width), block(cols), whole_block(sums), whole_block(up_sums)],
        [piece] * blk + [shape(width, f32), shape(width, bf16), shape(cols, bf16), sums, up_sums],
        [place_shape(pieces[0][0], width), pltpu.SemaphoreType.DMA((4,))],
    )
    rest = outs[blk:]
    return outs[:blk], [array.reshape(tokens, -1) for array in rest[:3]], rest[3:]


def first_back_kernel(ids, gate_ref, gss_ref, first_ref, vec_ref, *refs):
    pieces, refs = (refs[:2], refs[2:4]), refs[4:]
    gfs_ref, branch_ref, att_ref, sums_ref, w_ref, w_out_ref, sems = refs
    width = gss_ref.shape[1]

    @pl.when(pl.program_id(0) == 0)
    def _():
        load = Loader(ids, sems)
        load.columns(pieces, width // 2, w_ref.shape[-1] // 2, w_ref)
        load.columns(pieces, 0, width // 2, w_out_ref)
        load.wait()

    grad_hidden = gss_ref[...] + dot_right_t(gate_ref[...], flat(w_ref))
    normed, inverse = norm_stats(first_ref[...])
    grad = norm_pull(grad_hidden, normed, inverse, vector(vec_ref, "gain_first"))
    gfs_ref[...] = grad
    low = grad.astype(bf16)
    branch_ref[...] = low
    grad_att = dot_right_t(low, flat(w_out_ref)).astype(bf16)
    att_ref[0], att_ref[1] = pair_split(ids[1], grad_att, 128)
    add_sums(sums_ref, [low.astype(f32), grad_hidden * normed, grad_hidden])


def first_back(ids, grad_gate, grad_second_sum, first_sum, pieces, vectors, block, ties=()):
    tokens, cols = grad_gate.shape
    width = first_sum.shape[1]

    def row(size):
        return pl.BlockSpec((block, size), lambda i, ids: (i, 0))

    def shape(size, dtype):
        return jax.ShapeDtypeStruct((tokens, size), dtype)

    sums = jax.ShapeDtypeStruct((8, width), f32)
    piece = pieces[0][0]
    return kernel_call(
        first_back_kernel,
        ids,
        [grad_gate, grad_second_sum, first_sum, vectors, *pieces[0], *pieces[1]],
        ties,
        (tokens // block,),
        [row(cols), row(width), row(width), whole_block(vectors)] + [any_block()] * 4,
        (
            row(width),
            row(width),
            pl.BlockSpec((2, block, width // 2), lambda i, ids: (0, i, 0)),
            whole_block(sums),
        ),
        (
            shape(width, f32),
            shape(width, bf16),
            jax.ShapeDtypeStruct((2, tokens, width // 2), bf16),
            sums,
        ),
        [place_shape(piece, cols), place_shape(piece, width), pltpu.SemaphoreType.DMA((8,))],
    )


def beside(array, devices, per):
    groups = array.reshape(devices, per, -1, array.shape[-1])
    return jnp.concatenate(
        [groups[:, index].reshape(-1, array.shape[-1]) for index in range(per)], axis=1
    )


def down_grad_kernel(devices, per, ids, act_ref, g_ref, keep_ref, send_ref):
    halves = half_split(ids[1], dot_left_t(act_ref[...], g_ref[...]))
    for half, out in zip(halves, (keep_ref, send_ref)):
        out[...] = (beside(half, devices, per) if per > 1 else half).astype(bf16)


def down_grad(ids, active, grad_down_in, devices, ties=()):
    tokens, cols = active.shape
    width = grad_down_in.shape[1]
    per, block = cols // width, width
    inside = (width // devices) % 8 == 0
    groups = per if inside else 1
    out = pl.BlockSpec((block // groups, groups * width // 2), lambda i, ids: (i, 0))
    shape = jax.ShapeDtypeStruct((cols // groups, groups * width // 2), bf16)
    halves = kernel_call(
        partial(down_grad_kernel, devices // per, groups),
        ids,
        [active, grad_down_in],
        ties,
        (cols // block,),
        [pl.BlockSpec((tokens, block), lambda i, ids: (0, i)), whole_block(grad_down_in)],
        (out, out),
        (shape, shape),
    )
    return halves if inside else [beside(half, devices, per) for half in halves]


def up_grad_kernel(ids, h_ref, g_ref, g_far_ref, keep_ref, send_ref):
    keep_ref[...] = dot_left_t(h_ref[...], g_ref[...]).astype(bf16)
    send_ref[...] = dot_left_t(h_ref[...], g_far_ref[...]).astype(bf16)


def up_grad(ids, hidden_low, grad_gate, block, ties=()):
    tokens, width = hidden_low.shape
    cols = grad_gate.shape[1] // 2
    steps = cols // block
    shape = jax.ShapeDtypeStruct((width, cols), bf16)
    out = pl.BlockSpec((width, block), lambda j, ids: (0, j))
    return kernel_call(
        up_grad_kernel,
        ids,
        [hidden_low, grad_gate, grad_gate],
        ties,
        (steps,),
        [
            whole_block(hidden_low),
            pl.BlockSpec((tokens, block), lambda j, ids: (0, ids[1] * steps + j)),
            pl.BlockSpec((tokens, block), lambda j, ids: (0, (1 - ids[1]) * steps + j)),
        ],
        (out, out),
        (shape, shape),
    )


def left_grad_kernel(
    ids,
    x_ref,
    g_ref,
    g_far_ref,
    att_ref,
    branch_ref,
    sums_ref,
    sums_far_ref,
    first_ref,
    second_ref,
    up_ref,
    *outs,
):
    core, step = ids[1], pl.program_id(0)
    attended = pair_order(core, att_ref[0], att_ref[1], 128)
    out_grads = half_split(core, dot_left_t(attended, branch_ref[...]))
    sums = [ref[0, step][:1] for ref in (sums_ref, sums_far_ref)]
    rows = [
        pair_order(core, sums[0][:, at : at + 128], sums[1][:, at : at + 128], 128)
        for at in (0, 256)
    ]
    rows += [first_ref[:3], second_ref[:3], up_ref[...]]
    used = sum(row.shape[0] for row in rows)
    rows = jnp.concatenate(rows + [jnp.zeros((16 - used, rows[0].shape[1]), f32)], axis=0)
    lanes = lax.broadcasted_iota(jnp.int32, (16, 128), 1)
    eye = lanes == lax.broadcasted_iota(jnp.int32, lanes.shape, 0)
    columns = dot_left_t(rows.astype(bf16), jnp.where(eye, 1.0, 0.0).astype(bf16))
    cut = outs[0].shape[1] - 128
    for turn, ref in enumerate((g_ref, g_far_ref)):
        grad = dot_left_t(x_ref[...], ref[0])
        first = jnp.concatenate([grad[:, :cut], columns], axis=1)
        second = jnp.concatenate([grad[:, cut:], out_grads[turn]], axis=1)
        outs[turn][...] = first.astype(bf16)
        outs[2 + turn][...] = second.astype(bf16)


def left_grad(ids, left, grads, attended, grad_branch, sums, totals, ties=()):
    tokens, width = left.shape
    cut = grads[0].shape[2] - 384
    sizes = [cut + 128] * 2 + [384 + width // 2] * 2
    return kernel_call(
        left_grad_kernel,
        ids,
        [left, *grads, attended, grad_branch, *sums, *totals],
        ties,
        (width // 256,),
        [
            pl.BlockSpec((tokens, 256), lambda i, ids: (0, i)),
            *[whole_block(grad) for grad in grads],
            pl.BlockSpec((2, tokens, 128), lambda i, ids: (0, 0, i)),
            whole_block(grad_branch),
            *[whole_block(array) for array in sums],
        ]
        + [pl.BlockSpec((array.shape[0], 256), lambda i, ids: (0, i)) for array in totals],
        [pl.BlockSpec((256, size), lambda i, ids: (i, 0)) for size in sizes],
        [jax.ShapeDtypeStruct((width, size), bf16) for size in sizes],
    )


def input_grad_kernel(blk, ids, g_ref, g_far_ref, gfs_ref, *refs):
    pieces, refs = (refs[:2], refs[2:4]), refs[4:]
    outs, (w_ref, w_far_ref, sems) = refs[:blk], refs[blk:]
    step = pl.program_id(0)

    @pl.when(step == 0)
    def _():
        load = Loader(ids, sems)
        load.rows(pieces[0], 0, w_ref.shape[-1], w_ref)
        load.rows(pieces[1], 0, w_ref.shape[-1], w_far_ref)
        load.wait()

    width = gfs_ref.shape[-1]
    total = gfs_ref[...].reshape(-1, width)
    for ref, weights in ((g_ref, w_ref), (g_far_ref, w_far_ref)):
        total = total + dot_right_t(ref[...].reshape(-1, ref.shape[-1]), flat(weights))
    for piece, out in enumerate(outs):

        @pl.when(step == piece)
        def _():
            out[...] = total.astype(bf16).reshape(out.shape)


def input_grad(ids, grads, grad_first_sum, pieces, seqs, blk, ties=()):
    tokens, width = grad_first_sum.shape
    length = tokens // seqs
    rows = length // blk
    cols = grads[0].shape[2]
    piece = jax.ShapeDtypeStruct((seqs, rows, width), bf16)
    shape = place_shape(pieces[0][0], cols)
    pieces = [*pieces[0], *pieces[1]]
    return kernel_call(
        partial(input_grad_kernel, blk),
        ids,
        [
            *[grad.reshape(seqs, length, cols) for grad in grads],
            grad_first_sum.reshape(seqs, length, width),
            *pieces,
        ],
        ties,
        (blk,),
        [
            *[pl.BlockSpec((seqs, rows, cols), lambda d, ids: (0, ids[0] ^ d, 0))] * 2,
            pl.BlockSpec((seqs, rows, width), lambda d, ids: (0, ids[0] ^ d, 0)),
        ]
        + [any_block()] * len(pieces),
        [whole_block(piece)] * blk,
        [piece] * blk,
        [shape, shape, pltpu.SemaphoreType.DMA((len(pieces),))],
    )


class Grid:
    def __init__(self, mesh):
        batch, blk = mesh.shape["batch"], mesh.shape["blk"]
        self.sizes = {"z": batch // 2, "y": 2, "x": blk // 2, "c": 2}
        self.strides = {"c": 1, "x": 2, "y": blk, "z": 2 * blk}
        self.total = batch * blk
        self.blk = blk

    def digit(self, name):
        index = lax.axis_index("batch") * self.blk + lax.axis_index("blk")
        return (index // self.strides[name]) % self.sizes[name]

    def swap(self, array, name, delta=1):
        size, stride = self.sizes[name], self.strides[name]
        pairs = []
        for index in range(self.total):
            here = (index // stride) % size
            pairs.append((index, index + ((here ^ delta) - here) * stride))
        return lax.ppermute(array, both, pairs)

    def swap_blk(self, array, delta):
        pairs = [(index, index ^ delta) for index in range(self.total)]
        return lax.ppermute(array, both, pairs)


def place(parts, index):
    if len(parts) == 1:
        return parts[0][None]
    rows = []
    for target in range(len(parts)):
        row = parts[0]
        for delta in range(1, len(parts)):
            row = jnp.where(index == target ^ delta, parts[delta], row)
        rows.append(row)
    return jnp.stack(rows)


def pick(array, index):
    return lax.dynamic_index_in_dim(array, index, axis=0, keepdims=False)


def gather_core(grid, mine, other):
    cols = mine.shape[1]
    return place([mine, grid.swap(other, "c")], grid.digit("c")).reshape(-1, cols)


def gather_step(grid, run, held, name, *ties):
    parts = [grid.swap(held, name, d) for d in range(1, grid.sizes[name])]
    return place_parts(run, [held, *parts], name, ties)


def gather_last(grid, held, name):
    far = grid.swap(held, name)
    if held.shape[1] % 16 == 0:
        return [held, far]
    where = grid.digit(name)
    whole = jnp.moveaxis(place([held, far], where), 0, 1).reshape(4, 2, -1, held.shape[2])
    return [lax.dynamic_index_in_dim(whole, where ^ d, 1, keepdims=False) for d in range(2)]


def gather_pieces(grid, run, held, *ties):
    near, far = held
    if ties:
        (far,) = after(run, [far], *ties)
    return [[near, far], [grid.swap(near, "c"), grid.swap(far, "c")]]


def add_low(*parts):
    total = parts[0].astype(f32)
    for part in parts[1:]:
        total = total + part.astype(f32)
    return total


def fold_kernel(count, groups, ids, *refs):
    outs = refs[len(refs) - count :]
    refs = list(refs[: len(refs) - count])
    for out in outs:
        sums = []
        for terms in groups:
            picked, refs = refs[:terms], refs[terms:]
            total = picked[0][...].astype(f32)
            for ref in picked[1:]:
                total = total + ref[...].astype(f32)
            sums.append(total.astype(out.dtype))
        out[...] = jnp.concatenate(sums, axis=-1).reshape(out.shape)


def fold(ids, which, groups, ties):
    outer, count, rows, unused = groups[0][0].shape
    steps = 2 if outer % 2 == 0 else 1
    part = outer // steps

    def term_block(cols, delta):
        return pl.BlockSpec((part, 1, rows, cols), lambda i, ids: (i, ids[which] ^ delta, 0, 0))

    terms = [term for group in groups for term in group]
    cols = sum(group[0].shape[3] for group in groups)
    shape = jax.ShapeDtypeStruct((outer, rows, cols), bf16)
    return kernel_call(
        partial(fold_kernel, count, [len(group) for group in groups]),
        ids,
        [term for delta in range(count) for term in terms],
        ties,
        (steps,),
        [term_block(term.shape[3], delta) for delta in range(count) for term in terms],
        [pl.BlockSpec((part, rows, cols), lambda i, ids: (i, 0, 0))] * count,
        [shape] * count,
    )


class Scatter:
    def __init__(self, grid, ids, pairs, order):
        self.grid, self.ids, self.order = grid, ids, list(order)
        sizes = grid.sizes
        self.left = [("z", sizes["z"]), ("y", sizes["y"]), ("x", sizes["x"])]
        self.last = 2 * (pairs[0][0].shape[0] // grid.total)
        self.groups = [[keep, grid.swap(send, "c")] for keep, send in pairs]

    def join(self, other):
        self.groups = self.groups + other.groups
        return self

    def shaped(self, *shape):
        return [[term.reshape(*shape, term.shape[-1]) for term in group] for group in self.groups]

    def step(self, ties=()):
        name = self.order.pop(0)
        index = [left for left, unused in self.left].index(name)
        count = self.left[index][1]
        outer = math.prod(size for unused, size in self.left[:index])
        inner = math.prod(size for unused, size in self.left[index + 1 :]) * self.last
        sums = fold(self.ids, id_of[name], self.shaped(outer, count, inner), ties)
        self.left.pop(index)
        sent = [self.grid.swap(sums[delta], name, delta) for delta in range(1, count)]
        self.groups = [[sums[0], *sent]]

    def end(self, ties=()):
        mine, other = fold(self.ids, id_of["c"], self.shaped(1, 2, self.last // 2), ties)
        mine, other = [array.reshape(array.shape[1:]) for array in (mine, other)]
        return mine.astype(f32), self.grid.swap(other, "c").astype(f32)


def in_order(core, mine, other):
    return jnp.where(core == 0, mine, other), jnp.where(core == 0, other, mine)


def local(
    grid,
    inputs,
    w_qkv,
    bias_query,
    bias_value,
    w_out,
    bias_out,
    gain_first,
    shift_first,
    w_up,
    bias_up,
    w_down,
    bias_down,
    gain_second,
    shift_second,
    dam_mask,
    positions,
    counts,
    cot_values,
):
    groups, block_rows, width = inputs.shape
    head_count = dam_mask.shape[0]
    head_dim = width // head_count
    blk = grid.blk
    seqs = groups // blk
    length = blk * block_rows
    tokens = seqs * length
    here, core = lax.axis_index("blk"), grid.digit("c")
    ids = Run(jnp.stack([here, core] + [grid.digit(name) for name in "yzx"]).astype(jnp.int32))
    rows = w_qkv.shape[0]
    up_per = bias_up.shape[0] // rows
    half = width // 2
    pairs = width // 256

    vectors = (
        bias_query,
        bias_value,
        bias_out,
        gain_first,
        shift_first,
        bias_down,
        gain_second,
        shift_second,
    )
    stacked = jnp.concatenate(
        [
            jnp.stack(vectors),
            bias_up.reshape(rows, up_per).T,
            jnp.zeros((16 - len(vectors) - up_per, rows), bf16),
        ]
    )
    addend = jnp.where(dam_mask > 0, 0.0, masked_score).astype(bf16)
    halves = split_weights(ids, w_qkv, stacked, w_out, w_up, w_down)
    first_near, second_near, down_near = [gather_core(grid, *pair) for pair in halves]

    def over_x(held):
        return gather_step(grid, ids, held, "x").reshape(-1, held.shape[1])

    first_near = over_x(first_near)
    event = ids.token

    by_home = inputs.reshape(blk, seqs, block_rows, width)
    parts = [pick(by_home, here ^ delta) for delta in range(blk)]
    parts[2:] = after(ids, parts[2:], event)
    parts[1:] = [grid.swap_blk(parts[delta], delta) for delta in range(1, blk)]
    (addend,) = after(ids, [addend], event)
    mask_parts = [addend, grid.swap(addend, "c")]
    second_near = over_x(second_near)
    ties = [ids.token]
    down_near = over_x(down_near)
    ties.append(ids.token)

    first_z = gather_step(grid, ids, first_near, "z", *ties, *parts[2:])
    (second_near,) = after(ids, [second_near], ids.token)
    first_y = gather_last(grid, first_z, "y")
    first_pieces = gather_pieces(grid, ids, first_y)
    ties = []
    if grid.sizes["x"] > 1:
        far = grid.swap(addend, "x")
        mask_parts += [far, grid.swap(far, "c")]
        ties = [far]
    second_z = gather_step(grid, ids, second_near, "z", *ties)
    (down_near,) = after(ids, [down_near], ids.token)
    second_y = gather_last(grid, second_z, "y")
    token_rows, vector_rows, joined = qkv_projection(
        ids, parts, first_pieces, 3 * half, ties=[ids.token]
    )
    token_rows = token_rows.reshape(tokens, width)
    first_row = len(vectors)
    up_bias = vector_rows[first_row : first_row + up_per].T.reshape(2, 1, -1)

    attended, logs = attend(
        ids, joined, mask_parts, seqs, head_dim, ties=[ids.token]
    )
    down_z = gather_step(grid, ids, down_near, "z", ids.token)
    down_y = gather_last(grid, down_z, "y")
    second_pieces = gather_pieces(grid, ids, second_y, ids.token)
    first_sum, hidden_low = out_projection(
        ids, attended, second_pieces, token_rows, vector_rows, 2 * block_rows
    )
    active, slope = up_projection(ids, hidden_low, second_pieces, up_bias)
    down_pieces = gather_pieces(grid, ids, down_y, ids.token)

    my_positions = pick(positions.reshape(blk, seqs, -1), here)
    my_counts = pick(counts.reshape(blk, seqs), here)
    live = jnp.arange(positions.shape[1], dtype=jnp.int32)[None, :] < my_counts[:, None]
    marks = jnp.where(live, my_positions, -1)[:, None, :]
    result, (grad_second_sum, grad_down_in, grad_gate), (second_sums, up_sums) = down_projection(
        ids, active, slope, first_sum, down_pieces, vector_rows, marks, cot_values, seqs, blk
    )

    def home(pieces):
        return [pieces[0]] + [grid.swap_blk(pieces[delta], delta) for delta in range(1, blk)]

    result = home(result)
    down_halves = down_grad(ids, active, grad_down_in, grid.total)
    up_halves = up_grad(ids, hidden_low, grad_gate, width, ties=[ids.token])
    up_sum = Scatter(grid, ids, [up_halves], "yxz")
    ffn_sum = Scatter(grid, ids, [down_halves], "xyz")
    ffn_sum.step([ids.token])
    up_sum.step([ids.token])
    grad_first_sum, grad_branch, grad_attended, first_sums = first_back(
        ids,
        grad_gate,
        grad_second_sum,
        first_sum,
        second_pieces,
        vector_rows,
        2 * block_rows,
        ties=[ids.token],
    )
    result = after(ids, result, ids.token)
    def back(turn):
        return attend_back(
            ids,
            joined,
            attended,
            grad_attended,
            logs,
            mask_parts,
            turn,
            seqs,
            head_dim,
            ties=[ids.token],
        )

    far_grads, far_sums = back(1)
    ffn_sum.step([ids.token])
    up_sum.step([ids.token])
    near_grads, near_sums = back(0)
    grads, grad_sums = (near_grads, far_grads), (near_sums, far_sums)
    ffn_sum = up_sum.join(ffn_sum)
    ffn_sum.step([ids.token])
    up_rows = up_sums[0].reshape(width, up_per).T
    totals = [first_sums, second_sums, up_rows]
    halves = left_grad(
        ids, token_rows, grads, attended, grad_branch, grad_sums, totals, ties=[ids.token]
    )
    one_sum = Scatter(grid, ids, [halves[:2]], "xyz")
    two_sum = Scatter(grid, ids, [halves[2:]], "yxz")
    one_sum.step([ids.token])
    two_sum.step([ids.token])
    sent = input_grad(ids, grads, grad_first_sum, first_pieces, seqs, blk, ties=[ids.token])
    one_sum.step([ids.token])
    two_sum.step([ids.token])
    grad_inputs = home([sent[0], *after(ids, sent[1:], ids.token)])
    activations = place_parts(ids, result, "here", [ids.token])
    activations = activations.reshape(groups, block_rows, width)
    att_sum = one_sum.join(two_sum)
    att_sum.step([ids.token])
    share_ffn = ffn_sum.end([ids.token])
    grad_inputs = widen_parts(ids, grad_inputs, "here", [ids.token])
    grad_inputs = grad_inputs.reshape(groups, block_rows, width)
    share_att = att_sum.end([ids.token])

    cut = near_grads.shape[2] - 384
    share_qkv = [
        jnp.concatenate([share[:, :cut], share[:, cut + 128 : cut + 512]], axis=1)
        for share in share_att
    ]
    by_core = jnp.stack(in_order(core, *share_qkv), axis=0).reshape(2, rows, pairs, 3, 128)
    share_qkv = by_core.transpose(1, 3, 2, 0, 4).reshape(rows, 3 * width)
    share_out = jnp.concatenate(in_order(core, *[share[:, cut + 512 :] for share in share_att]), axis=1)
    up_cols = up_halves[0].shape[1]
    share_up = [share[:, :up_cols] for share in share_ffn]
    share_down = [
        share[:, up_cols:].reshape(rows, up_per, half).transpose(1, 0, 2).reshape(-1, half)
        for share in share_ffn
    ]
    shares = share_att[0][:, cut : cut + 128]
    share_vectors = [shares[:, index] for index in range(len(vectors))]
    share_bias_up = shares[:, len(vectors) : len(vectors) + up_per].reshape(-1)
    (
        share_bias_query,
        share_bias_value,
        share_bias_out,
        share_gain_first,
        share_shift_first,
        share_bias_down,
        share_gain_second,
        share_shift_second,
    ) = share_vectors
    return (
        activations,
        grad_inputs,
        share_qkv,
        share_bias_query,
        share_bias_value,
        share_out,
        share_bias_out,
        share_gain_first,
        share_shift_first,
        jnp.concatenate(in_order(core, *share_up), axis=1),
        share_bias_up,
        jnp.concatenate(in_order(core, *share_down), axis=1),
        share_bias_down,
        share_gain_second,
        share_shift_second,
    )


def solution(mesh):
    sharded = P(both)
    rows = P(both, None)
    whole = P("batch", "blk", None)
    return jax.shard_map(
        partial(local, Grid(mesh)),
        mesh=mesh,
        in_specs=(
            whole,
            rows,
            sharded,
            sharded,
            rows,
            sharded,
            sharded,
            sharded,
            rows,
            sharded,
            rows,
            sharded,
            sharded,
            sharded,
            P(None, "blk", None),
            P("batch", None),
            P("batch"),
            P("batch", None, None),
        ),
        out_specs=(
            whole,
            whole,
            rows,
            sharded,
            sharded,
            rows,
            sharded,
            sharded,
            sharded,
            rows,
            sharded,
            rows,
            sharded,
            sharded,
            sharded,
        ),
        check_vma=False,
    )
```

```python
import math
from functools import partial

import jax
import jax.numpy as jnp
from jax import lax
from jax.experimental import pallas as pl
from jax.experimental.pallas import tpu as pltpu
from jax.sharding import PartitionSpec as P

norm_eps = 1e-06
masked_score = -1e30
f32 = jnp.float32
bf16 = jnp.bfloat16
both = ("batch", "blk")
log2e = math.log2(math.e)
long, brief, least = 10**11, 100000000000, 100000000000
roomy = pltpu.CompilerParams(vmem_limit_bytes=48 << 20)
vector_names = (
    "bias_query",
    "bias_value",
    "bias_out",
    "gain_first",
    "shift_first",
    "bias_down",
    "gain_second",
    "shift_second",
)
row_of = {name: index for index, name in enumerate(vector_names)}


def dot(left, right):
    return jnp.dot(left, right, preferred_element_type=f32)


def dot_right_t(left, right):
    return lax.dot_general(left, right, (((1,), (1,)), ((), ())), preferred_element_type=f32)


def dot_left_t(left, right):
    return lax.dot_general(left, right, (((0,), (0,)), ((), ())), preferred_element_type=f32)


def norm_stats(rows):
    center = jnp.mean(rows, axis=-1, keepdims=True)
    centered = rows - center
    inverse = lax.rsqrt(jnp.mean(centered * centered, axis=-1, keepdims=True) + norm_eps)
    return centered * inverse, inverse


def norm_pull(upstream, normed, inverse, gain):
    scaled = upstream * gain
    inner = jnp.mean(scaled, axis=-1, keepdims=True)
    projected = jnp.mean(scaled * normed, axis=-1, keepdims=True)
    return inverse * (scaled - inner - normed * projected)


def vector(ref, name):
    index = row_of[name]
    return ref[index : index + 1, :]


def add_sums(sums_ref, rows):
    total = jnp.concatenate(
        [jnp.sum(row, axis=0, keepdims=True) for row in rows]
        + [jnp.zeros((sums_ref.shape[0] - len(rows), sums_ref.shape[1]), f32)],
        axis=0,
    )

    @pl.when(pl.program_id(0) == 0)
    def _():
        sums_ref[...] = total

    @pl.when(pl.program_id(0) > 0)
    def _():
        sums_ref[...] += total


def piece_rows(here, piece, rows):
    return pl.ds(pl.multiple_of((here ^ piece) * rows, rows), rows)


def stack_pieces(ref, places, cols):
    return jnp.concatenate([ref[0, place_, cols] for place_ in places], axis=0)


def any_block():
    return pl.BlockSpec(memory_space=pl.ANY)


def whole_block(array):
    return pl.BlockSpec(array.shape, lambda *unused: (0,) * len(array.shape))


def pair_order(core, first, second, wide):
    blocks = []
    for start in range(0, first.shape[-1], wide):
        left, right = first[:, start : start + wide], second[:, start : start + wide]
        blocks += [jnp.where(core == 0, left, right), jnp.where(core == 0, right, left)]
    return jnp.concatenate(blocks, axis=1)


def pair_split(core, array, wide):
    outs = []
    for turn in range(2):
        outs.append(
            jnp.concatenate(
                [
                    jnp.where(
                        core == turn,
                        array[:, start : start + wide],
                        array[:, start + wide : start + 2 * wide],
                    )
                    for start in range(0, array.shape[1], 2 * wide)
                ],
                axis=1,
            )
        )
    return outs


def half_split(core, array):
    half = array.shape[1] // 2
    left, right = array[:, :half], array[:, half:]
    return jnp.where(core == 0, left, right), jnp.where(core == 0, right, left)


class Run:
    def __init__(self, ids):
        self.ids, self.token = ids, None


id_of = {"here": 0, "c": 1, "y": 2, "z": 3, "x": 4}
token_shape = jax.ShapeDtypeStruct((8, 128), f32)


def after(run, arrays, *ties):
    shapes = [jax.ShapeDtypeStruct(array.shape, array.dtype) for array in arrays]

    def body(*refs):
        refs[-1][...] = jnp.zeros(token_shape.shape, f32)

    *arrays, run.token = pl.pallas_call(
        body,
        out_shape=shapes + [token_shape],
        in_specs=[any_block()] * (len(arrays) + len(ties)),
        out_specs=[any_block()] * len(arrays) + [pl.BlockSpec(memory_space=pltpu.VMEM)],
        input_output_aliases={index: index for index in range(len(arrays))},
    )(*arrays, *ties)
    return arrays


def kernel_call(
    kernel, run, arrays, ties, grid, in_specs, out_specs, out_shape, scratch=(), cost=long
):
    several = isinstance(out_shape, (list, tuple))
    out_specs, out_shape = [
        list(value) if several else [value] for value in (out_specs, out_shape)
    ]
    count, outs = 1 + len(arrays), len(out_shape)

    def body(*refs):
        inputs, refs = refs[:count], refs[count + len(ties) :]
        refs[outs][...] = jnp.zeros(token_shape.shape, f32)
        kernel(*inputs, *refs[:outs], *refs[outs + 1 :])

    *results, run.token = pl.pallas_call(
        body,
        out_shape=out_shape + [token_shape],
        grid_spec=pltpu.PrefetchScalarGridSpec(
            num_scalar_prefetch=1,
            grid=grid,
            in_specs=list(in_specs) + [any_block()] * len(ties),
            out_specs=out_specs + [whole_block(token_shape)],
            scratch_shapes=scratch,
        ),
        compiler_params=roomy,
        cost_estimate=pl.CostEstimate(flops=cost, bytes_accessed=1024, transcendentals=0),
    )(run.ids, *arrays, *ties)
    return results if several else results[0]


def place_kernel(digit, count, ids, *refs):
    parts, (out, sems) = refs[:count], refs[count:]
    copies = [
        pltpu.make_async_copy(part, out.at[ids[digit] ^ delta], sems.at[delta])
        for delta, part in enumerate(parts)
    ]
    for copy in copies:
        copy.start()
    for copy in copies:
        copy.wait()


def place_parts(run, parts, digit, ties=()):
    count = len(parts)
    return kernel_call(
        partial(place_kernel, id_of[digit], count),
        run,
        parts,
        ties,
        (1,),
        [whole_block(part) for part in parts],
        any_block(),
        jax.ShapeDtypeStruct((count, *parts[0].shape), parts[0].dtype),
        [pltpu.SemaphoreType.DMA((count,))],
        cost=least,
    )


def widen_kernel(digit, count, ids, *refs):
    for delta in range(count):
        refs[count][ids[digit] ^ delta] = refs[delta][...].astype(f32)


def widen_parts(run, parts, digit, ties=()):
    count = len(parts)
    shape = jax.ShapeDtypeStruct((count, *parts[0].shape), f32)
    return kernel_call(
        partial(widen_kernel, id_of[digit], count),
        run,
        parts,
        ties,
        (1,),
        [whole_block(part) for part in parts],
        whole_block(shape),
        shape,
    )


def addend_kernel(ids, mask_ref, out_ref):
    out_ref[...] = jnp.where(mask_ref[...] > 0, 0.0, masked_score).astype(bf16)


def mask_addend(run, mask, ties):
    heads, rows, cols = mask.shape
    block = pl.BlockSpec((heads // 4, rows, cols), lambda i, ids: (i, 0, 0))
    shape = jax.ShapeDtypeStruct(mask.shape, bf16)
    return kernel_call(addend_kernel, run, [mask], ties, (4,), [block], block, shape)


class Loader:
    def __init__(self, ids, sems, digit="y"):
        self.core, self.digit = ids[id_of["c"]], ids[id_of[digit]]
        self.sems, self.copies = sems, []

    def put(self, source, target):
        copy = pltpu.make_async_copy(source, target, self.sems.at[len(self.copies)])
        copy.start()
        self.copies.append(copy)

    def rows(self, pieces, start, size, target):
        for turn, piece in enumerate(pieces):
            self.put(piece.at[:, :, pl.ds(start, size)], target.at[:, self.digit ^ turn])

    def columns(self, both_cores, start, size, target):
        for other, pieces in enumerate(both_cores):
            lanes = pl.ds(pl.multiple_of((self.core ^ other) * size, 128), size)
            for turn, piece in enumerate(pieces):
                self.put(
                    piece.at[:, :, pl.ds(start, size)], target.at[:, self.digit ^ turn, :, lanes]
                )

    def wait(self):
        for copy in self.copies:
            copy.wait()


def flat(ref, first=None, count=None):
    value = ref[...] if first is None else ref[pl.ds(first, count)]
    return value.reshape(-1, value.shape[-1])


def place_shape(piece, cols):
    return pltpu.VMEM((piece.shape[0], 2, piece.shape[1], cols), bf16)


def split_kernel(ids, qkv_ref, vec_ref, out_ref, up_ref, down_ref, *outs):
    core = ids[1]
    width = down_ref.shape[1]
    lanes = lax.broadcasted_iota(jnp.int32, (vec_ref.shape[0], 128), 1)
    eye = lanes == lax.broadcasted_iota(jnp.int32, lanes.shape, 0)
    columns = dot_left_t(vec_ref[...], jnp.where(eye, 1.0, 0.0).astype(bf16)).astype(bf16)
    for turn in range(2):
        first, second, down = outs[3 * turn : 3 * turn + 3]
        pairs = []
        for start in range(0, width, 256):
            for part in range(3):
                left = qkv_ref[:, part * width + start : part * width + start + 128]
                right = qkv_ref[:, part * width + start + 128 : part * width + start + 256]
                pairs.append(jnp.where(core == turn, left, right))
        out_half, second[...] = [half_split(core, ref[...])[turn] for ref in (out_ref, up_ref)]
        first[...] = jnp.concatenate(pairs + [columns, out_half], axis=1)
        down[...] = half_split(core, down_ref[...])[turn]


def split_weights(ids, w_qkv, vectors, w_out, w_up, w_down, ties=()):
    rows, cols = w_qkv.shape
    arrays = [w_qkv, vectors, w_out, w_up, w_down]
    shapes = [
        jax.ShapeDtypeStruct((rows, cols // 2 + 128 + w_out.shape[1] // 2), bf16),
        jax.ShapeDtypeStruct((rows, w_up.shape[1] // 2), bf16),
        jax.ShapeDtypeStruct((w_down.shape[0], w_down.shape[1] // 2), bf16),
    ] * 2
    outs = kernel_call(
        split_kernel,
        ids,
        arrays,
        ties,
        (1,),
        [whole_block(array) for array in arrays],
        [whole_block(shape) for shape in shapes],
        shapes,
        cost=least,
    )
    return list(zip(outs[:3], outs[3:]))


def qkv_kernel(blk, ids, joined_ref, *refs):
    parts, refs = refs[:blk], refs[blk:]
    pieces, refs = (refs[:2], refs[2:4]), refs[4:]
    x_ref, vec_ref, out_ref, w_ref, w_far_ref, v_ref, sems = refs
    here, core = ids[0], ids[1]
    step = pl.program_id(0)
    cols = out_ref.shape[2]
    block = out_ref.shape[1]

    @pl.when(step == 0)
    def _():
        load = Loader(ids, sems)
        for piece, part in enumerate(parts):
            load.put(part, x_ref.at[:, here ^ piece])
        load.rows(pieces[0], 0, cols, w_ref)
        load.rows(pieces[1], 0, cols, w_far_ref)
        load.rows(pieces[0], cols, 128, v_ref)
        load.wait()
        vec_ref[...] = flat(v_ref).astype(f32).T[: vec_ref.shape[0]]

    per_seq = x_ref.shape[1] // 2
    rows = x_ref[step // per_seq, pl.ds(2 * (step % per_seq), 2)].reshape(-1, x_ref.shape[-1])
    for turn, weights in enumerate((w_ref, w_far_ref)):
        bias = []
        for start in range(0, vec_ref.shape[1], 256):
            for name in ("bias_query", None, "bias_value"):
                if name is None:
                    bias.append(jnp.zeros((1, 128), f32))
                    continue
                row = vector(vec_ref, name)
                bias.append(
                    jnp.where(
                        core == turn, row[:, start : start + 128], row[:, start + 128 : start + 256]
                    )
                )
        total = dot(rows, flat(weights)) + jnp.concatenate(bias, axis=1)
        low = total.astype(bf16)
        out_ref[turn] = low
        joined_ref[turn, pl.ds(pl.multiple_of(step * block, block), block), :] = low


def attend_kernel(head_dim, pair, seq, ids, qkv_ref, *rest):
    pieces, (o_ref, lse_ref) = rest[:-2], rest[-2:]
    here = ids[0]
    length, wide = o_ref.shape[1:]
    per = wide // head_dim
    rows = pieces[0].shape[1]
    lanes = lax.broadcasted_iota(jnp.int32, (1, wide), 1)
    log_lanes = lax.broadcasted_iota(jnp.int32, (1, lse_ref.shape[2]), 1)
    keys, values = qkv_ref[0, :, wide : 2 * wide], qkv_ref[0, :, 2 * wide :]
    for first in range(0, len(pieces), 4):
        span = range(first, min(first + 4, len(pieces)))
        places = [piece_rows(here, piece, rows) for piece in span]
        queries = stack_pieces(qkv_ref, places, slice(0, wide))
        out, logs = None, []
        for head in range(per):
            mine = lanes // head_dim == head
            scores = dot_right_t(jnp.where(mine, queries, 0), keys) * (head_dim**-0.5 * log2e)
            addend = jnp.concatenate([pieces[piece][head] for piece in span], axis=0)
            scores = scores + addend.astype(f32)
            top = jnp.max(scores, axis=1, keepdims=True)
            weights = jnp.exp2(scores - top)
            total = jnp.sum(weights, axis=1, keepdims=True)
            part = dot(weights.astype(bf16), values) * (1.0 / total)
            out = part if out is None else jnp.where(mine, part, out)
            logs.append(top + jnp.log2(total))
        for index, place_ in enumerate(places):
            here_rows = slice(index * rows, (index + 1) * rows)
            o_ref[0, place_, :] = out[here_rows].astype(bf16)
            start = seq * length + (here ^ span[index]) * rows
            log_place = pl.ds(pl.multiple_of(start, rows), rows)
            kept = lse_ref[0, log_place, :]
            for head in range(per):
                kept = jnp.where(log_lanes == pair * per + head, logs[head][here_rows], kept)
            lse_ref[0, log_place, :] = kept


def attend_back_kernel(head_dim, ids, qkv_ref, o_ref, g_ref, lse_ref, *rest):
    pieces, (out_ref, sums_ref) = rest[:-2], rest[-2:]
    here = ids[0]
    pair, seq = pl.program_id(1), pl.program_id(2)
    length, wide = o_ref.shape[1:]
    per = wide // head_dim
    rows = pieces[0].shape[1]
    lanes = lax.broadcasted_iota(jnp.int32, (1, wide), 1)
    log_lanes = lax.broadcasted_iota(jnp.int32, (1, lse_ref.shape[2]), 1)
    keys, values = qkv_ref[0, :, wide : 2 * wide], qkv_ref[0, :, 2 * wide :]
    everything = slice(None)
    back = head_dim**-0.5
    dk = jnp.zeros(keys.shape, f32)
    dv = jnp.zeros(keys.shape, f32)
    for first in range(0, len(pieces), 4):
        span = range(first, min(first + 4, len(pieces)))
        places = [piece_rows(here, piece, rows) for piece in span]
        queries = stack_pieces(qkv_ref, places, slice(0, wide))
        ups = stack_pieces(g_ref, places, everything)
        products = ups.astype(f32) * stack_pieces(o_ref, places, everything).astype(f32)
        starts = [seq * length + (here ^ piece) * rows for piece in span]
        log_places = [pl.ds(pl.multiple_of(at, rows), rows) for at in starts]
        logs = stack_pieces(lse_ref, log_places, everything)
        dq = None
        for head in range(per):
            mine = lanes // head_dim == head
            q_mine, g_mine = jnp.where(mine, queries, 0), jnp.where(mine, ups, 0)
            inner = jnp.sum(jnp.where(mine, products, 0.0), axis=1, keepdims=True)
            log = jnp.sum(
                jnp.where(log_lanes == pair * per + head, logs, 0.0), axis=1, keepdims=True
            )
            scores = dot_right_t(q_mine, keys) * (back * log2e)
            addend = jnp.concatenate([pieces[piece][head] for piece in span], axis=0)
            exact = jnp.exp2(scores + addend.astype(f32) - log)
            grads = (exact * (dot_right_t(g_mine, values) - inner)).astype(bf16)
            dv = dv + dot_left_t(exact.astype(bf16), g_mine)
            dk = dk + dot_left_t(grads, q_mine)
            part = dot(grads, keys)
            dq = part if dq is None else jnp.where(mine, part, dq)
        for index, place_ in enumerate(places):
            out_ref[0, place_, :wide] = (dq[index * rows : (index + 1) * rows] * back).astype(bf16)
    out_ref[0, :, wide : 2 * wide] = (dk * back).astype(bf16)
    out_ref[0, :, 2 * wide :] = dv.astype(bf16)
    sums = dot(jnp.ones((sums_ref.shape[2], length), bf16), out_ref[0])

    @pl.when(seq == 0)
    def _():
        sums_ref[0, 0] = sums

    @pl.when(seq > 0)
    def _():
        sums_ref[0, 0] += sums


def attention_specs(joined, mask_parts, turn=0):
    rows, length = mask_parts[0].shape[1:]

    def block(cols):
        return pl.BlockSpec((1, length, cols), lambda r, p, s, ids: (turn + r, s, p))

    logs = pl.BlockSpec((1, joined.shape[1], 128), lambda r, p, s, ids: (turn + r, 0, 0))
    mask = pl.BlockSpec((2, rows, length), lambda r, p, s, ids: (2 * p + (ids[1] ^ (turn + r)), 0, 0))
    return block, logs, [mask] * len(mask_parts)


def qkv_attend_kernel(blk, head_dim, steps, seqs, ids, *refs):
    mask_refs, inputs, refs = refs[:blk], refs[blk : 2 * blk + 4], refs[2 * blk + 4 :]
    x_ref, vec_ref, out_ref, o_ref, lse_ref, w_ref, w_far_ref, v_ref, joined_ref, sems = refs
    step = pl.program_id(0)

    @pl.when(step < steps)
    def _():
        qkv_kernel(
            blk, ids, joined_ref, *inputs, x_ref, vec_ref, out_ref, w_ref, w_far_ref, v_ref, sems
        )

    @pl.when(step >= steps)
    def _():
        turn, pair, seq = attend_step(step - steps, out_ref.shape[2] // 384, seqs)
        length = o_ref.shape[1]
        view = joined_ref.at[
            pl.ds(turn, 1),
            pl.ds(pl.multiple_of(seq * length, length), length),
            pl.ds(pl.multiple_of(pair * 384, 128), 384),
        ]
        attend_kernel(head_dim, pair, seq, ids, view, *mask_refs, o_ref, lse_ref)


def attend_step(step, pairs, seqs):
    step = jnp.maximum(step, 0)
    return step // (pairs * seqs), step // seqs % pairs, step % seqs


def qkv_attend(ids, parts, pieces, cols, mask_parts, head_dim, ties=()):
    blk = len(parts)
    seqs, block_rows, width = parts[0].shape
    length = blk * block_rows
    tokens = seqs * length
    block = 2 * block_rows
    steps = tokens // block
    pairs = cols // 384
    piece = pieces[0][0]
    shape = place_shape(piece, cols)
    x_shape = jax.ShapeDtypeStruct((seqs, blk, block_rows, width), bf16)
    v_shape = jax.ShapeDtypeStruct((16, width), f32)

    def at(index):
        def found(i, ids):
            return index(ids, *attend_step(i - steps, pairs, seqs))

        return found

    mask = pl.BlockSpec(
        (2, block_rows, length), at(lambda ids, r, p, s: (2 * p + (ids[1] ^ r), 0, 0))
    )
    return kernel_call(
        partial(qkv_attend_kernel, blk, head_dim, steps, seqs),
        ids,
        [*mask_parts, *parts, *pieces[0], *pieces[1]],
        ties,
        (steps + 2 * pairs * seqs,),
        [mask] * blk + [any_block()] * (blk + 4),
        (
            whole_block(x_shape),
            whole_block(v_shape),
            pl.BlockSpec((2, block, cols), lambda i, ids: (0, jnp.minimum(i, steps - 1), 0)),
            pl.BlockSpec((1, length, 128), at(lambda ids, r, p, s: (r, s, p))),
            pl.BlockSpec((1, tokens, 128), at(lambda ids, r, p, s: (r, 0, 0))),
        ),
        (
            x_shape,
            v_shape,
            jax.ShapeDtypeStruct((2, tokens, cols), bf16),
            jax.ShapeDtypeStruct((2, tokens, cols // 3), bf16),
            jax.ShapeDtypeStruct((2, tokens, 128), f32),
        ),
        [
            shape,
            shape,
            place_shape(piece, 128),
            pltpu.VMEM((2, tokens, cols), bf16),
            pltpu.SemaphoreType.DMA((blk + 6,)),
        ],
    )


def attend_back(
    ids, joined, attended, upstream, logs, mask_parts, turn, seqs, head_dim, ties=()
):
    tokens, cols = joined.shape[1:]
    count = cols // 384
    length = tokens // seqs
    block, log_block, masks = attention_specs(joined, mask_parts, turn)
    return kernel_call(
        partial(attend_back_kernel, head_dim),
        ids,
        [joined, attended, upstream, logs, *mask_parts],
        ties,
        (1, count, seqs),
        [block(384), block(128), block(128), log_block] + masks,
        (
            pl.BlockSpec((1, length, 384), lambda r, p, s, ids: (0, s, p)),
            pl.BlockSpec((1, 1, 8, 384), lambda r, p, s, ids: (r, p, 0, 0)),
        ),
        (
            jax.ShapeDtypeStruct((1, tokens, cols), bf16),
            jax.ShapeDtypeStruct((1, count, 8, 384), f32),
        ),
    )


def out_kernel(ids, att_ref, x_ref, vec_ref, *refs):
    pieces, (first_ref, low_ref, w_ref, sems) = (refs[:2], refs[2:4]), refs[4:]

    @pl.when(pl.program_id(0) == 0)
    def _():
        load = Loader(ids, sems)
        half = w_ref.shape[-1] // 2
        load.columns(pieces, pieces[0][0].shape[-1] - half, half, w_ref)
        load.wait()

    attended = pair_order(ids[1], att_ref[0], att_ref[1], 128)
    first = x_ref[...].astype(f32) + (dot(attended, flat(w_ref)) + vector(vec_ref, "bias_out"))
    first_ref[...] = first
    gain, shift = vector(vec_ref, "gain_first"), vector(vec_ref, "shift_first")
    low_ref[...] = (norm_stats(first)[0] * gain + shift).astype(bf16)


def out_projection(ids, attended, pieces, token_rows, vectors, block, ties=()):
    tokens, width = token_rows.shape
    row = pl.BlockSpec((block, width), lambda i, ids: (i, 0))
    return kernel_call(
        out_kernel,
        ids,
        [attended, token_rows, vectors, *pieces[0], *pieces[1]],
        ties,
        (tokens // block,),
        [
            pl.BlockSpec((2, block, width // 2), lambda i, ids: (0, i, 0)),
            row,
            whole_block(vectors),
        ]
        + [any_block()] * 4,
        (row, row),
        (jax.ShapeDtypeStruct((tokens, width), f32), jax.ShapeDtypeStruct((tokens, width), bf16)),
        [place_shape(pieces[0][0], width), pltpu.SemaphoreType.DMA((4,))],
        cost=brief,
    )


def up_kernel(chunk, steps, ids, h_ref, b_ref, *refs):
    pieces, (act_ref, der_ref, w_ref, w_far_ref, sems) = (refs[:2], refs[2:4]), refs[4:]
    step = pl.program_id(0)
    block = act_ref.shape[1]
    cols = w_ref.shape[-1]

    @pl.when(step == 0)
    def _():
        load = Loader(ids, sems)
        start = pieces[0][0].shape[-1] - cols
        load.rows(pieces[0], start, cols, w_ref)
        load.rows(pieces[1], start, cols, w_far_ref)
        load.wait()

    def run(ref):
        lanes = pl.ds(pl.multiple_of((step % steps) * block, block), block)
        weights = ref[:, :, :, lanes].reshape(-1, block)
        bias = b_ref[0]
        for first in range(0, h_ref.shape[0], chunk):
            place_ = slice(first, first + chunk)
            gate = dot(h_ref[place_, :], weights) + bias
            share = 0.5 + 0.5 * lax.erf(gate * math.sqrt(0.5))
            bell = jnp.exp2((-0.5 * log2e) * (gate * gate)) * (1.0 / math.sqrt(2.0 * math.pi))
            act_ref[place_, :] = (gate * share).astype(bf16)
            der_ref[place_, :] = (share + gate * bell).astype(bf16)

    pl.when(step < steps)(lambda: run(w_ref))
    pl.when(step >= steps)(lambda: run(w_far_ref))


def up_projection(ids, hidden_low, pieces, bias, ties=()):
    tokens, width = hidden_low.shape
    half = bias.shape[2]
    block = width
    steps = half // block
    out = pl.BlockSpec((tokens, block), lambda j, ids: (0, (ids[1] ^ (j // steps)) * steps + j % steps))
    shape = jax.ShapeDtypeStruct((tokens, 2 * half), bf16)
    scratch = place_shape(pieces[0][0], half)
    return kernel_call(
        partial(up_kernel, 128, steps),
        ids,
        [hidden_low, bias, *pieces[0], *pieces[1]],
        ties,
        (2 * steps,),
        [
            whole_block(hidden_low),
            pl.BlockSpec((1, 1, block), lambda j, ids: (ids[1] ^ (j // steps), 0, j % steps)),
        ]
        + [any_block()] * 4,
        (out, out),
        (shape, shape),
        [scratch, scratch, pltpu.SemaphoreType.DMA((4,))],
        cost=brief,
    )


def down_kernel(blk, ids, *refs):
    pos_ref, cot_ref, act_ref, der_ref, first_ref, vec_ref = refs[:6]
    mine, other = refs[6:8], refs[8:10]
    outs, refs = refs[10 : 10 + blk], refs[10 + blk :]
    gss_ref, gdi_ref, gate_ref, sums_ref, up_ref, w_ref, sems = refs
    step = pl.program_id(0)
    here = ids[0]
    seqs, rows, width = first_ref.shape

    @pl.when(step == 0)
    def _():
        load = Loader(ids, sems)
        load.columns((mine, other), 0, width // 2, w_ref)
        load.wait()

    weights = flat(w_ref)
    cols = act_ref.shape[-1]
    normed_one = norm_stats(first_ref[...].reshape(-1, width))[0]
    hidden = normed_one * vector(vec_ref, "gain_first") + vector(vec_ref, "shift_first")
    product = dot(act_ref[...].reshape(-1, cols), weights)
    second = hidden + (product + vector(vec_ref, "bias_down"))
    normed, inverse = norm_stats(second)
    gain = vector(vec_ref, "gain_second")
    result = (normed * gain + vector(vec_ref, "shift_second")).astype(bf16)
    for piece, out in enumerate(outs):

        @pl.when(step == piece)
        def _():
            out[...] = result.reshape(out.shape)

    slots = pos_ref.shape[-1]
    token = lax.broadcasted_iota(jnp.int32, (rows, slots), 0) + (here ^ step) * rows
    upstream = jnp.concatenate(
        [
            dot(jnp.where(token == pos_ref[seq], 1.0, 0.0).astype(bf16), cot_ref[seq])
            for seq in range(seqs)
        ],
        axis=0,
    )
    grad = norm_pull(upstream, normed, inverse, gain)
    gss_ref[...] = grad.reshape(gss_ref.shape)
    low = grad.astype(bf16)
    gdi_ref[...] = low.reshape(gdi_ref.shape)
    add_sums(sums_ref, [low.astype(f32), upstream * normed, upstream])
    grad_gate = dot_right_t(low, weights) * der_ref[...].reshape(-1, cols).astype(f32)
    grad_gate = grad_gate.astype(bf16)
    gate_ref[...] = grad_gate.reshape(gate_ref.shape)
    add_sums(up_ref, [grad_gate.astype(f32)])


def down_projection(
    ids, active, slope, first_sum, pieces, vectors, marks, cot_values, seqs, blk, ties=()
):
    tokens, cols = active.shape
    width = first_sum.shape[1]
    length = tokens // seqs
    rows = length // blk

    def block(size):
        return pl.BlockSpec((seqs, rows, size), lambda d, ids: (0, ids[0] ^ d, 0))

    def shape(size, dtype):
        return jax.ShapeDtypeStruct((seqs, length, size), dtype)

    piece = jax.ShapeDtypeStruct((seqs, rows, width), bf16)
    sums = jax.ShapeDtypeStruct((8, width), f32)
    up_sums = jax.ShapeDtypeStruct((8, cols), f32)
    slots = marks.shape[-1]
    by_seq = [array.reshape(seqs, length, -1) for array in (active, slope, first_sum)]
    outs = kernel_call(
        partial(down_kernel, blk),
        ids,
        [marks, cot_values, *by_seq, vectors, *pieces[0], *pieces[1]],
        ties,
        (blk,),
        [
            whole_block(marks),
            pl.BlockSpec((seqs, slots, width), lambda d, ids: (ids[0], 0, 0)),
            block(cols),
            block(cols),
            block(width),
            whole_block(vectors),
        ]
        + [any_block()] * 4,
        [whole_block(piece)] * blk
        + [block(width), block(width), block(cols), whole_block(sums), whole_block(up_sums)],
        [piece] * blk + [shape(width, f32), shape(width, bf16), shape(cols, bf16), sums, up_sums],
        [place_shape(pieces[0][0], width), pltpu.SemaphoreType.DMA((4,))],
    )
    rest = outs[blk:]
    return outs[:blk], [array.reshape(tokens, -1) for array in rest[:3]], rest[3:]


def first_back_kernel(ids, gate_ref, gss_ref, first_ref, vec_ref, *refs):
    pieces, out_pieces, refs = (refs[:2], refs[2:4]), (refs[4:6], refs[6:8]), refs[8:]
    gfs_ref, branch_ref, att_ref, sums_ref, w_ref, w_out_ref, sems = refs
    width = gss_ref.shape[1]

    @pl.when(pl.program_id(0) == 0)
    def _():
        load = Loader(ids, sems)
        load.columns(pieces, 0, w_ref.shape[-1] // 2, w_ref)
        start = out_pieces[0][0].shape[-1] - width // 2
        load.columns(out_pieces, start, width // 2, w_out_ref)
        load.wait()

    grad_hidden = gss_ref[...] + dot_right_t(gate_ref[...], flat(w_ref))
    normed, inverse = norm_stats(first_ref[...])
    grad = norm_pull(grad_hidden, normed, inverse, vector(vec_ref, "gain_first"))
    gfs_ref[...] = grad
    low = grad.astype(bf16)
    branch_ref[...] = low
    grad_att = dot_right_t(low, flat(w_out_ref)).astype(bf16)
    att_ref[0], att_ref[1] = pair_split(ids[1], grad_att, 128)
    add_sums(sums_ref, [low.astype(f32), grad_hidden * normed, grad_hidden])


def first_back(
    ids, grad_gate, grad_second_sum, first_sum, pieces, out_pieces, vectors, block, ties=()
):
    tokens, cols = grad_gate.shape
    width = first_sum.shape[1]

    def row(size):
        return pl.BlockSpec((block, size), lambda i, ids: (i, 0))

    def shape(size, dtype):
        return jax.ShapeDtypeStruct((tokens, size), dtype)

    sums = jax.ShapeDtypeStruct((8, width), f32)
    piece = pieces[0][0]
    return kernel_call(
        first_back_kernel,
        ids,
        [
            grad_gate,
            grad_second_sum,
            first_sum,
            vectors,
            *pieces[0],
            *pieces[1],
            *out_pieces[0],
            *out_pieces[1],
        ],
        ties,
        (tokens // block,),
        [row(cols), row(width), row(width), whole_block(vectors)] + [any_block()] * 8,
        (
            row(width),
            row(width),
            pl.BlockSpec((2, block, width // 2), lambda i, ids: (0, i, 0)),
            whole_block(sums),
        ),
        (
            shape(width, f32),
            shape(width, bf16),
            jax.ShapeDtypeStruct((2, tokens, width // 2), bf16),
            sums,
        ),
        [place_shape(piece, cols), place_shape(piece, width), pltpu.SemaphoreType.DMA((8,))],
    )


def beside(array, devices, per):
    groups = array.reshape(devices, per, -1, array.shape[-1])
    return jnp.concatenate(
        [groups[:, index].reshape(-1, array.shape[-1]) for index in range(per)], axis=1
    )


def down_grad_kernel(devices, per, ids, act_ref, g_ref, keep_ref, send_ref):
    halves = half_split(ids[1], dot_left_t(act_ref[...], g_ref[...]))
    for half, out in zip(halves, (keep_ref, send_ref)):
        out[...] = (beside(half, devices, per) if per > 1 else half).astype(bf16)


def down_grad(ids, active, grad_down_in, devices, ties=()):
    tokens, cols = active.shape
    width = grad_down_in.shape[1]
    per, block = cols // width, width
    inside = (width // devices) % 8 == 0
    groups = per if inside else 1
    out = pl.BlockSpec((block // groups, groups * width // 2), lambda i, ids: (i, 0))
    shape = jax.ShapeDtypeStruct((cols // groups, groups * width // 2), bf16)
    halves = kernel_call(
        partial(down_grad_kernel, devices // per, groups),
        ids,
        [active, grad_down_in],
        ties,
        (cols // block,),
        [pl.BlockSpec((tokens, block), lambda i, ids: (0, i)), whole_block(grad_down_in)],
        (out, out),
        (shape, shape),
    )
    return halves if inside else [beside(half, devices, per) for half in halves]


def up_grad_kernel(ids, h_ref, g_ref, g_far_ref, keep_ref, send_ref):
    keep_ref[...] = dot_left_t(h_ref[...], g_ref[...]).astype(bf16)
    send_ref[...] = dot_left_t(h_ref[...], g_far_ref[...]).astype(bf16)


def up_grad(ids, hidden_low, grad_gate, block, ties=()):
    tokens, width = hidden_low.shape
    cols = grad_gate.shape[1] // 2
    steps = cols // block
    shape = jax.ShapeDtypeStruct((width, cols), bf16)
    out = pl.BlockSpec((width, block), lambda j, ids: (0, j))
    return kernel_call(
        up_grad_kernel,
        ids,
        [hidden_low, grad_gate, grad_gate],
        ties,
        (steps,),
        [
            whole_block(hidden_low),
            pl.BlockSpec((tokens, block), lambda j, ids: (0, ids[1] * steps + j)),
            pl.BlockSpec((tokens, block), lambda j, ids: (0, (1 - ids[1]) * steps + j)),
        ],
        (out, out),
        (shape, shape),
    )


def left_grad_kernel(
    ids,
    x_ref,
    g_ref,
    g_far_ref,
    att_ref,
    branch_ref,
    sums_ref,
    sums_far_ref,
    first_ref,
    second_ref,
    up_ref,
    *outs,
):
    core, step = ids[1], pl.program_id(0)
    attended = pair_order(core, att_ref[0], att_ref[1], 128)
    out_grads = half_split(core, dot_left_t(attended, branch_ref[...]))
    sums = [ref[0, step][:1] for ref in (sums_ref, sums_far_ref)]
    rows = [
        pair_order(core, sums[0][:, at : at + 128], sums[1][:, at : at + 128], 128)
        for at in (0, 256)
    ]
    rows += [first_ref[:3], second_ref[:3], up_ref[...]]
    used = sum(row.shape[0] for row in rows)
    rows = jnp.concatenate(rows + [jnp.zeros((16 - used, rows[0].shape[1]), f32)], axis=0)
    lanes = lax.broadcasted_iota(jnp.int32, (16, 128), 1)
    eye = lanes == lax.broadcasted_iota(jnp.int32, lanes.shape, 0)
    columns = dot_left_t(rows.astype(bf16), jnp.where(eye, 1.0, 0.0).astype(bf16))
    cut = outs[0].shape[1] - 128
    for turn, ref in enumerate((g_ref, g_far_ref)):
        grad = dot_left_t(x_ref[...], ref[0])
        first = jnp.concatenate([grad[:, :cut], columns], axis=1)
        second = jnp.concatenate([grad[:, cut:], out_grads[turn]], axis=1)
        outs[turn][...] = first.astype(bf16)
        outs[2 + turn][...] = second.astype(bf16)


def left_grad(ids, left, grads, attended, grad_branch, sums, totals, ties=()):
    tokens, width = left.shape
    cut = grads[0].shape[2] - 384
    sizes = [cut + 128] * 2 + [384 + width // 2] * 2
    return kernel_call(
        left_grad_kernel,
        ids,
        [left, *grads, attended, grad_branch, *sums, *totals],
        ties,
        (width // 256,),
        [
            pl.BlockSpec((tokens, 256), lambda i, ids: (0, i)),
            *[whole_block(grad) for grad in grads],
            pl.BlockSpec((2, tokens, 128), lambda i, ids: (0, 0, i)),
            whole_block(grad_branch),
            *[whole_block(array) for array in sums],
        ]
        + [pl.BlockSpec((array.shape[0], 256), lambda i, ids: (0, i)) for array in totals],
        [pl.BlockSpec((256, size), lambda i, ids: (i, 0)) for size in sizes],
        [jax.ShapeDtypeStruct((width, size), bf16) for size in sizes],
    )


def input_grad_kernel(blk, ids, g_ref, g_far_ref, gfs_ref, *refs):
    pieces, refs = (refs[:2], refs[2:4]), refs[4:]
    outs, (w_ref, w_far_ref, sems) = refs[:blk], refs[blk:]
    step = pl.program_id(0)

    @pl.when(step == 0)
    def _():
        load = Loader(ids, sems)
        load.rows(pieces[0], 0, w_ref.shape[-1], w_ref)
        load.rows(pieces[1], 0, w_ref.shape[-1], w_far_ref)
        load.wait()

    width = gfs_ref.shape[-1]
    total = gfs_ref[...].reshape(-1, width)
    for ref, weights in ((g_ref, w_ref), (g_far_ref, w_far_ref)):
        total = total + dot_right_t(ref[...].reshape(-1, ref.shape[-1]), flat(weights))
    for piece, out in enumerate(outs):

        @pl.when(step == piece)
        def _():
            out[...] = total.astype(bf16).reshape(out.shape)


def input_grad(ids, grads, grad_first_sum, pieces, seqs, blk, ties=()):
    tokens, width = grad_first_sum.shape
    length = tokens // seqs
    rows = length // blk
    cols = grads[0].shape[2]
    piece = jax.ShapeDtypeStruct((seqs, rows, width), bf16)
    shape = place_shape(pieces[0][0], cols)
    pieces = [*pieces[0], *pieces[1]]
    return kernel_call(
        partial(input_grad_kernel, blk),
        ids,
        [
            *[grad.reshape(seqs, length, cols) for grad in grads],
            grad_first_sum.reshape(seqs, length, width),
            *pieces,
        ],
        ties,
        (blk,),
        [
            *[pl.BlockSpec((seqs, rows, cols), lambda d, ids: (0, ids[0] ^ d, 0))] * 2,
            pl.BlockSpec((seqs, rows, width), lambda d, ids: (0, ids[0] ^ d, 0)),
        ]
        + [any_block()] * len(pieces),
        [whole_block(piece)] * blk,
        [piece] * blk,
        [shape, shape, pltpu.SemaphoreType.DMA((len(pieces),))],
    )


class Grid:
    def __init__(self, mesh):
        batch, blk = mesh.shape["batch"], mesh.shape["blk"]
        self.sizes = {"z": batch // 2, "y": 2, "x": blk // 2, "c": 2}
        self.strides = {"c": 1, "x": 2, "y": blk, "z": 2 * blk}
        self.total = batch * blk
        self.blk = blk

    def digit(self, name):
        index = lax.axis_index("batch") * self.blk + lax.axis_index("blk")
        return (index // self.strides[name]) % self.sizes[name]

    def swap(self, array, name, delta=1):
        size, stride = self.sizes[name], self.strides[name]
        pairs = []
        for index in range(self.total):
            here = (index // stride) % size
            pairs.append((index, index + ((here ^ delta) - here) * stride))
        return lax.ppermute(array, both, pairs)

    def swap_blk(self, array, delta):
        pairs = [(index, index ^ delta) for index in range(self.total)]
        return lax.ppermute(array, both, pairs)


def place(parts, index):
    if len(parts) == 1:
        return parts[0][None]
    rows = []
    for target in range(len(parts)):
        row = parts[0]
        for delta in range(1, len(parts)):
            row = jnp.where(index == target ^ delta, parts[delta], row)
        rows.append(row)
    return jnp.stack(rows)


def pick(array, index):
    return lax.dynamic_index_in_dim(array, index, axis=0, keepdims=False)


def gather_core(grid, mine, other):
    cols = mine.shape[1]
    return place([mine, grid.swap(other, "c")], grid.digit("c")).reshape(-1, cols)


def gather_step(grid, run, held, name, *ties):
    parts = [grid.swap(held, name, d) for d in range(1, grid.sizes[name])]
    return place_parts(run, [held, *parts], name, ties)


def gather_last(grid, held, name):
    far = grid.swap(held, name)
    if held.shape[1] % 16 == 0:
        return [held, far]
    where = grid.digit(name)
    whole = jnp.moveaxis(place([held, far], where), 0, 1).reshape(4, 2, -1, held.shape[2])
    return [lax.dynamic_index_in_dim(whole, where ^ d, 1, keepdims=False) for d in range(2)]


def gather_pieces(grid, run, held, *ties):
    near, far = held
    if ties:
        (far,) = after(run, [far], *ties)
    return [[near, far], [grid.swap(near, "c"), grid.swap(far, "c")]]


def add_low(*parts):
    total = parts[0].astype(f32)
    for part in parts[1:]:
        total = total + part.astype(f32)
    return total


def fold_kernel(count, groups, ids, *refs):
    outs = refs[len(refs) - count :]
    refs = list(refs[: len(refs) - count])
    for out in outs:
        sums = []
        for terms in groups:
            picked, refs = refs[:terms], refs[terms:]
            total = picked[0][...].astype(f32)
            for ref in picked[1:]:
                total = total + ref[...].astype(f32)
            sums.append(total.astype(out.dtype))
        out[...] = jnp.concatenate(sums, axis=-1).reshape(out.shape)


def fold(ids, which, groups, ties):
    outer, count, rows, unused = groups[0][0].shape
    steps = 2 if outer % 2 == 0 else 1
    part = outer // steps

    def term_block(cols, delta):
        return pl.BlockSpec((part, 1, rows, cols), lambda i, ids: (i, ids[which] ^ delta, 0, 0))

    terms = [term for group in groups for term in group]
    cols = sum(group[0].shape[3] for group in groups)
    shape = jax.ShapeDtypeStruct((outer, rows, cols), bf16)
    return kernel_call(
        partial(fold_kernel, count, [len(group) for group in groups]),
        ids,
        [term for delta in range(count) for term in terms],
        ties,
        (steps,),
        [term_block(term.shape[3], delta) for delta in range(count) for term in terms],
        [pl.BlockSpec((part, rows, cols), lambda i, ids: (i, 0, 0))] * count,
        [shape] * count,
    )


class Scatter:
    def __init__(self, grid, ids, pairs, order):
        self.grid, self.ids, self.order = grid, ids, list(order)
        sizes = grid.sizes
        self.left = [("z", sizes["z"]), ("y", sizes["y"]), ("x", sizes["x"])]
        self.last = 2 * (pairs[0][0].shape[0] // grid.total)
        self.groups = [[keep, grid.swap(send, "c")] for keep, send in pairs]

    def join(self, other):
        self.groups = self.groups + other.groups
        return self

    def shaped(self, *shape):
        return [[term.reshape(*shape, term.shape[-1]) for term in group] for group in self.groups]

    def step(self, ties=()):
        name = self.order.pop(0)
        index = [left for left, unused in self.left].index(name)
        count = self.left[index][1]
        outer = math.prod(size for unused, size in self.left[:index])
        inner = math.prod(size for unused, size in self.left[index + 1 :]) * self.last
        sums = fold(self.ids, id_of[name], self.shaped(outer, count, inner), ties)
        self.left.pop(index)
        sent = [self.grid.swap(sums[delta], name, delta) for delta in range(1, count)]
        self.groups = [[sums[0], *sent]]

    def end(self, ties=()):
        mine, other = fold(self.ids, id_of["c"], self.shaped(1, 2, self.last // 2), ties)
        mine, other = [array.reshape(array.shape[1:]) for array in (mine, other)]
        return mine.astype(f32), self.grid.swap(other, "c").astype(f32)


def in_order(core, mine, other):
    return jnp.where(core == 0, mine, other), jnp.where(core == 0, other, mine)


def local(
    grid,
    inputs,
    w_qkv,
    bias_query,
    bias_value,
    w_out,
    bias_out,
    gain_first,
    shift_first,
    w_up,
    bias_up,
    w_down,
    bias_down,
    gain_second,
    shift_second,
    dam_mask,
    positions,
    counts,
    cot_values,
):
    groups, block_rows, width = inputs.shape
    head_count = dam_mask.shape[0]
    head_dim = width // head_count
    blk = grid.blk
    seqs = groups // blk
    length = blk * block_rows
    tokens = seqs * length
    here, core = lax.axis_index("blk"), grid.digit("c")
    ids = Run(jnp.stack([here, core] + [grid.digit(name) for name in "yzx"]).astype(jnp.int32))
    rows = w_qkv.shape[0]
    up_per = bias_up.shape[0] // rows
    half = width // 2
    pairs = width // 256

    vectors = (
        bias_query,
        bias_value,
        bias_out,
        gain_first,
        shift_first,
        bias_down,
        gain_second,
        shift_second,
    )
    stacked = jnp.concatenate(
        [
            jnp.stack(vectors),
            bias_up.reshape(rows, up_per).T,
            jnp.zeros((16 - len(vectors) - up_per, rows), bf16),
        ]
    )
    halves = split_weights(ids, w_qkv, stacked, w_out, w_up, w_down)
    first_near, second_near, down_near = [gather_core(grid, *pair) for pair in halves]

    def over_x(held):
        return gather_step(grid, ids, held, "x").reshape(-1, held.shape[1])

    first_near = over_x(first_near)
    event = ids.token

    by_home = inputs.reshape(blk, seqs, block_rows, width)
    parts = [pick(by_home, here ^ delta) for delta in range(blk)]
    parts[2:] = after(ids, parts[2:], event)
    parts[1:] = [grid.swap_blk(parts[delta], delta) for delta in range(1, blk)]
    addend = mask_addend(ids, dam_mask, [event])
    mask_parts = [addend, grid.swap(addend, "c")]
    second_near, down_near = after(ids, [second_near, down_near], event)
    second_near = over_x(second_near)
    ties = [ids.token]
    down_near = over_x(down_near)
    ties.append(ids.token)

    first_z = gather_step(grid, ids, first_near, "z", *ties, *parts[2:])
    (second_near,) = after(ids, [second_near], ids.token)
    first_y = gather_last(grid, first_z, "y")
    first_pieces = gather_pieces(grid, ids, first_y)
    ties = []
    if grid.sizes["x"] > 1:
        far = grid.swap(addend, "x")
        mask_parts += [far, grid.swap(far, "c")]
        ties = [far]
    second_z = gather_step(grid, ids, second_near, "z", *ties)
    (down_near,) = after(ids, [down_near], ids.token)
    second_y = gather_last(grid, second_z, "y")
    token_rows, vector_rows, joined, attended, logs = qkv_attend(
        ids, parts, first_pieces, 3 * half, mask_parts, head_dim, ties=[ids.token]
    )
    token_rows = token_rows.reshape(tokens, width)
    first_row = len(vectors)
    up_bias = vector_rows[first_row : first_row + up_per].T.reshape(2, 1, -1)
    down_z = gather_step(grid, ids, down_near, "z", ids.token)
    down_y = gather_last(grid, down_z, "y")
    second_pieces = gather_pieces(grid, ids, second_y, ids.token)
    first_sum, hidden_low = out_projection(
        ids, attended, first_pieces, token_rows, vector_rows, 2 * block_rows
    )
    active, slope = up_projection(ids, hidden_low, second_pieces, up_bias)
    down_pieces = gather_pieces(grid, ids, down_y, ids.token)

    my_positions = pick(positions.reshape(blk, seqs, -1), here)
    my_counts = pick(counts.reshape(blk, seqs), here)
    live = jnp.arange(positions.shape[1], dtype=jnp.int32)[None, :] < my_counts[:, None]
    marks = jnp.where(live, my_positions, -1)[:, None, :]
    result, (grad_second_sum, grad_down_in, grad_gate), (second_sums, up_sums) = down_projection(
        ids, active, slope, first_sum, down_pieces, vector_rows, marks, cot_values, seqs, blk
    )

    def home(pieces):
        return [pieces[0]] + [grid.swap_blk(pieces[delta], delta) for delta in range(1, blk)]

    result = home(result)
    down_halves = down_grad(ids, active, grad_down_in, grid.total)
    up_halves = up_grad(ids, hidden_low, grad_gate, width, ties=[ids.token])
    up_sum = Scatter(grid, ids, [up_halves], "yxz")
    ffn_sum = Scatter(grid, ids, [down_halves], "xyz")
    ffn_sum.step([ids.token])
    up_sum.step([ids.token])
    grad_first_sum, grad_branch, grad_attended, first_sums = first_back(
        ids,
        grad_gate,
        grad_second_sum,
        first_sum,
        second_pieces,
        first_pieces,
        vector_rows,
        2 * block_rows,
        ties=[ids.token],
    )
    result = after(ids, result, ids.token)
    def back(turn):
        return attend_back(
            ids,
            joined,
            attended,
            grad_attended,
            logs,
            mask_parts,
            turn,
            seqs,
            head_dim,
            ties=[ids.token],
        )

    far_grads, far_sums = back(1)
    ffn_sum.step([ids.token])
    up_sum.step([ids.token])
    near_grads, near_sums = back(0)
    grads, grad_sums = (near_grads, far_grads), (near_sums, far_sums)
    ffn_sum = up_sum.join(ffn_sum)
    ffn_sum.step([ids.token])
    up_rows = up_sums[0].reshape(width, up_per).T
    totals = [first_sums, second_sums, up_rows]
    halves = left_grad(
        ids, token_rows, grads, attended, grad_branch, grad_sums, totals, ties=[ids.token]
    )
    one_sum = Scatter(grid, ids, [halves[:2]], "xyz")
    two_sum = Scatter(grid, ids, [halves[2:]], "yxz")
    one_sum.step([ids.token])
    two_sum.step([ids.token])
    sent = input_grad(ids, grads, grad_first_sum, first_pieces, seqs, blk, ties=[ids.token])
    one_sum.step([ids.token])
    two_sum.step([ids.token])
    grad_inputs = home(sent)
    activations = place_parts(ids, result, "here", [ids.token])
    activations = activations.reshape(groups, block_rows, width)
    att_sum = one_sum.join(two_sum)
    att_sum.step([ids.token])
    share_ffn = ffn_sum.end([ids.token])
    share_att = att_sum.end([ids.token])
    grad_inputs = widen_parts(ids, grad_inputs, "here", [ids.token])
    grad_inputs = grad_inputs.reshape(groups, block_rows, width)

    cut = near_grads.shape[2] - 384
    share_qkv = [
        jnp.concatenate([share[:, :cut], share[:, cut + 128 : cut + 512]], axis=1)
        for share in share_att
    ]
    by_core = jnp.stack(in_order(core, *share_qkv), axis=0).reshape(2, rows, pairs, 3, 128)
    share_qkv = by_core.transpose(1, 3, 2, 0, 4).reshape(rows, 3 * width)
    share_out = jnp.concatenate(in_order(core, *[share[:, cut + 512 :] for share in share_att]), axis=1)
    up_cols = up_halves[0].shape[1]
    share_up = [share[:, :up_cols] for share in share_ffn]
    share_down = [
        share[:, up_cols:].reshape(rows, up_per, half).transpose(1, 0, 2).reshape(-1, half)
        for share in share_ffn
    ]
    shares = share_att[0][:, cut : cut + 128]
    share_vectors = [shares[:, index] for index in range(len(vectors))]
    share_bias_up = shares[:, len(vectors) : len(vectors) + up_per].reshape(-1)
    (
        share_bias_query,
        share_bias_value,
        share_bias_out,
        share_gain_first,
        share_shift_first,
        share_bias_down,
        share_gain_second,
        share_shift_second,
    ) = share_vectors
    return (
        activations,
        grad_inputs,
        share_qkv,
        share_bias_query,
        share_bias_value,
        share_out,
        share_bias_out,
        share_gain_first,
        share_shift_first,
        jnp.concatenate(in_order(core, *share_up), axis=1),
        share_bias_up,
        jnp.concatenate(in_order(core, *share_down), axis=1),
        share_bias_down,
        share_gain_second,
        share_shift_second,
    )


def solution(mesh):
    sharded = P(both)
    rows = P(both, None)
    whole = P("batch", "blk", None)
    return jax.shard_map(
        partial(local, Grid(mesh)),
        mesh=mesh,
        in_specs=(
            whole,
            rows,
            sharded,
            sharded,
            rows,
            sharded,
            sharded,
            sharded,
            rows,
            sharded,
            rows,
            sharded,
            sharded,
            sharded,
            P(None, "blk", None),
            P("batch", None),
            P("batch"),
            P("batch", None, None),
        ),
        out_specs=(
            whole,
            whole,
            rows,
            sharded,
            sharded,
            rows,
            sharded,
            sharded,
            sharded,
            rows,
            sharded,
            rows,
            sharded,
            sharded,
            sharded,
        ),
        check_vma=False,
    )
```

```python
import math
from functools import partial

import jax
import jax.numpy as jnp
from jax import lax
from jax.experimental import pallas as pl
from jax.experimental.pallas import tpu as pltpu
from jax.sharding import PartitionSpec as P

norm_eps = 1e-06
masked_score = -1e30
f32 = jnp.float32
bf16 = jnp.bfloat16
both = ("batch", "blk")
log2e = math.log2(math.e)
long, brief, least = 10**11, 100000000000, 100000000000
roomy = pltpu.CompilerParams(vmem_limit_bytes=48 << 20)
vector_names = (
    "bias_query",
    "bias_value",
    "bias_out",
    "gain_first",
    "shift_first",
    "bias_down",
    "gain_second",
    "shift_second",
)
row_of = {name: index for index, name in enumerate(vector_names)}


def dot(left, right):
    return jnp.dot(left, right, preferred_element_type=f32)


def dot_right_t(left, right):
    return lax.dot_general(left, right, (((1,), (1,)), ((), ())), preferred_element_type=f32)


def dot_left_t(left, right):
    return lax.dot_general(left, right, (((0,), (0,)), ((), ())), preferred_element_type=f32)


def norm_stats(rows):
    center = jnp.mean(rows, axis=-1, keepdims=True)
    centered = rows - center
    inverse = lax.rsqrt(jnp.mean(centered * centered, axis=-1, keepdims=True) + norm_eps)
    return centered * inverse, inverse


def norm_pull(upstream, normed, inverse, gain):
    scaled = upstream * gain
    inner = jnp.mean(scaled, axis=-1, keepdims=True)
    projected = jnp.mean(scaled * normed, axis=-1, keepdims=True)
    return inverse * (scaled - inner - normed * projected)


def vector(ref, name):
    index = row_of[name]
    return ref[index : index + 1, :]


def piece_rows(here, piece, rows):
    return pl.ds(pl.multiple_of((here ^ piece) * rows, rows), rows)


def stack_pieces(ref, places, cols):
    return jnp.concatenate([ref[0, place_, cols] for place_ in places], axis=0)


def any_block():
    return pl.BlockSpec(memory_space=pl.ANY)


def whole_block(array):
    return pl.BlockSpec(array.shape, lambda *unused: (0,) * len(array.shape))


def pair_order(core, first, second, wide):
    blocks = []
    for start in range(0, first.shape[-1], wide):
        left, right = first[:, start : start + wide], second[:, start : start + wide]
        blocks += [jnp.where(core == 0, left, right), jnp.where(core == 0, right, left)]
    return jnp.concatenate(blocks, axis=1)


def pair_split(core, array, wide):
    outs = []
    for turn in range(2):
        outs.append(
            jnp.concatenate(
                [
                    jnp.where(
                        core == turn,
                        array[:, start : start + wide],
                        array[:, start + wide : start + 2 * wide],
                    )
                    for start in range(0, array.shape[1], 2 * wide)
                ],
                axis=1,
            )
        )
    return outs


def half_split(core, array):
    half = array.shape[1] // 2
    left, right = array[:, :half], array[:, half:]
    return jnp.where(core == 0, left, right), jnp.where(core == 0, right, left)


class Run:
    def __init__(self, ids):
        self.ids, self.token = ids, None


id_of = {"here": 0, "c": 1, "y": 2, "z": 3, "x": 4}
token_shape = jax.ShapeDtypeStruct((8, 128), f32)


def after(run, arrays, *ties):
    shapes = [jax.ShapeDtypeStruct(array.shape, array.dtype) for array in arrays]

    def body(*refs):
        refs[-1][...] = jnp.zeros(token_shape.shape, f32)

    *arrays, run.token = pl.pallas_call(
        body,
        out_shape=shapes + [token_shape],
        in_specs=[any_block()] * (len(arrays) + len(ties)),
        out_specs=[any_block()] * len(arrays) + [pl.BlockSpec(memory_space=pltpu.VMEM)],
        input_output_aliases={index: index for index in range(len(arrays))},
    )(*arrays, *ties)
    return arrays


def kernel_call(
    kernel, run, arrays, ties, grid, in_specs, out_specs, out_shape, scratch=(), cost=long
):
    several = isinstance(out_shape, (list, tuple))
    out_specs, out_shape = [
        list(value) if several else [value] for value in (out_specs, out_shape)
    ]
    count, outs = 1 + len(arrays), len(out_shape)

    def body(*refs):
        inputs, refs = refs[:count], refs[count + len(ties) :]
        refs[outs][...] = jnp.zeros(token_shape.shape, f32)
        kernel(*inputs, *refs[:outs], *refs[outs + 1 :])

    *results, run.token = pl.pallas_call(
        body,
        out_shape=out_shape + [token_shape],
        grid_spec=pltpu.PrefetchScalarGridSpec(
            num_scalar_prefetch=1,
            grid=grid,
            in_specs=list(in_specs) + [any_block()] * len(ties),
            out_specs=out_specs + [whole_block(token_shape)],
            scratch_shapes=scratch,
        ),
        compiler_params=roomy,
        cost_estimate=pl.CostEstimate(flops=cost, bytes_accessed=1024, transcendentals=0),
    )(run.ids, *arrays, *ties)
    return results if several else results[0]


def place_kernel(digit, count, ids, *refs):
    parts, (out, sems) = refs[:count], refs[count:]
    copies = [
        pltpu.make_async_copy(part, out.at[ids[digit] ^ delta], sems.at[delta])
        for delta, part in enumerate(parts)
    ]
    for copy in copies:
        copy.start()
    for copy in copies:
        copy.wait()


def place_parts(run, parts, digit, ties=()):
    count = len(parts)
    return kernel_call(
        partial(place_kernel, id_of[digit], count),
        run,
        parts,
        ties,
        (1,),
        [whole_block(part) for part in parts],
        any_block(),
        jax.ShapeDtypeStruct((count, *parts[0].shape), parts[0].dtype),
        [pltpu.SemaphoreType.DMA((count,))],
        cost=least,
    )


def widen_kernel(digit, count, ids, *refs):
    for delta in range(count):
        refs[count][ids[digit] ^ delta] = refs[delta][...].astype(f32)


def widen_parts(run, parts, digit, ties=()):
    count = len(parts)
    shape = jax.ShapeDtypeStruct((count, *parts[0].shape), f32)
    return kernel_call(
        partial(widen_kernel, id_of[digit], count),
        run,
        parts,
        ties,
        (1,),
        [whole_block(part) for part in parts],
        whole_block(shape),
        shape,
    )


def addend_kernel(ids, mask_ref, out_ref):
    out_ref[...] = jnp.where(mask_ref[...] > 0, 0.0, masked_score).astype(bf16)


def mask_addend(run, mask, ties):
    heads, rows, cols = mask.shape
    block = pl.BlockSpec((heads // 4, rows, cols), lambda i, ids: (i, 0, 0))
    shape = jax.ShapeDtypeStruct(mask.shape, bf16)
    return kernel_call(addend_kernel, run, [mask], ties, (4,), [block], block, shape)


class Loader:
    def __init__(self, ids, sems, digit="y"):
        self.core, self.digit = ids[id_of["c"]], ids[id_of[digit]]
        self.sems, self.copies = sems, []

    def put(self, source, target):
        copy = pltpu.make_async_copy(source, target, self.sems.at[len(self.copies)])
        copy.start()
        self.copies.append(copy)

    def rows(self, pieces, start, size, target):
        for turn, piece in enumerate(pieces):
            self.put(piece.at[:, :, pl.ds(start, size)], target.at[:, self.digit ^ turn])

    def columns(self, both_cores, start, size, target):
        for other, pieces in enumerate(both_cores):
            lanes = pl.ds(pl.multiple_of((self.core ^ other) * size, 128), size)
            for turn, piece in enumerate(pieces):
                self.put(
                    piece.at[:, :, pl.ds(start, size)], target.at[:, self.digit ^ turn, :, lanes]
                )

    def wait(self):
        for copy in self.copies:
            copy.wait()


def flat(ref, first=None, count=None):
    value = ref[...] if first is None else ref[pl.ds(first, count)]
    return value.reshape(-1, value.shape[-1])


def place_shape(piece, cols):
    return pltpu.VMEM((piece.shape[0], 2, piece.shape[1], cols), bf16)


def split_kernel(ids, qkv_ref, vec_ref, out_ref, up_ref, down_ref, *outs):
    core = ids[1]
    width = down_ref.shape[1]
    lanes = lax.broadcasted_iota(jnp.int32, (vec_ref.shape[0], 128), 1)
    eye = lanes == lax.broadcasted_iota(jnp.int32, lanes.shape, 0)
    columns = dot_left_t(vec_ref[...], jnp.where(eye, 1.0, 0.0).astype(bf16)).astype(bf16)
    for turn in range(2):
        first, second, down = outs[3 * turn : 3 * turn + 3]
        pairs = []
        for start in range(0, width, 256):
            for part in range(3):
                left = qkv_ref[:, part * width + start : part * width + start + 128]
                right = qkv_ref[:, part * width + start + 128 : part * width + start + 256]
                pairs.append(jnp.where(core == turn, left, right))
        out_half, second[...] = [half_split(core, ref[...])[turn] for ref in (out_ref, up_ref)]
        first[...] = jnp.concatenate(pairs + [columns, out_half], axis=1)
        down[...] = half_split(core, down_ref[...])[turn]


def split_weights(ids, w_qkv, vectors, w_out, w_up, w_down, ties=()):
    rows, cols = w_qkv.shape
    arrays = [w_qkv, vectors, w_out, w_up, w_down]
    shapes = [
        jax.ShapeDtypeStruct((rows, cols // 2 + 128 + w_out.shape[1] // 2), bf16),
        jax.ShapeDtypeStruct((rows, w_up.shape[1] // 2), bf16),
        jax.ShapeDtypeStruct((w_down.shape[0], w_down.shape[1] // 2), bf16),
    ] * 2
    outs = kernel_call(
        split_kernel,
        ids,
        arrays,
        ties,
        (1,),
        [whole_block(array) for array in arrays],
        [whole_block(shape) for shape in shapes],
        shapes,
        cost=least,
    )
    return list(zip(outs[:3], outs[3:]))


def qkv_kernel(blk, ids, joined_ref, *refs):
    parts, refs = refs[:blk], refs[blk:]
    pieces, refs = (refs[:2], refs[2:4]), refs[4:]
    x_ref, vec_ref, out_ref, w_ref, w_far_ref, v_ref, sems = refs
    here, core = ids[0], ids[1]
    step = pl.program_id(0)
    cols = out_ref.shape[2]
    block = out_ref.shape[1]

    @pl.when(step == 0)
    def _():
        load = Loader(ids, sems)
        for piece, part in enumerate(parts):
            load.put(part, x_ref.at[:, here ^ piece])
        load.rows(pieces[0], 0, cols, w_ref)
        load.rows(pieces[1], 0, cols, w_far_ref)
        load.rows(pieces[0], cols, 128, v_ref)
        load.wait()
        vec_ref[...] = flat(v_ref).astype(f32).T[: vec_ref.shape[0]]

    per_seq = x_ref.shape[1] // 2
    rows = x_ref[step // per_seq, pl.ds(2 * (step % per_seq), 2)].reshape(-1, x_ref.shape[-1])
    for turn, weights in enumerate((w_ref, w_far_ref)):
        bias = []
        for start in range(0, vec_ref.shape[1], 256):
            for name in ("bias_query", None, "bias_value"):
                if name is None:
                    bias.append(jnp.zeros((1, 128), f32))
                    continue
                row = vector(vec_ref, name)
                bias.append(
                    jnp.where(
                        core == turn, row[:, start : start + 128], row[:, start + 128 : start + 256]
                    )
                )
        total = dot(rows, flat(weights)) + jnp.concatenate(bias, axis=1)
        low = total.astype(bf16)
        out_ref[turn] = low
        joined_ref[turn, pl.ds(pl.multiple_of(step * block, block), block), :] = low


def attend_kernel(head_dim, pair, seq, ids, qkv_ref, *rest):
    pieces, (o_ref, lse_ref) = rest[:-2], rest[-2:]
    here = ids[0]
    length, wide = o_ref.shape[1:]
    per = wide // head_dim
    rows = pieces[0].shape[1]
    lanes = lax.broadcasted_iota(jnp.int32, (1, wide), 1)
    log_lanes = lax.broadcasted_iota(jnp.int32, (1, lse_ref.shape[2]), 1)
    keys, values = qkv_ref[0, :, wide : 2 * wide], qkv_ref[0, :, 2 * wide :]
    for first in range(0, len(pieces), 4):
        span = range(first, min(first + 4, len(pieces)))
        places = [piece_rows(here, piece, rows) for piece in span]
        queries = stack_pieces(qkv_ref, places, slice(0, wide))
        out, logs = None, []
        for head in range(per):
            mine = lanes // head_dim == head
            scores = dot_right_t(jnp.where(mine, queries, 0), keys) * (head_dim**-0.5 * log2e)
            addend = jnp.concatenate([pieces[piece][head] for piece in span], axis=0)
            scores = scores + addend.astype(f32)
            top = jnp.max(scores, axis=1, keepdims=True)
            weights = jnp.exp2(scores - top)
            total = jnp.sum(weights, axis=1, keepdims=True)
            part = dot(weights.astype(bf16), values) * (1.0 / total)
            out = part if out is None else jnp.where(mine, part, out)
            logs.append(top + jnp.log2(total))
        for index, place_ in enumerate(places):
            here_rows = slice(index * rows, (index + 1) * rows)
            o_ref[0, place_, :] = out[here_rows].astype(bf16)
            start = seq * length + (here ^ span[index]) * rows
            log_place = pl.ds(pl.multiple_of(start, rows), rows)
            kept = lse_ref[0, log_place, :]
            for head in range(per):
                kept = jnp.where(log_lanes == pair * per + head, logs[head][here_rows], kept)
            lse_ref[0, log_place, :] = kept


def attend_back_kernel(head_dim, ids, qkv_ref, o_ref, g_ref, lse_ref, *rest):
    pieces, (out_ref, sums_ref) = rest[:-2], rest[-2:]
    here = ids[0]
    pair, seq = pl.program_id(1), pl.program_id(2)
    length, wide = o_ref.shape[1:]
    per = wide // head_dim
    rows = pieces[0].shape[1]
    lanes = lax.broadcasted_iota(jnp.int32, (1, wide), 1)
    log_lanes = lax.broadcasted_iota(jnp.int32, (1, lse_ref.shape[2]), 1)
    keys, values = qkv_ref[0, :, wide : 2 * wide], qkv_ref[0, :, 2 * wide :]
    everything = slice(None)
    back = head_dim**-0.5
    dk = jnp.zeros(keys.shape, f32)
    dv = jnp.zeros(keys.shape, f32)
    for first in range(0, len(pieces), 4):
        span = range(first, min(first + 4, len(pieces)))
        places = [piece_rows(here, piece, rows) for piece in span]
        queries = stack_pieces(qkv_ref, places, slice(0, wide))
        ups = stack_pieces(g_ref, places, everything)
        products = ups.astype(f32) * stack_pieces(o_ref, places, everything).astype(f32)
        starts = [seq * length + (here ^ piece) * rows for piece in span]
        log_places = [pl.ds(pl.multiple_of(at, rows), rows) for at in starts]
        logs = stack_pieces(lse_ref, log_places, everything)
        dq = None
        for head in range(per):
            mine = lanes // head_dim == head
            q_mine, g_mine = jnp.where(mine, queries, 0), jnp.where(mine, ups, 0)
            inner = jnp.sum(jnp.where(mine, products, 0.0), axis=1, keepdims=True)
            log = jnp.sum(
                jnp.where(log_lanes == pair * per + head, logs, 0.0), axis=1, keepdims=True
            )
            scores = dot_right_t(q_mine, keys) * (back * log2e)
            addend = jnp.concatenate([pieces[piece][head] for piece in span], axis=0)
            exact = jnp.exp2(scores + addend.astype(f32) - log)
            grads = (exact * (dot_right_t(g_mine, values) - inner)).astype(bf16)
            dv = dv + dot_left_t(exact.astype(bf16), g_mine)
            dk = dk + dot_left_t(grads, q_mine)
            part = dot(grads, keys)
            dq = part if dq is None else jnp.where(mine, part, dq)
        for index, place_ in enumerate(places):
            out_ref[0, place_, :wide] = (dq[index * rows : (index + 1) * rows] * back).astype(bf16)
    out_ref[0, :, wide : 2 * wide] = (dk * back).astype(bf16)
    out_ref[0, :, 2 * wide :] = dv.astype(bf16)
    sums = dot(jnp.ones((sums_ref.shape[2], length), bf16), out_ref[0])

    @pl.when(seq == 0)
    def _():
        sums_ref[0, 0] = sums

    @pl.when(seq > 0)
    def _():
        sums_ref[0, 0] += sums


def attention_specs(joined, mask_parts, turn=0):
    rows, length = mask_parts[0].shape[1:]

    def block(cols):
        return pl.BlockSpec((1, length, cols), lambda r, p, s, ids: (turn + r, s, p))

    logs = pl.BlockSpec((1, joined.shape[1], 128), lambda r, p, s, ids: (turn + r, 0, 0))
    mask = pl.BlockSpec((2, rows, length), lambda r, p, s, ids: (2 * p + (ids[1] ^ (turn + r)), 0, 0))
    return block, logs, [mask] * len(mask_parts)


def qkv_attend_kernel(blk, head_dim, steps, seqs, ids, *refs):
    mask_refs, inputs, refs = refs[:blk], refs[blk : 2 * blk + 4], refs[2 * blk + 4 :]
    x_ref, vec_ref, out_ref, o_ref, lse_ref, w_ref, w_far_ref, v_ref, joined_ref, sems = refs
    step = pl.program_id(0)

    @pl.when(step < steps)
    def _():
        qkv_kernel(
            blk, ids, joined_ref, *inputs, x_ref, vec_ref, out_ref, w_ref, w_far_ref, v_ref, sems
        )

    @pl.when(step >= steps)
    def _():
        turn, pair, seq = attend_step(step - steps, out_ref.shape[2] // 384, seqs)
        length = o_ref.shape[1]
        view = joined_ref.at[
            pl.ds(turn, 1),
            pl.ds(pl.multiple_of(seq * length, length), length),
            pl.ds(pl.multiple_of(pair * 384, 128), 384),
        ]
        attend_kernel(head_dim, pair, seq, ids, view, *mask_refs, o_ref, lse_ref)


def attend_step(step, pairs, seqs):
    step = jnp.maximum(step, 0)
    return step // (pairs * seqs), step // seqs % pairs, step % seqs


def qkv_attend(ids, parts, pieces, cols, mask_parts, head_dim, ties=()):
    blk = len(parts)
    seqs, block_rows, width = parts[0].shape
    length = blk * block_rows
    tokens = seqs * length
    block = 2 * block_rows
    steps = tokens // block
    pairs = cols // 384
    piece = pieces[0][0]
    shape = place_shape(piece, cols)
    x_shape = jax.ShapeDtypeStruct((seqs, blk, block_rows, width), bf16)
    v_shape = jax.ShapeDtypeStruct((16, width), f32)

    def at(index):
        def found(i, ids):
            return index(ids, *attend_step(i - steps, pairs, seqs))

        return found

    mask = pl.BlockSpec(
        (2, block_rows, length), at(lambda ids, r, p, s: (2 * p + (ids[1] ^ r), 0, 0))
    )
    return kernel_call(
        partial(qkv_attend_kernel, blk, head_dim, steps, seqs),
        ids,
        [*mask_parts, *parts, *pieces[0], *pieces[1]],
        ties,
        (steps + 2 * pairs * seqs,),
        [mask] * blk + [any_block()] * (blk + 4),
        (
            whole_block(x_shape),
            whole_block(v_shape),
            pl.BlockSpec((2, block, cols), lambda i, ids: (0, jnp.minimum(i, steps - 1), 0)),
            pl.BlockSpec((1, length, 128), at(lambda ids, r, p, s: (r, s, p))),
            pl.BlockSpec((1, tokens, 128), at(lambda ids, r, p, s: (r, 0, 0))),
        ),
        (
            x_shape,
            v_shape,
            jax.ShapeDtypeStruct((2, tokens, cols), bf16),
            jax.ShapeDtypeStruct((2, tokens, cols // 3), bf16),
            jax.ShapeDtypeStruct((2, tokens, 128), f32),
        ),
        [
            shape,
            shape,
            place_shape(piece, 128),
            pltpu.VMEM((2, tokens, cols), bf16),
            pltpu.SemaphoreType.DMA((blk + 6,)),
        ],
    )


def attend_back(
    ids, joined, attended, upstream, logs, mask_parts, turn, seqs, head_dim, ties=()
):
    tokens, cols = joined.shape[1:]
    count = cols // 384
    length = tokens // seqs
    block, log_block, masks = attention_specs(joined, mask_parts, turn)
    return kernel_call(
        partial(attend_back_kernel, head_dim),
        ids,
        [joined, attended, upstream, logs, *mask_parts],
        ties,
        (1, count, seqs),
        [block(384), block(128), block(128), log_block] + masks,
        (
            pl.BlockSpec((1, length, 384), lambda r, p, s, ids: (0, s, p)),
            pl.BlockSpec((1, 1, 8, 384), lambda r, p, s, ids: (r, p, 0, 0)),
        ),
        (
            jax.ShapeDtypeStruct((1, tokens, cols), bf16),
            jax.ShapeDtypeStruct((1, count, 8, 384), f32),
        ),
    )


def out_kernel(ids, att_ref, x_ref, vec_ref, *refs):
    pieces, (first_ref, low_ref, w_ref, sems) = (refs[:2], refs[2:4]), refs[4:]

    @pl.when(pl.program_id(0) == 0)
    def _():
        load = Loader(ids, sems)
        half = w_ref.shape[-1] // 2
        load.columns(pieces, pieces[0][0].shape[-1] - half, half, w_ref)
        load.wait()

    attended = pair_order(ids[1], att_ref[0], att_ref[1], 128)
    first = x_ref[...].astype(f32) + (dot(attended, flat(w_ref)) + vector(vec_ref, "bias_out"))
    first_ref[...] = first
    gain, shift = vector(vec_ref, "gain_first"), vector(vec_ref, "shift_first")
    low_ref[...] = (norm_stats(first)[0] * gain + shift).astype(bf16)


def out_projection(ids, attended, pieces, token_rows, vectors, block, ties=()):
    tokens, width = token_rows.shape
    row = pl.BlockSpec((block, width), lambda i, ids: (i, 0))
    return kernel_call(
        out_kernel,
        ids,
        [attended, token_rows, vectors, *pieces[0], *pieces[1]],
        ties,
        (tokens // block,),
        [
            pl.BlockSpec((2, block, width // 2), lambda i, ids: (0, i, 0)),
            row,
            whole_block(vectors),
        ]
        + [any_block()] * 4,
        (row, row),
        (jax.ShapeDtypeStruct((tokens, width), f32), jax.ShapeDtypeStruct((tokens, width), bf16)),
        [place_shape(pieces[0][0], width), pltpu.SemaphoreType.DMA((4,))],
        cost=brief,
    )


def up_kernel(chunk, steps, ids, h_ref, b_ref, *refs):
    pieces, (act_ref, der_ref, w_ref, w_far_ref, sems) = (refs[:2], refs[2:4]), refs[4:]
    step = pl.program_id(0)
    block = act_ref.shape[1]
    cols = w_ref.shape[-1]

    @pl.when(step == 0)
    def _():
        load = Loader(ids, sems)
        start = pieces[0][0].shape[-1] - cols
        load.rows(pieces[0], start, cols, w_ref)
        load.rows(pieces[1], start, cols, w_far_ref)
        load.wait()

    def run(ref):
        lanes = pl.ds(pl.multiple_of((step % steps) * block, block), block)
        weights = ref[:, :, :, lanes].reshape(-1, block)
        bias = b_ref[0]
        for first in range(0, h_ref.shape[0], chunk):
            place_ = slice(first, first + chunk)
            gate = dot(h_ref[place_, :], weights) + bias
            share = 0.5 + 0.5 * lax.erf(gate * math.sqrt(0.5))
            bell = jnp.exp2((-0.5 * log2e) * (gate * gate)) * (1.0 / math.sqrt(2.0 * math.pi))
            act_ref[place_, :] = (gate * share).astype(bf16)
            der_ref[place_, :] = (share + gate * bell).astype(bf16)

    pl.when(step < steps)(lambda: run(w_ref))
    pl.when(step >= steps)(lambda: run(w_far_ref))


def up_projection(ids, hidden_low, pieces, bias, ties=()):
    tokens, width = hidden_low.shape
    half = bias.shape[2]
    block = width
    steps = half // block
    out = pl.BlockSpec((tokens, block), lambda j, ids: (0, (ids[1] ^ (j // steps)) * steps + j % steps))
    shape = jax.ShapeDtypeStruct((tokens, 2 * half), bf16)
    scratch = place_shape(pieces[0][0], half)
    return kernel_call(
        partial(up_kernel, 128, steps),
        ids,
        [hidden_low, bias, *pieces[0], *pieces[1]],
        ties,
        (2 * steps,),
        [
            whole_block(hidden_low),
            pl.BlockSpec((1, 1, block), lambda j, ids: (ids[1] ^ (j // steps), 0, j % steps)),
        ]
        + [any_block()] * 4,
        (out, out),
        (shape, shape),
        [scratch, scratch, pltpu.SemaphoreType.DMA((4,))],
        cost=brief,
    )


def down_kernel(blk, ids, *refs):
    pos_ref, cot_ref, act_ref, der_ref, first_ref, vec_ref = refs[:6]
    mine, other = refs[6:8], refs[8:10]
    outs, refs = refs[10 : 10 + blk], refs[10 + blk :]
    gss_ref, gdi_ref, gate_ref, sums_ref, up_ref, w_ref, product_ref, sems = refs
    step = pl.program_id(0)
    here = ids[0]
    seqs, rows, width = first_ref.shape
    cols = act_ref.shape[-1]

    def product():
        return dot(act_ref[...].reshape(-1, cols), flat(w_ref))

    def add_to(ref, parts):
        total = [jnp.sum(part, axis=0, keepdims=True) for part in parts]
        total.append(jnp.zeros((ref.shape[0] - len(parts), ref.shape[1]), f32))
        ref[...] = jnp.where(step == 1, 0.0, ref[...]) + jnp.concatenate(total, axis=0)

    def take_on(multiplied):
        normed_one = norm_stats(first_ref[...].reshape(-1, width))[0]
        hidden = normed_one * vector(vec_ref, "gain_first") + vector(vec_ref, "shift_first")
        normed, inverse = norm_stats(hidden + (multiplied + vector(vec_ref, "bias_down")))
        gain = vector(vec_ref, "gain_second")
        result = (normed * gain + vector(vec_ref, "shift_second")).astype(bf16)
        slots = pos_ref.shape[-1]
        token = lax.broadcasted_iota(jnp.int32, (rows, slots), 0) + (here ^ (step - 1)) * rows
        upstream = jnp.concatenate(
            [
                dot(jnp.where(token == pos_ref[seq], 1.0, 0.0).astype(bf16), cot_ref[seq])
                for seq in range(seqs)
            ],
            axis=0,
        )
        grad = norm_pull(upstream, normed, inverse, gain)
        gss_ref[...] = grad.reshape(gss_ref.shape)
        low = grad.astype(bf16)
        gdi_ref[...] = low.reshape(gdi_ref.shape)
        grad_gate = dot_right_t(low, flat(w_ref)) * der_ref[...].reshape(-1, cols).astype(f32)
        grad_gate = grad_gate.astype(bf16)
        gate_ref[...] = grad_gate.reshape(gate_ref.shape)
        add_to(sums_ref, [low.astype(f32), upstream * normed, upstream])
        add_to(up_ref, [grad_gate.astype(f32)])
        return result

    def keep(result):
        for piece, out in enumerate(outs):

            @pl.when(step == piece + 1)
            def _():
                out[...] = result.reshape(out.shape)

    @pl.when(step == 0)
    def _():
        load = Loader(ids, sems)
        load.columns((mine, other), 0, width // 2, w_ref)
        load.wait()
        product_ref[...] = product()

    @pl.when((step > 0) & (step < blk))
    def _():
        following = product()
        result = take_on(product_ref[...])
        product_ref[...] = following
        keep(result)

    @pl.when(step == blk)
    def _():
        keep(take_on(product_ref[...]))


def down_projection(
    ids, active, slope, first_sum, pieces, vectors, marks, cot_values, seqs, blk, ties=()
):
    tokens, cols = active.shape
    width = first_sum.shape[1]
    length = tokens // seqs
    rows = length // blk

    def ahead(size):
        return pl.BlockSpec(
            (seqs, rows, size), lambda d, ids: (0, ids[0] ^ jnp.minimum(d, blk - 1), 0)
        )

    def block(size):
        return pl.BlockSpec(
            (seqs, rows, size), lambda d, ids: (0, ids[0] ^ jnp.maximum(d - 1, 0), 0)
        )

    def shape(size, dtype):
        return jax.ShapeDtypeStruct((seqs, length, size), dtype)

    piece = jax.ShapeDtypeStruct((seqs, rows, width), bf16)
    sums = jax.ShapeDtypeStruct((8, width), f32)
    up_sums = jax.ShapeDtypeStruct((8, cols), f32)
    slots = marks.shape[-1]
    by_seq = [array.reshape(seqs, length, -1) for array in (active, slope, first_sum)]
    outs = kernel_call(
        partial(down_kernel, blk),
        ids,
        [marks, cot_values, *by_seq, vectors, *pieces[0], *pieces[1]],
        ties,
        (blk + 1,),
        [
            whole_block(marks),
            pl.BlockSpec((seqs, slots, width), lambda d, ids: (ids[0], 0, 0)),
            ahead(cols),
            block(cols),
            block(width),
            whole_block(vectors),
        ]
        + [any_block()] * 4,
        [whole_block(piece)] * blk
        + [block(width), block(width), block(cols), whole_block(sums), whole_block(up_sums)],
        [piece] * blk + [shape(width, f32), shape(width, bf16), shape(cols, bf16), sums, up_sums],
        [
            place_shape(pieces[0][0], width),
            pltpu.VMEM((seqs * rows, width), f32),
            pltpu.SemaphoreType.DMA((4,)),
        ],
    )
    rest = outs[blk:]
    return outs[:blk], [array.reshape(tokens, -1) for array in rest[:3]], rest[3:]


def first_back_kernel(steps, ids, gate_ref, gss_ref, first_ref, vec_ref, *refs):
    pieces, out_pieces, refs = (refs[:2], refs[2:4]), (refs[4:6], refs[6:8]), refs[8:]
    gfs_ref, branch_ref, att_ref, sums_ref, w_ref, w_out_ref, product_ref, sems = refs
    width = gss_ref.shape[1]
    step = pl.program_id(0)

    def product():
        return dot_right_t(gate_ref[...], flat(w_ref))

    def take_on(multiplied):
        grad_hidden = gss_ref[...] + multiplied
        normed, inverse = norm_stats(first_ref[...])
        grad = norm_pull(grad_hidden, normed, inverse, vector(vec_ref, "gain_first"))
        gfs_ref[...] = grad
        low = grad.astype(bf16)
        branch_ref[...] = low
        grad_att = dot_right_t(low, flat(w_out_ref)).astype(bf16)
        att_ref[0], att_ref[1] = pair_split(ids[1], grad_att, 128)
        total = [
            jnp.sum(part, axis=0, keepdims=True)
            for part in (low.astype(f32), grad_hidden * normed, grad_hidden)
        ]
        total.append(jnp.zeros((sums_ref.shape[0] - len(total), width), f32))
        sums_ref[...] = jnp.where(step == 1, 0.0, sums_ref[...]) + jnp.concatenate(total, axis=0)

    @pl.when(step == 0)
    def _():
        load = Loader(ids, sems)
        load.columns(pieces, 0, w_ref.shape[-1] // 2, w_ref)
        start = out_pieces[0][0].shape[-1] - width // 2
        load.columns(out_pieces, start, width // 2, w_out_ref)
        load.wait()
        product_ref[...] = product()

    @pl.when((step > 0) & (step < steps))
    def _():
        following = product()
        take_on(product_ref[...])
        product_ref[...] = following

    @pl.when(step == steps)
    def _():
        take_on(product_ref[...])


def first_back(
    ids, grad_gate, grad_second_sum, first_sum, pieces, out_pieces, vectors, block, ties=()
):
    tokens, cols = grad_gate.shape
    width = first_sum.shape[1]

    steps = tokens // block

    def ahead(size):
        return pl.BlockSpec((block, size), lambda i, ids: (jnp.minimum(i, steps - 1), 0))

    def row(size):
        return pl.BlockSpec((block, size), lambda i, ids: (jnp.maximum(i - 1, 0), 0))

    def shape(size, dtype):
        return jax.ShapeDtypeStruct((tokens, size), dtype)

    sums = jax.ShapeDtypeStruct((8, width), f32)
    piece = pieces[0][0]
    return kernel_call(
        partial(first_back_kernel, steps),
        ids,
        [
            grad_gate,
            grad_second_sum,
            first_sum,
            vectors,
            *pieces[0],
            *pieces[1],
            *out_pieces[0],
            *out_pieces[1],
        ],
        ties,
        (steps + 1,),
        [ahead(cols), row(width), row(width), whole_block(vectors)] + [any_block()] * 8,
        (
            row(width),
            row(width),
            pl.BlockSpec(
                (2, block, width // 2), lambda i, ids: (0, jnp.maximum(i - 1, 0), 0)
            ),
            whole_block(sums),
        ),
        (
            shape(width, f32),
            shape(width, bf16),
            jax.ShapeDtypeStruct((2, tokens, width // 2), bf16),
            sums,
        ),
        [
            place_shape(piece, cols),
            place_shape(piece, width),
            pltpu.VMEM((block, width), f32),
            pltpu.SemaphoreType.DMA((8,)),
        ],
    )


def beside(array, devices, per):
    groups = array.reshape(devices, per, -1, array.shape[-1])
    return jnp.concatenate(
        [groups[:, index].reshape(-1, array.shape[-1]) for index in range(per)], axis=1
    )


def down_grad_kernel(devices, per, ids, act_ref, g_ref, keep_ref, send_ref):
    halves = half_split(ids[1], dot_left_t(act_ref[...], g_ref[...]))
    for half, out in zip(halves, (keep_ref, send_ref)):
        out[...] = (beside(half, devices, per) if per > 1 else half).astype(bf16)


def down_grad(ids, active, grad_down_in, devices, ties=()):
    tokens, cols = active.shape
    width = grad_down_in.shape[1]
    per, block = cols // width, width
    inside = (width // devices) % 8 == 0
    groups = per if inside else 1
    out = pl.BlockSpec((block // groups, groups * width // 2), lambda i, ids: (i, 0))
    shape = jax.ShapeDtypeStruct((cols // groups, groups * width // 2), bf16)
    halves = kernel_call(
        partial(down_grad_kernel, devices // per, groups),
        ids,
        [active, grad_down_in],
        ties,
        (cols // block,),
        [pl.BlockSpec((tokens, block), lambda i, ids: (0, i)), whole_block(grad_down_in)],
        (out, out),
        (shape, shape),
    )
    return halves if inside else [beside(half, devices, per) for half in halves]


def up_grad_kernel(ids, h_ref, g_ref, g_far_ref, keep_ref, send_ref):
    keep_ref[...] = dot_left_t(h_ref[...], g_ref[...]).astype(bf16)
    send_ref[...] = dot_left_t(h_ref[...], g_far_ref[...]).astype(bf16)


def up_grad(ids, hidden_low, grad_gate, block, ties=()):
    tokens, width = hidden_low.shape
    cols = grad_gate.shape[1] // 2
    steps = cols // block
    shape = jax.ShapeDtypeStruct((width, cols), bf16)
    out = pl.BlockSpec((width, block), lambda j, ids: (0, j))
    return kernel_call(
        up_grad_kernel,
        ids,
        [hidden_low, grad_gate, grad_gate],
        ties,
        (steps,),
        [
            whole_block(hidden_low),
            pl.BlockSpec((tokens, block), lambda j, ids: (0, ids[1] * steps + j)),
            pl.BlockSpec((tokens, block), lambda j, ids: (0, (1 - ids[1]) * steps + j)),
        ],
        (out, out),
        (shape, shape),
    )


def left_grad_kernel(
    ids,
    x_ref,
    g_ref,
    g_far_ref,
    att_ref,
    branch_ref,
    sums_ref,
    sums_far_ref,
    first_ref,
    second_ref,
    up_ref,
    *outs,
):
    core, step = ids[1], pl.program_id(0)
    attended = pair_order(core, att_ref[0], att_ref[1], 128)
    out_grads = half_split(core, dot_left_t(attended, branch_ref[...]))
    sums = [ref[0, step][:1] for ref in (sums_ref, sums_far_ref)]
    rows = [
        pair_order(core, sums[0][:, at : at + 128], sums[1][:, at : at + 128], 128)
        for at in (0, 256)
    ]
    rows += [first_ref[:3], second_ref[:3], up_ref[...]]
    used = sum(row.shape[0] for row in rows)
    rows = jnp.concatenate(rows + [jnp.zeros((16 - used, rows[0].shape[1]), f32)], axis=0)
    lanes = lax.broadcasted_iota(jnp.int32, (16, 128), 1)
    eye = lanes == lax.broadcasted_iota(jnp.int32, lanes.shape, 0)
    columns = dot_left_t(rows.astype(bf16), jnp.where(eye, 1.0, 0.0).astype(bf16))
    cut = outs[0].shape[1] - 128
    for turn, ref in enumerate((g_ref, g_far_ref)):
        grad = dot_left_t(x_ref[...], ref[0])
        first = jnp.concatenate([grad[:, :cut], columns], axis=1)
        second = jnp.concatenate([grad[:, cut:], out_grads[turn]], axis=1)
        outs[turn][...] = first.astype(bf16)
        outs[2 + turn][...] = second.astype(bf16)


def left_grad(ids, left, grads, attended, grad_branch, sums, totals, ties=()):
    tokens, width = left.shape
    cut = grads[0].shape[2] - 384
    sizes = [cut + 128] * 2 + [384 + width // 2] * 2
    return kernel_call(
        left_grad_kernel,
        ids,
        [left, *grads, attended, grad_branch, *sums, *totals],
        ties,
        (width // 256,),
        [
            pl.BlockSpec((tokens, 256), lambda i, ids: (0, i)),
            *[whole_block(grad) for grad in grads],
            pl.BlockSpec((2, tokens, 128), lambda i, ids: (0, 0, i)),
            whole_block(grad_branch),
            *[whole_block(array) for array in sums],
        ]
        + [pl.BlockSpec((array.shape[0], 256), lambda i, ids: (0, i)) for array in totals],
        [pl.BlockSpec((256, size), lambda i, ids: (i, 0)) for size in sizes],
        [jax.ShapeDtypeStruct((width, size), bf16) for size in sizes],
    )


def input_grad_kernel(blk, ids, g_ref, g_far_ref, gfs_ref, *refs):
    pieces, refs = (refs[:2], refs[2:4]), refs[4:]
    outs, (w_ref, w_far_ref, sems) = refs[:blk], refs[blk:]
    step = pl.program_id(0)

    @pl.when(step == 0)
    def _():
        load = Loader(ids, sems)
        load.rows(pieces[0], 0, w_ref.shape[-1], w_ref)
        load.rows(pieces[1], 0, w_ref.shape[-1], w_far_ref)
        load.wait()

    width = gfs_ref.shape[-1]
    total = gfs_ref[...].reshape(-1, width)
    for ref, weights in ((g_ref, w_ref), (g_far_ref, w_far_ref)):
        total = total + dot_right_t(ref[...].reshape(-1, ref.shape[-1]), flat(weights))
    for piece, out in enumerate(outs):

        @pl.when(step == piece)
        def _():
            out[...] = total.astype(bf16).reshape(out.shape)


def input_grad(ids, grads, grad_first_sum, pieces, seqs, blk, ties=()):
    tokens, width = grad_first_sum.shape
    length = tokens // seqs
    rows = length // blk
    cols = grads[0].shape[2]
    piece = jax.ShapeDtypeStruct((seqs, rows, width), bf16)
    shape = place_shape(pieces[0][0], cols)
    pieces = [*pieces[0], *pieces[1]]
    return kernel_call(
        partial(input_grad_kernel, blk),
        ids,
        [
            *[grad.reshape(seqs, length, cols) for grad in grads],
            grad_first_sum.reshape(seqs, length, width),
            *pieces,
        ],
        ties,
        (blk,),
        [
            *[pl.BlockSpec((seqs, rows, cols), lambda d, ids: (0, ids[0] ^ d, 0))] * 2,
            pl.BlockSpec((seqs, rows, width), lambda d, ids: (0, ids[0] ^ d, 0)),
        ]
        + [any_block()] * len(pieces),
        [whole_block(piece)] * blk,
        [piece] * blk,
        [shape, shape, pltpu.SemaphoreType.DMA((len(pieces),))],
    )


class Grid:
    def __init__(self, mesh):
        batch, blk = mesh.shape["batch"], mesh.shape["blk"]
        self.sizes = {"z": batch // 2, "y": 2, "x": blk // 2, "c": 2}
        self.strides = {"c": 1, "x": 2, "y": blk, "z": 2 * blk}
        self.total = batch * blk
        self.blk = blk

    def digit(self, name):
        index = lax.axis_index("batch") * self.blk + lax.axis_index("blk")
        return (index // self.strides[name]) % self.sizes[name]

    def swap(self, array, name, delta=1):
        size, stride = self.sizes[name], self.strides[name]
        pairs = []
        for index in range(self.total):
            here = (index // stride) % size
            pairs.append((index, index + ((here ^ delta) - here) * stride))
        return lax.ppermute(array, both, pairs)

    def swap_blk(self, array, delta):
        pairs = [(index, index ^ delta) for index in range(self.total)]
        return lax.ppermute(array, both, pairs)


def place(parts, index):
    if len(parts) == 1:
        return parts[0][None]
    rows = []
    for target in range(len(parts)):
        row = parts[0]
        for delta in range(1, len(parts)):
            row = jnp.where(index == target ^ delta, parts[delta], row)
        rows.append(row)
    return jnp.stack(rows)


def pick(array, index):
    return lax.dynamic_index_in_dim(array, index, axis=0, keepdims=False)


def gather_core(grid, mine, other):
    cols = mine.shape[1]
    return place([mine, grid.swap(other, "c")], grid.digit("c")).reshape(-1, cols)


def gather_step(grid, run, held, name, *ties):
    parts = [grid.swap(held, name, d) for d in range(1, grid.sizes[name])]
    return place_parts(run, [held, *parts], name, ties)


def gather_last(grid, held, name):
    far = grid.swap(held, name)
    if held.shape[1] % 16 == 0:
        return [held, far]
    where = grid.digit(name)
    whole = jnp.moveaxis(place([held, far], where), 0, 1).reshape(4, 2, -1, held.shape[2])
    return [lax.dynamic_index_in_dim(whole, where ^ d, 1, keepdims=False) for d in range(2)]


def gather_pieces(grid, run, held, *ties):
    near, far = held
    if ties:
        (far,) = after(run, [far], *ties)
    return [[near, far], [grid.swap(near, "c"), grid.swap(far, "c")]]


def add_low(*parts):
    total = parts[0].astype(f32)
    for part in parts[1:]:
        total = total + part.astype(f32)
    return total


def fold_kernel(count, groups, ids, *refs):
    outs = refs[len(refs) - count :]
    refs = list(refs[: len(refs) - count])
    for out in outs:
        sums = []
        for terms in groups:
            picked, refs = refs[:terms], refs[terms:]
            total = picked[0][...].astype(f32)
            for ref in picked[1:]:
                total = total + ref[...].astype(f32)
            sums.append(total.astype(out.dtype))
        out[...] = jnp.concatenate(sums, axis=-1).reshape(out.shape)


def fold(ids, which, groups, ties):
    outer, count, rows, unused = groups[0][0].shape
    steps = 2 if outer % 2 == 0 else 1
    part = outer // steps

    def term_block(cols, delta):
        return pl.BlockSpec((part, 1, rows, cols), lambda i, ids: (i, ids[which] ^ delta, 0, 0))

    terms = [term for group in groups for term in group]
    cols = sum(group[0].shape[3] for group in groups)
    shape = jax.ShapeDtypeStruct((outer, rows, cols), bf16)
    return kernel_call(
        partial(fold_kernel, count, [len(group) for group in groups]),
        ids,
        [term for delta in range(count) for term in terms],
        ties,
        (steps,),
        [term_block(term.shape[3], delta) for delta in range(count) for term in terms],
        [pl.BlockSpec((part, rows, cols), lambda i, ids: (i, 0, 0))] * count,
        [shape] * count,
    )


class Scatter:
    def __init__(self, grid, ids, pairs, order):
        self.grid, self.ids, self.order = grid, ids, list(order)
        sizes = grid.sizes
        self.left = [("z", sizes["z"]), ("y", sizes["y"]), ("x", sizes["x"])]
        self.last = 2 * (pairs[0][0].shape[0] // grid.total)
        self.groups = [[keep, grid.swap(send, "c")] for keep, send in pairs]

    def join(self, other):
        self.groups = self.groups + other.groups
        return self

    def shaped(self, *shape):
        return [[term.reshape(*shape, term.shape[-1]) for term in group] for group in self.groups]

    def step(self, ties=()):
        name = self.order.pop(0)
        index = [left for left, unused in self.left].index(name)
        count = self.left[index][1]
        outer = math.prod(size for unused, size in self.left[:index])
        inner = math.prod(size for unused, size in self.left[index + 1 :]) * self.last
        sums = fold(self.ids, id_of[name], self.shaped(outer, count, inner), ties)
        self.left.pop(index)
        sent = [self.grid.swap(sums[delta], name, delta) for delta in range(1, count)]
        self.groups = [[sums[0], *sent]]

    def end(self, ties=()):
        mine, other = fold(self.ids, id_of["c"], self.shaped(1, 2, self.last // 2), ties)
        mine, other = [array.reshape(array.shape[1:]) for array in (mine, other)]
        return mine.astype(f32), self.grid.swap(other, "c").astype(f32)


def in_order(core, mine, other):
    return jnp.where(core == 0, mine, other), jnp.where(core == 0, other, mine)


def local(
    grid,
    inputs,
    w_qkv,
    bias_query,
    bias_value,
    w_out,
    bias_out,
    gain_first,
    shift_first,
    w_up,
    bias_up,
    w_down,
    bias_down,
    gain_second,
    shift_second,
    dam_mask,
    positions,
    counts,
    cot_values,
):
    groups, block_rows, width = inputs.shape
    head_count = dam_mask.shape[0]
    head_dim = width // head_count
    blk = grid.blk
    seqs = groups // blk
    length = blk * block_rows
    tokens = seqs * length
    here, core = lax.axis_index("blk"), grid.digit("c")
    ids = Run(jnp.stack([here, core] + [grid.digit(name) for name in "yzx"]).astype(jnp.int32))
    rows = w_qkv.shape[0]
    up_per = bias_up.shape[0] // rows
    half = width // 2
    pairs = width // 256

    vectors = (
        bias_query,
        bias_value,
        bias_out,
        gain_first,
        shift_first,
        bias_down,
        gain_second,
        shift_second,
    )
    stacked = jnp.concatenate(
        [
            jnp.stack(vectors),
            bias_up.reshape(rows, up_per).T,
            jnp.zeros((16 - len(vectors) - up_per, rows), bf16),
        ]
    )
    halves = split_weights(ids, w_qkv, stacked, w_out, w_up, w_down)
    first_near, second_near, down_near = [gather_core(grid, *pair) for pair in halves]

    def over_x(held):
        return gather_step(grid, ids, held, "x").reshape(-1, held.shape[1])

    first_near = over_x(first_near)
    event = ids.token

    by_home = inputs.reshape(blk, seqs, block_rows, width)
    parts = [pick(by_home, here ^ delta) for delta in range(blk)]
    parts[1:] = after(ids, parts[1:], event)
    parts[1:] = [grid.swap_blk(parts[delta], delta) for delta in range(1, blk)]
    addend = mask_addend(ids, dam_mask, [event])
    mask_parts = [addend, grid.swap(addend, "c")]
    second_near, down_near = after(ids, [second_near, down_near], event)
    second_near = over_x(second_near)
    ties = [ids.token]
    down_near = over_x(down_near)
    ties.append(ids.token)

    first_z = gather_step(grid, ids, first_near, "z", *ties, *parts[2:])
    (second_near,) = after(ids, [second_near], ids.token)
    first_y = gather_last(grid, first_z, "y")
    first_pieces = gather_pieces(grid, ids, first_y)
    ties = []
    if grid.sizes["x"] > 1:
        far = grid.swap(addend, "x")
        mask_parts += [far, grid.swap(far, "c")]
        ties = [far]
    second_z = gather_step(grid, ids, second_near, "z", *ties)
    (down_near,) = after(ids, [down_near], ids.token)
    second_y = gather_last(grid, second_z, "y")
    token_rows, vector_rows, joined, attended, logs = qkv_attend(
        ids, parts, first_pieces, 3 * half, mask_parts, head_dim, ties=[ids.token]
    )
    token_rows = token_rows.reshape(tokens, width)
    first_row = len(vectors)
    up_bias = vector_rows[first_row : first_row + up_per].T.reshape(2, 1, -1)
    down_z = gather_step(grid, ids, down_near, "z", ids.token)
    down_y = gather_last(grid, down_z, "y")
    second_pieces = gather_pieces(grid, ids, second_y, ids.token)
    first_sum, hidden_low = out_projection(
        ids, attended, first_pieces, token_rows, vector_rows, 2 * block_rows
    )
    active, slope = up_projection(ids, hidden_low, second_pieces, up_bias)
    down_pieces = gather_pieces(grid, ids, down_y, ids.token)

    my_positions = pick(positions.reshape(blk, seqs, -1), here)
    my_counts = pick(counts.reshape(blk, seqs), here)
    live = jnp.arange(positions.shape[1], dtype=jnp.int32)[None, :] < my_counts[:, None]
    marks = jnp.where(live, my_positions, -1)[:, None, :]
    result, (grad_second_sum, grad_down_in, grad_gate), (second_sums, up_sums) = down_projection(
        ids, active, slope, first_sum, down_pieces, vector_rows, marks, cot_values, seqs, blk
    )

    def home(pieces):
        return [pieces[0]] + [grid.swap_blk(pieces[delta], delta) for delta in range(1, blk)]

    result = home(result)
    down_halves = down_grad(ids, active, grad_down_in, grid.total)
    up_halves = up_grad(ids, hidden_low, grad_gate, width, ties=[ids.token])
    up_sum = Scatter(grid, ids, [up_halves], "yxz")
    ffn_sum = Scatter(grid, ids, [down_halves], "xyz")
    ffn_sum.step([ids.token])
    up_sum.step([ids.token])
    grad_first_sum, grad_branch, grad_attended, first_sums = first_back(
        ids,
        grad_gate,
        grad_second_sum,
        first_sum,
        second_pieces,
        first_pieces,
        vector_rows,
        2 * block_rows,
        ties=[ids.token],
    )
    result = after(ids, result, ids.token)
    def back(turn):
        return attend_back(
            ids,
            joined,
            attended,
            grad_attended,
            logs,
            mask_parts,
            turn,
            seqs,
            head_dim,
            ties=[ids.token],
        )

    far_grads, far_sums = back(1)
    ffn_sum.step([ids.token])
    up_sum.step([ids.token])
    near_grads, near_sums = back(0)
    grads, grad_sums = (near_grads, far_grads), (near_sums, far_sums)
    ffn_sum = up_sum.join(ffn_sum)
    ffn_sum.step([ids.token])
    up_rows = up_sums[0].reshape(width, up_per).T
    totals = [first_sums, second_sums, up_rows]
    halves = left_grad(
        ids, token_rows, grads, attended, grad_branch, grad_sums, totals, ties=[ids.token]
    )
    one_sum = Scatter(grid, ids, [halves[:2]], "xyz")
    two_sum = Scatter(grid, ids, [halves[2:]], "yxz")
    one_sum.step([ids.token])
    two_sum.step([ids.token])
    sent = input_grad(ids, grads, grad_first_sum, first_pieces, seqs, blk, ties=[ids.token])
    one_sum.step([ids.token])
    two_sum.step([ids.token])
    grad_inputs = home(sent)
    activations = place_parts(ids, result, "here", [ids.token])
    activations = activations.reshape(groups, block_rows, width)
    att_sum = one_sum.join(two_sum)
    att_sum.step([ids.token])
    share_ffn = ffn_sum.end([ids.token])
    grad_inputs = widen_parts(ids, grad_inputs, "here", [ids.token])
    grad_inputs = grad_inputs.reshape(groups, block_rows, width)
    share_att = att_sum.end([ids.token])

    cut = near_grads.shape[2] - 384
    share_qkv = [
        jnp.concatenate([share[:, :cut], share[:, cut + 128 : cut + 512]], axis=1)
        for share in share_att
    ]
    by_core = jnp.stack(in_order(core, *share_qkv), axis=0).reshape(2, rows, pairs, 3, 128)
    share_qkv = by_core.transpose(1, 3, 2, 0, 4).reshape(rows, 3 * width)
    share_out = jnp.concatenate(in_order(core, *[share[:, cut + 512 :] for share in share_att]), axis=1)
    up_cols = up_halves[0].shape[1]
    share_up = [share[:, :up_cols] for share in share_ffn]
    share_down = [
        share[:, up_cols:].reshape(rows, up_per, half).transpose(1, 0, 2).reshape(-1, half)
        for share in share_ffn
    ]
    shares = share_att[0][:, cut : cut + 128]
    share_vectors = [shares[:, index] for index in range(len(vectors))]
    share_bias_up = shares[:, len(vectors) : len(vectors) + up_per].reshape(-1)
    (
        share_bias_query,
        share_bias_value,
        share_bias_out,
        share_gain_first,
        share_shift_first,
        share_bias_down,
        share_gain_second,
        share_shift_second,
    ) = share_vectors
    return (
        activations,
        grad_inputs,
        share_qkv,
        share_bias_query,
        share_bias_value,
        share_out,
        share_bias_out,
        share_gain_first,
        share_shift_first,
        jnp.concatenate(in_order(core, *share_up), axis=1),
        share_bias_up,
        jnp.concatenate(in_order(core, *share_down), axis=1),
        share_bias_down,
        share_gain_second,
        share_shift_second,
    )


def solution(mesh):
    sharded = P(both)
    rows = P(both, None)
    whole = P("batch", "blk", None)
    return jax.shard_map(
        partial(local, Grid(mesh)),
        mesh=mesh,
        in_specs=(
            whole,
            rows,
            sharded,
            sharded,
            rows,
            sharded,
            sharded,
            sharded,
            rows,
            sharded,
            rows,
            sharded,
            sharded,
            sharded,
            P(None, "blk", None),
            P("batch", None),
            P("batch"),
            P("batch", None, None),
        ),
        out_specs=(
            whole,
            whole,
            rows,
            sharded,
            sharded,
            rows,
            sharded,
            sharded,
            sharded,
            rows,
            sharded,
            rows,
            sharded,
            sharded,
            sharded,
        ),
        check_vma=False,
    )
```

```python
import math
from functools import partial

import jax
import jax.numpy as jnp
from jax import lax
from jax.experimental import pallas as pl
from jax.experimental.pallas import tpu as pltpu
from jax.sharding import PartitionSpec as P

norm_eps = 1e-06
masked_score = -1e30
f32 = jnp.float32
bf16 = jnp.bfloat16
both = ("batch", "blk")
log2e = math.log2(math.e)
long, brief, least = 10**11, 100000000000, 100000000000
roomy = pltpu.CompilerParams(vmem_limit_bytes=48 << 20)
vector_names = (
    "bias_query",
    "bias_value",
    "bias_out",
    "gain_first",
    "shift_first",
    "bias_down",
    "gain_second",
    "shift_second",
)
row_of = {name: index for index, name in enumerate(vector_names)}


def dot(left, right):
    return jnp.dot(left, right, preferred_element_type=f32)


def dot_right_t(left, right):
    return lax.dot_general(left, right, (((1,), (1,)), ((), ())), preferred_element_type=f32)


def dot_left_t(left, right):
    return lax.dot_general(left, right, (((0,), (0,)), ((), ())), preferred_element_type=f32)


def norm_stats(rows):
    center = jnp.mean(rows, axis=-1, keepdims=True)
    centered = rows - center
    inverse = lax.rsqrt(jnp.mean(centered * centered, axis=-1, keepdims=True) + norm_eps)
    return centered * inverse, inverse


def norm_pull(upstream, normed, inverse, gain):
    scaled = upstream * gain
    inner = jnp.mean(scaled, axis=-1, keepdims=True)
    projected = jnp.mean(scaled * normed, axis=-1, keepdims=True)
    return inverse * (scaled - inner - normed * projected)


def vector(ref, name):
    index = row_of[name]
    return ref[index : index + 1, :]


def piece_rows(here, piece, rows):
    return pl.ds(pl.multiple_of((here ^ piece) * rows, rows), rows)


def stack_pieces(ref, places, cols):
    return jnp.concatenate([ref[0, place_, cols] for place_ in places], axis=0)


def any_block():
    return pl.BlockSpec(memory_space=pl.ANY)


def whole_block(array):
    return pl.BlockSpec(array.shape, lambda *unused: (0,) * len(array.shape))


def pair_order(core, first, second, wide):
    blocks = []
    for start in range(0, first.shape[-1], wide):
        left, right = first[:, start : start + wide], second[:, start : start + wide]
        blocks += [jnp.where(core == 0, left, right), jnp.where(core == 0, right, left)]
    return jnp.concatenate(blocks, axis=1)


def pair_split(core, array, wide):
    outs = []
    for turn in range(2):
        outs.append(
            jnp.concatenate(
                [
                    jnp.where(
                        core == turn,
                        array[:, start : start + wide],
                        array[:, start + wide : start + 2 * wide],
                    )
                    for start in range(0, array.shape[1], 2 * wide)
                ],
                axis=1,
            )
        )
    return outs


def half_split(core, array):
    half = array.shape[1] // 2
    left, right = array[:, :half], array[:, half:]
    return jnp.where(core == 0, left, right), jnp.where(core == 0, right, left)


class Run:
    def __init__(self, ids):
        self.ids, self.token = ids, None


id_of = {"here": 0, "c": 1, "y": 2, "z": 3, "x": 4}
token_shape = jax.ShapeDtypeStruct((8, 128), f32)


def after(run, arrays, *ties):
    shapes = [jax.ShapeDtypeStruct(array.shape, array.dtype) for array in arrays]

    def body(*refs):
        refs[-1][...] = jnp.zeros(token_shape.shape, f32)

    *arrays, run.token = pl.pallas_call(
        body,
        out_shape=shapes + [token_shape],
        in_specs=[any_block()] * (len(arrays) + len(ties)),
        out_specs=[any_block()] * len(arrays) + [pl.BlockSpec(memory_space=pltpu.VMEM)],
        input_output_aliases={index: index for index in range(len(arrays))},
    )(*arrays, *ties)
    return arrays


def kernel_call(
    kernel, run, arrays, ties, grid, in_specs, out_specs, out_shape, scratch=(), cost=long
):
    several = isinstance(out_shape, (list, tuple))
    out_specs, out_shape = [
        list(value) if several else [value] for value in (out_specs, out_shape)
    ]
    count, outs = 1 + len(arrays), len(out_shape)

    def body(*refs):
        inputs, refs = refs[:count], refs[count + len(ties) :]
        refs[outs][...] = jnp.zeros(token_shape.shape, f32)
        kernel(*inputs, *refs[:outs], *refs[outs + 1 :])

    *results, run.token = pl.pallas_call(
        body,
        out_shape=out_shape + [token_shape],
        grid_spec=pltpu.PrefetchScalarGridSpec(
            num_scalar_prefetch=1,
            grid=grid,
            in_specs=list(in_specs) + [any_block()] * len(ties),
            out_specs=out_specs + [whole_block(token_shape)],
            scratch_shapes=scratch,
        ),
        compiler_params=roomy,
        cost_estimate=pl.CostEstimate(flops=cost, bytes_accessed=1024, transcendentals=0),
    )(run.ids, *arrays, *ties)
    return results if several else results[0]


def place_kernel(digit, count, ids, *refs):
    parts, (out, sems) = refs[:count], refs[count:]
    copies = [
        pltpu.make_async_copy(part, out.at[ids[digit] ^ delta], sems.at[delta])
        for delta, part in enumerate(parts)
    ]
    for copy in copies:
        copy.start()
    for copy in copies:
        copy.wait()


def place_parts(run, parts, digit, ties=()):
    count = len(parts)
    return kernel_call(
        partial(place_kernel, id_of[digit], count),
        run,
        parts,
        ties,
        (1,),
        [whole_block(part) for part in parts],
        any_block(),
        jax.ShapeDtypeStruct((count, *parts[0].shape), parts[0].dtype),
        [pltpu.SemaphoreType.DMA((count,))],
        cost=least,
    )


def widen_kernel(digit, count, ids, *refs):
    for delta in range(count):
        refs[count][ids[digit] ^ delta] = refs[delta][...].astype(f32)


def widen_parts(run, parts, digit, ties=()):
    count = len(parts)
    shape = jax.ShapeDtypeStruct((count, *parts[0].shape), f32)
    return kernel_call(
        partial(widen_kernel, id_of[digit], count),
        run,
        parts,
        ties,
        (1,),
        [whole_block(part) for part in parts],
        whole_block(shape),
        shape,
    )


def addend_kernel(ids, mask_ref, out_ref):
    out_ref[...] = jnp.where(mask_ref[...] > 0, 0.0, masked_score).astype(bf16)


def mask_addend(run, mask, ties):
    heads, rows, cols = mask.shape
    block = pl.BlockSpec((heads // 4, rows, cols), lambda i, ids: (i, 0, 0))
    shape = jax.ShapeDtypeStruct(mask.shape, bf16)
    return kernel_call(addend_kernel, run, [mask], ties, (4,), [block], block, shape)


class Loader:
    def __init__(self, ids, sems, digit="y"):
        self.core, self.digit = ids[id_of["c"]], ids[id_of[digit]]
        self.sems, self.copies = sems, []

    def put(self, source, target):
        copy = pltpu.make_async_copy(source, target, self.sems.at[len(self.copies)])
        copy.start()
        self.copies.append(copy)

    def rows(self, pieces, start, size, target):
        for turn, piece in enumerate(pieces):
            self.put(piece.at[:, :, pl.ds(start, size)], target.at[:, self.digit ^ turn])

    def columns(self, both_cores, start, size, target):
        for other, pieces in enumerate(both_cores):
            lanes = pl.ds(pl.multiple_of((self.core ^ other) * size, 128), size)
            for turn, piece in enumerate(pieces):
                self.put(
                    piece.at[:, :, pl.ds(start, size)], target.at[:, self.digit ^ turn, :, lanes]
                )

    def wait(self):
        for copy in self.copies:
            copy.wait()


def flat(ref, first=None, count=None):
    value = ref[...] if first is None else ref[pl.ds(first, count)]
    return value.reshape(-1, value.shape[-1])


def place_shape(piece, cols):
    return pltpu.VMEM((piece.shape[0], 2, piece.shape[1], cols), bf16)


def split_kernel(ids, qkv_ref, vec_ref, out_ref, up_ref, down_ref, *outs):
    core = ids[1]
    width = down_ref.shape[1]
    lanes = lax.broadcasted_iota(jnp.int32, (vec_ref.shape[0], 128), 1)
    eye = lanes == lax.broadcasted_iota(jnp.int32, lanes.shape, 0)
    columns = dot_left_t(vec_ref[...], jnp.where(eye, 1.0, 0.0).astype(bf16)).astype(bf16)
    for turn in range(2):
        first, second, down = outs[3 * turn : 3 * turn + 3]
        pairs = []
        for start in range(0, width, 256):
            for part in range(3):
                left = qkv_ref[:, part * width + start : part * width + start + 128]
                right = qkv_ref[:, part * width + start + 128 : part * width + start + 256]
                pairs.append(jnp.where(core == turn, left, right))
        out_half, second[...] = [half_split(core, ref[...])[turn] for ref in (out_ref, up_ref)]
        first[...] = jnp.concatenate(pairs + [columns, out_half], axis=1)
        down[...] = half_split(core, down_ref[...])[turn]


def split_weights(ids, w_qkv, vectors, w_out, w_up, w_down, ties=()):
    rows, cols = w_qkv.shape
    arrays = [w_qkv, vectors, w_out, w_up, w_down]
    shapes = [
        jax.ShapeDtypeStruct((rows, cols // 2 + 128 + w_out.shape[1] // 2), bf16),
        jax.ShapeDtypeStruct((rows, w_up.shape[1] // 2), bf16),
        jax.ShapeDtypeStruct((w_down.shape[0], w_down.shape[1] // 2), bf16),
    ] * 2
    outs = kernel_call(
        split_kernel,
        ids,
        arrays,
        ties,
        (1,),
        [whole_block(array) for array in arrays],
        [whole_block(shape) for shape in shapes],
        shapes,
        cost=least,
    )
    return list(zip(outs[:3], outs[3:]))


def qkv_kernel(blk, ids, joined_ref, *refs):
    parts, refs = refs[:blk], refs[blk:]
    pieces, refs = (refs[:2], refs[2:4]), refs[4:]
    x_ref, vec_ref, out_ref, w_ref, w_far_ref, v_ref, sems = refs
    here, core = ids[0], ids[1]
    step = pl.program_id(0)
    cols = out_ref.shape[2]
    block = out_ref.shape[1]

    @pl.when(step == 0)
    def _():
        load = Loader(ids, sems)
        for piece, part in enumerate(parts):
            load.put(part, x_ref.at[:, here ^ piece])
        load.rows(pieces[0], 0, cols, w_ref)
        load.rows(pieces[1], 0, cols, w_far_ref)
        load.rows(pieces[0], cols, 128, v_ref)
        load.wait()
        vec_ref[...] = flat(v_ref).astype(f32).T[: vec_ref.shape[0]]

    per_seq = x_ref.shape[1] // 2
    rows = x_ref[step // per_seq, pl.ds(2 * (step % per_seq), 2)].reshape(-1, x_ref.shape[-1])
    for turn, weights in enumerate((w_ref, w_far_ref)):
        bias = []
        for start in range(0, vec_ref.shape[1], 256):
            for name in ("bias_query", None, "bias_value"):
                if name is None:
                    bias.append(jnp.zeros((1, 128), f32))
                    continue
                row = vector(vec_ref, name)
                bias.append(
                    jnp.where(
                        core == turn, row[:, start : start + 128], row[:, start + 128 : start + 256]
                    )
                )
        total = dot(rows, flat(weights)) + jnp.concatenate(bias, axis=1)
        low = total.astype(bf16)
        out_ref[turn] = low
        joined_ref[turn, pl.ds(pl.multiple_of(step * block, block), block), :] = low


def attend_kernel(head_dim, pair, seq, ids, qkv_ref, *rest):
    pieces, (o_ref, lse_ref) = rest[:-2], rest[-2:]
    here = ids[0]
    length, wide = o_ref.shape[1:]
    per = wide // head_dim
    rows = pieces[0].shape[1]
    lanes = lax.broadcasted_iota(jnp.int32, (1, wide), 1)
    log_lanes = lax.broadcasted_iota(jnp.int32, (1, lse_ref.shape[2]), 1)
    keys, values = qkv_ref[0, :, wide : 2 * wide], qkv_ref[0, :, 2 * wide :]
    for first in range(0, len(pieces), 4):
        span = range(first, min(first + 4, len(pieces)))
        places = [piece_rows(here, piece, rows) for piece in span]
        queries = stack_pieces(qkv_ref, places, slice(0, wide))
        out, logs = None, []
        for head in range(per):
            mine = lanes // head_dim == head
            scores = dot_right_t(jnp.where(mine, queries, 0), keys) * (head_dim**-0.5 * log2e)
            addend = jnp.concatenate([pieces[piece][head] for piece in span], axis=0)
            scores = scores + addend.astype(f32)
            top = jnp.max(scores, axis=1, keepdims=True)
            weights = jnp.exp2(scores - top)
            total = jnp.sum(weights, axis=1, keepdims=True)
            part = dot(weights.astype(bf16), values) * (1.0 / total)
            out = part if out is None else jnp.where(mine, part, out)
            logs.append(top + jnp.log2(total))
        for index, place_ in enumerate(places):
            here_rows = slice(index * rows, (index + 1) * rows)
            o_ref[0, place_, :] = out[here_rows].astype(bf16)
            start = seq * length + (here ^ span[index]) * rows
            log_place = pl.ds(pl.multiple_of(start, rows), rows)
            kept = lse_ref[0, log_place, :]
            for head in range(per):
                kept = jnp.where(log_lanes == pair * per + head, logs[head][here_rows], kept)
            lse_ref[0, log_place, :] = kept


def attend_back_kernel(head_dim, ids, qkv_ref, o_ref, g_ref, lse_ref, *rest):
    pieces, (out_ref, sums_ref) = rest[:-2], rest[-2:]
    here = ids[0]
    pair, seq = pl.program_id(1), pl.program_id(2)
    length, wide = o_ref.shape[1:]
    per = wide // head_dim
    rows = pieces[0].shape[1]
    lanes = lax.broadcasted_iota(jnp.int32, (1, wide), 1)
    log_lanes = lax.broadcasted_iota(jnp.int32, (1, lse_ref.shape[2]), 1)
    keys, values = qkv_ref[0, :, wide : 2 * wide], qkv_ref[0, :, 2 * wide :]
    everything = slice(None)
    back = head_dim**-0.5
    dk = jnp.zeros(keys.shape, f32)
    dv = jnp.zeros(keys.shape, f32)
    for first in range(0, len(pieces), 4):
        span = range(first, min(first + 4, len(pieces)))
        places = [piece_rows(here, piece, rows) for piece in span]
        queries = stack_pieces(qkv_ref, places, slice(0, wide))
        ups = stack_pieces(g_ref, places, everything)
        products = ups.astype(f32) * stack_pieces(o_ref, places, everything).astype(f32)
        starts = [seq * length + (here ^ piece) * rows for piece in span]
        log_places = [pl.ds(pl.multiple_of(at, rows), rows) for at in starts]
        logs = stack_pieces(lse_ref, log_places, everything)
        dq = None
        for head in range(per):
            mine = lanes // head_dim == head
            q_mine, g_mine = jnp.where(mine, queries, 0), jnp.where(mine, ups, 0)
            inner = jnp.sum(jnp.where(mine, products, 0.0), axis=1, keepdims=True)
            log = jnp.sum(
                jnp.where(log_lanes == pair * per + head, logs, 0.0), axis=1, keepdims=True
            )
            scores = dot_right_t(q_mine, keys) * (back * log2e)
            addend = jnp.concatenate([pieces[piece][head] for piece in span], axis=0)
            exact = jnp.exp2(scores + addend.astype(f32) - log)
            grads = (exact * (dot_right_t(g_mine, values) - inner)).astype(bf16)
            dv = dv + dot_left_t(exact.astype(bf16), g_mine)
            dk = dk + dot_left_t(grads, q_mine)
            part = dot(grads, keys)
            dq = part if dq is None else jnp.where(mine, part, dq)
        for index, place_ in enumerate(places):
            out_ref[0, place_, :wide] = (dq[index * rows : (index + 1) * rows] * back).astype(bf16)
    out_ref[0, :, wide : 2 * wide] = (dk * back).astype(bf16)
    out_ref[0, :, 2 * wide :] = dv.astype(bf16)
    sums = dot(jnp.ones((sums_ref.shape[2], length), bf16), out_ref[0])

    @pl.when(seq == 0)
    def _():
        sums_ref[0, 0] = sums

    @pl.when(seq > 0)
    def _():
        sums_ref[0, 0] += sums


def attention_specs(joined, mask_parts, turn=0):
    rows, length = mask_parts[0].shape[1:]

    def block(cols):
        return pl.BlockSpec((1, length, cols), lambda r, p, s, ids: (turn + r, s, p))

    logs = pl.BlockSpec((1, joined.shape[1], 128), lambda r, p, s, ids: (turn + r, 0, 0))
    mask = pl.BlockSpec((2, rows, length), lambda r, p, s, ids: (2 * p + (ids[1] ^ (turn + r)), 0, 0))
    return block, logs, [mask] * len(mask_parts)


def qkv_attend_kernel(blk, head_dim, steps, seqs, ids, *refs):
    mask_refs, inputs, refs = refs[:blk], refs[blk : 2 * blk + 4], refs[2 * blk + 4 :]
    x_ref, vec_ref, out_ref, o_ref, lse_ref, w_ref, w_far_ref, v_ref, joined_ref, sems = refs
    step = pl.program_id(0)

    @pl.when(step < steps)
    def _():
        qkv_kernel(
            blk, ids, joined_ref, *inputs, x_ref, vec_ref, out_ref, w_ref, w_far_ref, v_ref, sems
        )

    @pl.when(step >= steps)
    def _():
        turn, pair, seq = attend_step(step - steps, out_ref.shape[2] // 384, seqs)
        length = o_ref.shape[1]
        view = joined_ref.at[
            pl.ds(turn, 1),
            pl.ds(pl.multiple_of(seq * length, length), length),
            pl.ds(pl.multiple_of(pair * 384, 128), 384),
        ]
        attend_kernel(head_dim, pair, seq, ids, view, *mask_refs, o_ref, lse_ref)


def attend_step(step, pairs, seqs):
    step = jnp.maximum(step, 0)
    return step // (pairs * seqs), step // seqs % pairs, step % seqs


def qkv_attend(ids, parts, pieces, cols, mask_parts, head_dim, ties=()):
    blk = len(parts)
    seqs, block_rows, width = parts[0].shape
    length = blk * block_rows
    tokens = seqs * length
    block = 2 * block_rows
    steps = tokens // block
    pairs = cols // 384
    piece = pieces[0][0]
    shape = place_shape(piece, cols)
    x_shape = jax.ShapeDtypeStruct((seqs, blk, block_rows, width), bf16)
    v_shape = jax.ShapeDtypeStruct((16, width), f32)

    def at(index):
        def found(i, ids):
            return index(ids, *attend_step(i - steps, pairs, seqs))

        return found

    mask = pl.BlockSpec(
        (2, block_rows, length), at(lambda ids, r, p, s: (2 * p + (ids[1] ^ r), 0, 0))
    )
    return kernel_call(
        partial(qkv_attend_kernel, blk, head_dim, steps, seqs),
        ids,
        [*mask_parts, *parts, *pieces[0], *pieces[1]],
        ties,
        (steps + 2 * pairs * seqs,),
        [mask] * blk + [any_block()] * (blk + 4),
        (
            whole_block(x_shape),
            whole_block(v_shape),
            pl.BlockSpec((2, block, cols), lambda i, ids: (0, jnp.minimum(i, steps - 1), 0)),
            pl.BlockSpec((1, length, 128), at(lambda ids, r, p, s: (r, s, p))),
            pl.BlockSpec((1, tokens, 128), at(lambda ids, r, p, s: (r, 0, 0))),
        ),
        (
            x_shape,
            v_shape,
            jax.ShapeDtypeStruct((2, tokens, cols), bf16),
            jax.ShapeDtypeStruct((2, tokens, cols // 3), bf16),
            jax.ShapeDtypeStruct((2, tokens, 128), f32),
        ),
        [
            shape,
            shape,
            place_shape(piece, 128),
            pltpu.VMEM((2, tokens, cols), bf16),
            pltpu.SemaphoreType.DMA((blk + 6,)),
        ],
    )


def attend_back(
    ids, joined, attended, upstream, logs, mask_parts, turn, seqs, head_dim, ties=()
):
    tokens, cols = joined.shape[1:]
    count = cols // 384
    length = tokens // seqs
    block, log_block, masks = attention_specs(joined, mask_parts, turn)
    return kernel_call(
        partial(attend_back_kernel, head_dim),
        ids,
        [joined, attended, upstream, logs, *mask_parts],
        ties,
        (1, count, seqs),
        [block(384), block(128), block(128), log_block] + masks,
        (
            pl.BlockSpec((1, length, 384), lambda r, p, s, ids: (0, s, p)),
            pl.BlockSpec((1, 1, 8, 384), lambda r, p, s, ids: (r, p, 0, 0)),
        ),
        (
            jax.ShapeDtypeStruct((1, tokens, cols), bf16),
            jax.ShapeDtypeStruct((1, count, 8, 384), f32),
        ),
    )


def out_kernel(ids, att_ref, x_ref, vec_ref, *refs):
    pieces, (first_ref, low_ref, w_ref, sems) = (refs[:2], refs[2:4]), refs[4:]

    @pl.when(pl.program_id(0) == 0)
    def _():
        load = Loader(ids, sems)
        half = w_ref.shape[-1] // 2
        load.columns(pieces, pieces[0][0].shape[-1] - half, half, w_ref)
        load.wait()

    attended = pair_order(ids[1], att_ref[0], att_ref[1], 128)
    first = x_ref[...].astype(f32) + (dot(attended, flat(w_ref)) + vector(vec_ref, "bias_out"))
    first_ref[...] = first
    gain, shift = vector(vec_ref, "gain_first"), vector(vec_ref, "shift_first")
    low_ref[...] = (norm_stats(first)[0] * gain + shift).astype(bf16)


def out_projection(ids, attended, pieces, token_rows, vectors, block, ties=()):
    tokens, width = token_rows.shape
    row = pl.BlockSpec((block, width), lambda i, ids: (i, 0))
    return kernel_call(
        out_kernel,
        ids,
        [attended, token_rows, vectors, *pieces[0], *pieces[1]],
        ties,
        (tokens // block,),
        [
            pl.BlockSpec((2, block, width // 2), lambda i, ids: (0, i, 0)),
            row,
            whole_block(vectors),
        ]
        + [any_block()] * 4,
        (row, row),
        (jax.ShapeDtypeStruct((tokens, width), f32), jax.ShapeDtypeStruct((tokens, width), bf16)),
        [place_shape(pieces[0][0], width), pltpu.SemaphoreType.DMA((4,))],
        cost=brief,
    )


def up_kernel(chunk, steps, ids, h_ref, b_ref, *refs):
    pieces, (act_ref, der_ref, w_ref, w_far_ref, sems) = (refs[:2], refs[2:4]), refs[4:]
    step = pl.program_id(0)
    block = act_ref.shape[1]
    cols = w_ref.shape[-1]

    @pl.when(step == 0)
    def _():
        load = Loader(ids, sems)
        start = pieces[0][0].shape[-1] - cols
        load.rows(pieces[0], start, cols, w_ref)
        load.rows(pieces[1], start, cols, w_far_ref)
        load.wait()

    def run(ref):
        lanes = pl.ds(pl.multiple_of((step % steps) * block, block), block)
        weights = ref[:, :, :, lanes].reshape(-1, block)
        bias = b_ref[0]
        for first in range(0, h_ref.shape[0], chunk):
            place_ = slice(first, first + chunk)
            gate = dot(h_ref[place_, :], weights) + bias
            share = 0.5 + 0.5 * lax.erf(gate * math.sqrt(0.5))
            bell = jnp.exp2((-0.5 * log2e) * (gate * gate)) * (1.0 / math.sqrt(2.0 * math.pi))
            act_ref[place_, :] = (gate * share).astype(bf16)
            der_ref[place_, :] = (share + gate * bell).astype(bf16)

    pl.when(step < steps)(lambda: run(w_ref))
    pl.when(step >= steps)(lambda: run(w_far_ref))


def up_projection(ids, hidden_low, pieces, bias, ties=()):
    tokens, width = hidden_low.shape
    half = bias.shape[2]
    block = width
    steps = half // block
    out = pl.BlockSpec((tokens, block), lambda j, ids: (0, (ids[1] ^ (j // steps)) * steps + j % steps))
    shape = jax.ShapeDtypeStruct((tokens, 2 * half), bf16)
    scratch = place_shape(pieces[0][0], half)
    return kernel_call(
        partial(up_kernel, 128, steps),
        ids,
        [hidden_low, bias, *pieces[0], *pieces[1]],
        ties,
        (2 * steps,),
        [
            whole_block(hidden_low),
            pl.BlockSpec((1, 1, block), lambda j, ids: (ids[1] ^ (j // steps), 0, j % steps)),
        ]
        + [any_block()] * 4,
        (out, out),
        (shape, shape),
        [scratch, scratch, pltpu.SemaphoreType.DMA((4,))],
        cost=brief,
    )


def down_kernel(blk, ids, *refs):
    pos_ref, cot_ref, act_ref, der_ref, first_ref, vec_ref = refs[:6]
    mine, other = refs[6:8], refs[8:10]
    outs, refs = refs[10 : 10 + blk], refs[10 + blk :]
    gss_ref, gdi_ref, gate_ref, sums_ref, up_ref, w_ref, product_ref, sems = refs
    step = pl.program_id(0)
    here = ids[0]
    seqs, rows, width = first_ref.shape
    cols = act_ref.shape[-1]

    def product():
        return dot(act_ref[...].reshape(-1, cols), flat(w_ref))

    def add_to(ref, parts):
        total = [jnp.sum(part, axis=0, keepdims=True) for part in parts]
        total.append(jnp.zeros((ref.shape[0] - len(parts), ref.shape[1]), f32))
        ref[...] = jnp.where(step == 1, 0.0, ref[...]) + jnp.concatenate(total, axis=0)

    def take_on(multiplied):
        normed_one = norm_stats(first_ref[...].reshape(-1, width))[0]
        hidden = normed_one * vector(vec_ref, "gain_first") + vector(vec_ref, "shift_first")
        normed, inverse = norm_stats(hidden + (multiplied + vector(vec_ref, "bias_down")))
        gain = vector(vec_ref, "gain_second")
        result = (normed * gain + vector(vec_ref, "shift_second")).astype(bf16)
        slots = pos_ref.shape[-1]
        token = lax.broadcasted_iota(jnp.int32, (rows, slots), 0) + (here ^ (step - 1)) * rows
        upstream = jnp.concatenate(
            [
                dot(jnp.where(token == pos_ref[seq], 1.0, 0.0).astype(bf16), cot_ref[seq])
                for seq in range(seqs)
            ],
            axis=0,
        )
        grad = norm_pull(upstream, normed, inverse, gain)
        gss_ref[...] = grad.reshape(gss_ref.shape)
        low = grad.astype(bf16)
        gdi_ref[...] = low.reshape(gdi_ref.shape)
        grad_gate = dot_right_t(low, flat(w_ref)) * der_ref[...].reshape(-1, cols).astype(f32)
        grad_gate = grad_gate.astype(bf16)
        gate_ref[...] = grad_gate.reshape(gate_ref.shape)
        add_to(sums_ref, [low.astype(f32), upstream * normed, upstream])
        add_to(up_ref, [grad_gate.astype(f32)])
        return result

    def keep(result):
        for piece, out in enumerate(outs):

            @pl.when(step == piece + 1)
            def _():
                out[...] = result.reshape(out.shape)

    @pl.when(step == 0)
    def _():
        load = Loader(ids, sems)
        load.columns((mine, other), 0, width // 2, w_ref)
        load.wait()
        product_ref[...] = product()

    @pl.when((step > 0) & (step < blk))
    def _():
        following = product()
        result = take_on(product_ref[...])
        product_ref[...] = following
        keep(result)

    @pl.when(step == blk)
    def _():
        keep(take_on(product_ref[...]))


def down_projection(
    ids, active, slope, first_sum, pieces, vectors, marks, cot_values, seqs, blk, ties=()
):
    tokens, cols = active.shape
    width = first_sum.shape[1]
    length = tokens // seqs
    rows = length // blk

    def ahead(size):
        return pl.BlockSpec(
            (seqs, rows, size), lambda d, ids: (0, ids[0] ^ jnp.minimum(d, blk - 1), 0)
        )

    def block(size):
        return pl.BlockSpec(
            (seqs, rows, size), lambda d, ids: (0, ids[0] ^ jnp.maximum(d - 1, 0), 0)
        )

    def shape(size, dtype):
        return jax.ShapeDtypeStruct((seqs, length, size), dtype)

    piece = jax.ShapeDtypeStruct((seqs, rows, width), bf16)
    sums = jax.ShapeDtypeStruct((8, width), f32)
    up_sums = jax.ShapeDtypeStruct((8, cols), f32)
    slots = marks.shape[-1]
    by_seq = [array.reshape(seqs, length, -1) for array in (active, slope, first_sum)]
    outs = kernel_call(
        partial(down_kernel, blk),
        ids,
        [marks, cot_values, *by_seq, vectors, *pieces[0], *pieces[1]],
        ties,
        (blk + 1,),
        [
            whole_block(marks),
            pl.BlockSpec((seqs, slots, width), lambda d, ids: (ids[0], 0, 0)),
            ahead(cols),
            block(cols),
            block(width),
            whole_block(vectors),
        ]
        + [any_block()] * 4,
        [whole_block(piece)] * blk
        + [block(width), block(width), block(cols), whole_block(sums), whole_block(up_sums)],
        [piece] * blk + [shape(width, f32), shape(width, bf16), shape(cols, bf16), sums, up_sums],
        [
            place_shape(pieces[0][0], width),
            pltpu.VMEM((seqs * rows, width), f32),
            pltpu.SemaphoreType.DMA((4,)),
        ],
    )
    rest = outs[blk:]
    return outs[:blk], [array.reshape(tokens, -1) for array in rest[:3]], rest[3:]


def first_back_kernel(steps, ids, gate_ref, gss_ref, first_ref, vec_ref, *refs):
    pieces, out_pieces, refs = (refs[:2], refs[2:4]), (refs[4:6], refs[6:8]), refs[8:]
    gfs_ref, branch_ref, att_ref, sums_ref, w_ref, w_out_ref, product_ref, sems = refs
    width = gss_ref.shape[1]
    step = pl.program_id(0)

    def product():
        return dot_right_t(gate_ref[...], flat(w_ref))

    def take_on(multiplied):
        grad_hidden = gss_ref[...] + multiplied
        normed, inverse = norm_stats(first_ref[...])
        grad = norm_pull(grad_hidden, normed, inverse, vector(vec_ref, "gain_first"))
        gfs_ref[...] = grad
        low = grad.astype(bf16)
        branch_ref[...] = low
        grad_att = dot_right_t(low, flat(w_out_ref)).astype(bf16)
        att_ref[0], att_ref[1] = pair_split(ids[1], grad_att, 128)
        total = [
            jnp.sum(part, axis=0, keepdims=True)
            for part in (low.astype(f32), grad_hidden * normed, grad_hidden)
        ]
        total.append(jnp.zeros((sums_ref.shape[0] - len(total), width), f32))
        sums_ref[...] = jnp.where(step == 1, 0.0, sums_ref[...]) + jnp.concatenate(total, axis=0)

    @pl.when(step == 0)
    def _():
        load = Loader(ids, sems)
        load.columns(pieces, 0, w_ref.shape[-1] // 2, w_ref)
        start = out_pieces[0][0].shape[-1] - width // 2
        load.columns(out_pieces, start, width // 2, w_out_ref)
        load.wait()
        product_ref[...] = product()

    @pl.when((step > 0) & (step < steps))
    def _():
        following = product()
        take_on(product_ref[...])
        product_ref[...] = following

    @pl.when(step == steps)
    def _():
        take_on(product_ref[...])


def first_back(
    ids, grad_gate, grad_second_sum, first_sum, pieces, out_pieces, vectors, block, ties=()
):
    tokens, cols = grad_gate.shape
    width = first_sum.shape[1]

    steps = tokens // block

    def ahead(size):
        return pl.BlockSpec((block, size), lambda i, ids: (jnp.minimum(i, steps - 1), 0))

    def row(size):
        return pl.BlockSpec((block, size), lambda i, ids: (jnp.maximum(i - 1, 0), 0))

    def shape(size, dtype):
        return jax.ShapeDtypeStruct((tokens, size), dtype)

    sums = jax.ShapeDtypeStruct((8, width), f32)
    piece = pieces[0][0]
    return kernel_call(
        partial(first_back_kernel, steps),
        ids,
        [
            grad_gate,
            grad_second_sum,
            first_sum,
            vectors,
            *pieces[0],
            *pieces[1],
            *out_pieces[0],
            *out_pieces[1],
        ],
        ties,
        (steps + 1,),
        [ahead(cols), row(width), row(width), whole_block(vectors)] + [any_block()] * 8,
        (
            row(width),
            row(width),
            pl.BlockSpec(
                (2, block, width // 2), lambda i, ids: (0, jnp.maximum(i - 1, 0), 0)
            ),
            whole_block(sums),
        ),
        (
            shape(width, f32),
            shape(width, bf16),
            jax.ShapeDtypeStruct((2, tokens, width // 2), bf16),
            sums,
        ),
        [
            place_shape(piece, cols),
            place_shape(piece, width),
            pltpu.VMEM((block, width), f32),
            pltpu.SemaphoreType.DMA((8,)),
        ],
    )


def beside(array, devices, per):
    groups = array.reshape(devices, per, -1, array.shape[-1])
    return jnp.concatenate(
        [groups[:, index].reshape(-1, array.shape[-1]) for index in range(per)], axis=1
    )


def down_grad_kernel(devices, per, ids, act_ref, g_ref, keep_ref, send_ref):
    halves = half_split(ids[1], dot_left_t(act_ref[...], g_ref[...]))
    for half, out in zip(halves, (keep_ref, send_ref)):
        out[...] = (beside(half, devices, per) if per > 1 else half).astype(bf16)


def down_grad(ids, active, grad_down_in, devices, ties=()):
    tokens, cols = active.shape
    width = grad_down_in.shape[1]
    per, block = cols // width, width
    inside = (width // devices) % 8 == 0
    groups = per if inside else 1
    out = pl.BlockSpec((block // groups, groups * width // 2), lambda i, ids: (i, 0))
    shape = jax.ShapeDtypeStruct((cols // groups, groups * width // 2), bf16)
    halves = kernel_call(
        partial(down_grad_kernel, devices // per, groups),
        ids,
        [active, grad_down_in],
        ties,
        (cols // block,),
        [pl.BlockSpec((tokens, block), lambda i, ids: (0, i)), whole_block(grad_down_in)],
        (out, out),
        (shape, shape),
    )
    return halves if inside else [beside(half, devices, per) for half in halves]


def up_grad_kernel(ids, h_ref, g_ref, g_far_ref, keep_ref, send_ref):
    keep_ref[...] = dot_left_t(h_ref[...], g_ref[...]).astype(bf16)
    send_ref[...] = dot_left_t(h_ref[...], g_far_ref[...]).astype(bf16)


def up_grad(ids, hidden_low, grad_gate, block, ties=()):
    tokens, width = hidden_low.shape
    cols = grad_gate.shape[1] // 2
    steps = cols // block
    shape = jax.ShapeDtypeStruct((width, cols), bf16)
    out = pl.BlockSpec((width, block), lambda j, ids: (0, j))
    return kernel_call(
        up_grad_kernel,
        ids,
        [hidden_low, grad_gate, grad_gate],
        ties,
        (steps,),
        [
            whole_block(hidden_low),
            pl.BlockSpec((tokens, block), lambda j, ids: (0, ids[1] * steps + j)),
            pl.BlockSpec((tokens, block), lambda j, ids: (0, (1 - ids[1]) * steps + j)),
        ],
        (out, out),
        (shape, shape),
    )


def left_grad_kernel(
    ids,
    x_ref,
    g_ref,
    g_far_ref,
    att_ref,
    branch_ref,
    sums_ref,
    sums_far_ref,
    first_ref,
    second_ref,
    up_ref,
    *outs,
):
    core, step = ids[1], pl.program_id(0)
    attended = pair_order(core, att_ref[0], att_ref[1], 128)
    out_grads = half_split(core, dot_left_t(attended, branch_ref[...]))
    sums = [ref[0, step][:1] for ref in (sums_ref, sums_far_ref)]
    rows = [
        pair_order(core, sums[0][:, at : at + 128], sums[1][:, at : at + 128], 128)
        for at in (0, 256)
    ]
    rows += [first_ref[:3], second_ref[:3], up_ref[...]]
    used = sum(row.shape[0] for row in rows)
    rows = jnp.concatenate(rows + [jnp.zeros((16 - used, rows[0].shape[1]), f32)], axis=0)
    lanes = lax.broadcasted_iota(jnp.int32, (16, 128), 1)
    eye = lanes == lax.broadcasted_iota(jnp.int32, lanes.shape, 0)
    columns = dot_left_t(rows.astype(bf16), jnp.where(eye, 1.0, 0.0).astype(bf16))
    cut = outs[0].shape[1] - 128
    for turn, ref in enumerate((g_ref, g_far_ref)):
        grad = dot_left_t(x_ref[...], ref[0])
        first = jnp.concatenate([grad[:, :cut], columns], axis=1)
        second = jnp.concatenate([grad[:, cut:], out_grads[turn]], axis=1)
        outs[turn][...] = first.astype(bf16)
        outs[2 + turn][...] = second.astype(bf16)


def left_grad(ids, left, grads, attended, grad_branch, sums, totals, ties=()):
    tokens, width = left.shape
    cut = grads[0].shape[2] - 384
    sizes = [cut + 128] * 2 + [384 + width // 2] * 2
    return kernel_call(
        left_grad_kernel,
        ids,
        [left, *grads, attended, grad_branch, *sums, *totals],
        ties,
        (width // 256,),
        [
            pl.BlockSpec((tokens, 256), lambda i, ids: (0, i)),
            *[whole_block(grad) for grad in grads],
            pl.BlockSpec((2, tokens, 128), lambda i, ids: (0, 0, i)),
            whole_block(grad_branch),
            *[whole_block(array) for array in sums],
        ]
        + [pl.BlockSpec((array.shape[0], 256), lambda i, ids: (0, i)) for array in totals],
        [pl.BlockSpec((256, size), lambda i, ids: (i, 0)) for size in sizes],
        [jax.ShapeDtypeStruct((width, size), bf16) for size in sizes],
    )


def input_grad_kernel(blk, ids, g_ref, g_far_ref, gfs_ref, *refs):
    pieces, refs = (refs[:2], refs[2:4]), refs[4:]
    outs, (w_ref, w_far_ref, sems) = refs[:blk], refs[blk:]
    step = pl.program_id(0)

    @pl.when(step == 0)
    def _():
        load = Loader(ids, sems)
        load.rows(pieces[0], 0, w_ref.shape[-1], w_ref)
        load.rows(pieces[1], 0, w_ref.shape[-1], w_far_ref)
        load.wait()

    width = gfs_ref.shape[-1]
    total = gfs_ref[...].reshape(-1, width)
    for ref, weights in ((g_ref, w_ref), (g_far_ref, w_far_ref)):
        total = total + dot_right_t(ref[...].reshape(-1, ref.shape[-1]), flat(weights))
    for piece, out in enumerate(outs):

        @pl.when(step == piece)
        def _():
            out[...] = total.astype(bf16).reshape(out.shape)


def input_grad(ids, grads, grad_first_sum, pieces, seqs, blk, ties=()):
    tokens, width = grad_first_sum.shape
    length = tokens // seqs
    rows = length // blk
    cols = grads[0].shape[2]
    piece = jax.ShapeDtypeStruct((seqs, rows, width), bf16)
    shape = place_shape(pieces[0][0], cols)
    pieces = [*pieces[0], *pieces[1]]
    return kernel_call(
        partial(input_grad_kernel, blk),
        ids,
        [
            *[grad.reshape(seqs, length, cols) for grad in grads],
            grad_first_sum.reshape(seqs, length, width),
            *pieces,
        ],
        ties,
        (blk,),
        [
            *[pl.BlockSpec((seqs, rows, cols), lambda d, ids: (0, ids[0] ^ d, 0))] * 2,
            pl.BlockSpec((seqs, rows, width), lambda d, ids: (0, ids[0] ^ d, 0)),
        ]
        + [any_block()] * len(pieces),
        [whole_block(piece)] * blk,
        [piece] * blk,
        [shape, shape, pltpu.SemaphoreType.DMA((len(pieces),))],
    )


class Grid:
    def __init__(self, mesh):
        batch, blk = mesh.shape["batch"], mesh.shape["blk"]
        self.sizes = {"z": batch // 2, "y": 2, "x": blk // 2, "c": 2}
        self.strides = {"c": 1, "x": 2, "y": blk, "z": 2 * blk}
        self.total = batch * blk
        self.blk = blk

    def digit(self, name):
        index = lax.axis_index("batch") * self.blk + lax.axis_index("blk")
        return (index // self.strides[name]) % self.sizes[name]

    def swap(self, array, name, delta=1):
        size, stride = self.sizes[name], self.strides[name]
        pairs = []
        for index in range(self.total):
            here = (index // stride) % size
            pairs.append((index, index + ((here ^ delta) - here) * stride))
        return lax.ppermute(array, both, pairs)

    def swap_blk(self, array, delta):
        pairs = [(index, index ^ delta) for index in range(self.total)]
        return lax.ppermute(array, both, pairs)


def place(parts, index):
    if len(parts) == 1:
        return parts[0][None]
    rows = []
    for target in range(len(parts)):
        row = parts[0]
        for delta in range(1, len(parts)):
            row = jnp.where(index == target ^ delta, parts[delta], row)
        rows.append(row)
    return jnp.stack(rows)


def pick(array, index):
    return lax.dynamic_index_in_dim(array, index, axis=0, keepdims=False)


def gather_core(grid, mine, other):
    cols = mine.shape[1]
    return place([mine, grid.swap(other, "c")], grid.digit("c")).reshape(-1, cols)


def gather_step(grid, run, held, name, *ties):
    parts = [grid.swap(held, name, d) for d in range(1, grid.sizes[name])]
    return place_parts(run, [held, *parts], name, ties)


def gather_last(grid, held, name):
    far = grid.swap(held, name)
    if held.shape[1] % 16 == 0:
        return [held, far]
    where = grid.digit(name)
    whole = jnp.moveaxis(place([held, far], where), 0, 1).reshape(4, 2, -1, held.shape[2])
    return [lax.dynamic_index_in_dim(whole, where ^ d, 1, keepdims=False) for d in range(2)]


def gather_pieces(grid, run, held, *ties):
    near, far = held
    if ties:
        (far,) = after(run, [far], *ties)
    return [[near, far], [grid.swap(near, "c"), grid.swap(far, "c")]]


def add_low(*parts):
    total = parts[0].astype(f32)
    for part in parts[1:]:
        total = total + part.astype(f32)
    return total


def fold_kernel(count, groups, ids, *refs):
    outs = refs[len(refs) - count :]
    refs = list(refs[: len(refs) - count])
    for out in outs:
        sums = []
        for terms in groups:
            picked, refs = refs[:terms], refs[terms:]
            total = picked[0][...].astype(f32)
            for ref in picked[1:]:
                total = total + ref[...].astype(f32)
            sums.append(total.astype(out.dtype))
        out[...] = jnp.concatenate(sums, axis=-1).reshape(out.shape)


def fold(ids, which, groups, ties):
    outer, count, rows, unused = groups[0][0].shape
    steps = 2 if outer % 2 == 0 else 1
    part = outer // steps

    def term_block(cols, delta):
        return pl.BlockSpec((part, 1, rows, cols), lambda i, ids: (i, ids[which] ^ delta, 0, 0))

    terms = [term for group in groups for term in group]
    cols = sum(group[0].shape[3] for group in groups)
    shape = jax.ShapeDtypeStruct((outer, rows, cols), bf16)
    return kernel_call(
        partial(fold_kernel, count, [len(group) for group in groups]),
        ids,
        [term for delta in range(count) for term in terms],
        ties,
        (steps,),
        [term_block(term.shape[3], delta) for delta in range(count) for term in terms],
        [pl.BlockSpec((part, rows, cols), lambda i, ids: (i, 0, 0))] * count,
        [shape] * count,
    )


class Scatter:
    def __init__(self, grid, ids, pairs, order):
        self.grid, self.ids, self.order = grid, ids, list(order)
        sizes = grid.sizes
        self.left = [("z", sizes["z"]), ("y", sizes["y"]), ("x", sizes["x"])]
        self.last = 2 * (pairs[0][0].shape[0] // grid.total)
        self.groups = [[keep, grid.swap(send, "c")] for keep, send in pairs]

    def join(self, other):
        self.groups = self.groups + other.groups
        return self

    def shaped(self, *shape):
        return [[term.reshape(*shape, term.shape[-1]) for term in group] for group in self.groups]

    def step(self, ties=()):
        name = self.order.pop(0)
        index = [left for left, unused in self.left].index(name)
        count = self.left[index][1]
        outer = math.prod(size for unused, size in self.left[:index])
        inner = math.prod(size for unused, size in self.left[index + 1 :]) * self.last
        sums = fold(self.ids, id_of[name], self.shaped(outer, count, inner), ties)
        self.left.pop(index)
        sent = [self.grid.swap(sums[delta], name, delta) for delta in range(1, count)]
        self.groups = [[sums[0], *sent]]

    def end(self, ties=()):
        mine, other = fold(self.ids, id_of["c"], self.shaped(1, 2, self.last // 2), ties)
        mine, other = [array.reshape(array.shape[1:]) for array in (mine, other)]
        return mine.astype(f32), self.grid.swap(other, "c").astype(f32)


def in_order(core, mine, other):
    return jnp.where(core == 0, mine, other), jnp.where(core == 0, other, mine)


def local(
    grid,
    inputs,
    w_qkv,
    bias_query,
    bias_value,
    w_out,
    bias_out,
    gain_first,
    shift_first,
    w_up,
    bias_up,
    w_down,
    bias_down,
    gain_second,
    shift_second,
    dam_mask,
    positions,
    counts,
    cot_values,
):
    groups, block_rows, width = inputs.shape
    head_count = dam_mask.shape[0]
    head_dim = width // head_count
    blk = grid.blk
    seqs = groups // blk
    length = blk * block_rows
    tokens = seqs * length
    here, core = lax.axis_index("blk"), grid.digit("c")
    ids = Run(jnp.stack([here, core] + [grid.digit(name) for name in "yzx"]).astype(jnp.int32))
    rows = w_qkv.shape[0]
    up_per = bias_up.shape[0] // rows
    half = width // 2
    pairs = width // 256

    vectors = (
        bias_query,
        bias_value,
        bias_out,
        gain_first,
        shift_first,
        bias_down,
        gain_second,
        shift_second,
    )
    stacked = jnp.concatenate(
        [
            jnp.stack(vectors),
            bias_up.reshape(rows, up_per).T,
            jnp.zeros((16 - len(vectors) - up_per, rows), bf16),
        ]
    )
    halves = split_weights(ids, w_qkv, stacked, w_out, w_up, w_down)
    first_near, second_near, down_near = [gather_core(grid, *pair) for pair in halves]

    def over_x(held):
        return gather_step(grid, ids, held, "x").reshape(-1, held.shape[1])

    first_near = over_x(first_near)
    event = ids.token

    by_home = inputs.reshape(blk, seqs, block_rows, width)
    parts = [pick(by_home, here ^ delta) for delta in range(blk)]
    parts[1:] = after(ids, parts[1:], event)
    parts[1:] = [grid.swap_blk(parts[delta], delta) for delta in range(1, blk)]
    addend = mask_addend(ids, dam_mask, [event])
    mask_parts = [addend, grid.swap(addend, "c")]
    second_near, down_near = after(ids, [second_near, down_near], event)
    second_near = over_x(second_near)
    ties = [ids.token]
    down_near = over_x(down_near)
    ties.append(ids.token)

    first_z = gather_step(grid, ids, first_near, "z", *ties, *parts[2:])
    (second_near,) = after(ids, [second_near], ids.token)
    first_y = gather_last(grid, first_z, "y")
    first_pieces = gather_pieces(grid, ids, first_y)
    ties = []
    if grid.sizes["x"] > 1:
        far = grid.swap(addend, "x")
        mask_parts += [far, grid.swap(far, "c")]
        ties = [far]
    second_z = gather_step(grid, ids, second_near, "z", *ties)
    (down_near,) = after(ids, [down_near], ids.token)
    second_y = gather_last(grid, second_z, "y")
    token_rows, vector_rows, joined, attended, logs = qkv_attend(
        ids, parts, first_pieces, 3 * half, mask_parts, head_dim, ties=[ids.token]
    )
    token_rows = token_rows.reshape(tokens, width)
    first_row = len(vectors)
    up_bias = vector_rows[first_row : first_row + up_per].T.reshape(2, 1, -1)
    down_z = gather_step(grid, ids, down_near, "z", ids.token)
    down_y = gather_last(grid, down_z, "y")
    second_pieces = gather_pieces(grid, ids, second_y, ids.token)
    first_sum, hidden_low = out_projection(
        ids, attended, first_pieces, token_rows, vector_rows, 2 * block_rows
    )
    active, slope = up_projection(ids, hidden_low, second_pieces, up_bias)
    down_pieces = gather_pieces(grid, ids, down_y, ids.token)

    my_positions = pick(positions.reshape(blk, seqs, -1), here)
    my_counts = pick(counts.reshape(blk, seqs), here)
    live = jnp.arange(positions.shape[1], dtype=jnp.int32)[None, :] < my_counts[:, None]
    marks = jnp.where(live, my_positions, -1)[:, None, :]
    result, (grad_second_sum, grad_down_in, grad_gate), (second_sums, up_sums) = down_projection(
        ids, active, slope, first_sum, down_pieces, vector_rows, marks, cot_values, seqs, blk
    )

    def home(pieces):
        return [pieces[0]] + [grid.swap_blk(pieces[delta], delta) for delta in range(1, blk)]

    result = home(result)
    down_halves = down_grad(ids, active, grad_down_in, grid.total)
    up_halves = up_grad(ids, hidden_low, grad_gate, width, ties=[ids.token])
    up_sum = Scatter(grid, ids, [up_halves], "yxz")
    ffn_sum = Scatter(grid, ids, [down_halves], "xyz")
    ffn_sum.step([ids.token])
    up_sum.step([ids.token])
    grad_first_sum, grad_branch, grad_attended, first_sums = first_back(
        ids,
        grad_gate,
        grad_second_sum,
        first_sum,
        second_pieces,
        first_pieces,
        vector_rows,
        2 * block_rows,
        ties=[ids.token],
    )
    result = after(ids, result, ids.token)
    def back(turn):
        return attend_back(
            ids,
            joined,
            attended,
            grad_attended,
            logs,
            mask_parts,
            turn,
            seqs,
            head_dim,
            ties=[ids.token],
        )

    far_grads, far_sums = back(1)
    ffn_sum.step([ids.token])
    up_sum.step([ids.token])
    near_grads, near_sums = back(0)
    grads, grad_sums = (near_grads, far_grads), (near_sums, far_sums)
    ffn_sum = up_sum.join(ffn_sum)
    ffn_sum.step([ids.token])
    up_rows = up_sums[0].reshape(width, up_per).T
    totals = [first_sums, second_sums, up_rows]
    halves = left_grad(
        ids, token_rows, grads, attended, grad_branch, grad_sums, totals, ties=[ids.token]
    )
    one_sum = Scatter(grid, ids, [halves[:2]], "xyz")
    two_sum = Scatter(grid, ids, [halves[2:]], "yxz")
    one_sum.step([ids.token])
    two_sum.step([ids.token])
    sent = input_grad(ids, grads, grad_first_sum, first_pieces, seqs, blk, ties=[ids.token])
    one_sum.step([ids.token])
    two_sum.step([ids.token])
    grad_inputs = home(sent)
    activations = place_parts(ids, result, "here", [ids.token])
    activations = activations.reshape(groups, block_rows, width)
    att_sum = one_sum.join(two_sum)
    att_sum.step([ids.token])
    share_ffn = ffn_sum.end([ids.token])
    share_att = att_sum.end([ids.token])
    grad_inputs = widen_parts(ids, grad_inputs, "here", [ids.token])
    grad_inputs = grad_inputs.reshape(groups, block_rows, width)

    cut = near_grads.shape[2] - 384
    share_qkv = [
        jnp.concatenate([share[:, :cut], share[:, cut + 128 : cut + 512]], axis=1)
        for share in share_att
    ]
    by_core = jnp.stack(in_order(core, *share_qkv), axis=0).reshape(2, rows, pairs, 3, 128)
    share_qkv = by_core.transpose(1, 3, 2, 0, 4).reshape(rows, 3 * width)
    share_out = jnp.concatenate(in_order(core, *[share[:, cut + 512 :] for share in share_att]), axis=1)
    up_cols = up_halves[0].shape[1]
    share_up = [share[:, :up_cols] for share in share_ffn]
    share_down = [
        share[:, up_cols:].reshape(rows, up_per, half).transpose(1, 0, 2).reshape(-1, half)
        for share in share_ffn
    ]
    shares = share_att[0][:, cut : cut + 128]
    share_vectors = [shares[:, index] for index in range(len(vectors))]
    share_bias_up = shares[:, len(vectors) : len(vectors) + up_per].reshape(-1)
    (
        share_bias_query,
        share_bias_value,
        share_bias_out,
        share_gain_first,
        share_shift_first,
        share_bias_down,
        share_gain_second,
        share_shift_second,
    ) = share_vectors
    return (
        activations,
        grad_inputs,
        share_qkv,
        share_bias_query,
        share_bias_value,
        share_out,
        share_bias_out,
        share_gain_first,
        share_shift_first,
        jnp.concatenate(in_order(core, *share_up), axis=1),
        share_bias_up,
        jnp.concatenate(in_order(core, *share_down), axis=1),
        share_bias_down,
        share_gain_second,
        share_shift_second,
    )


def solution(mesh):
    sharded = P(both)
    rows = P(both, None)
    whole = P("batch", "blk", None)
    return jax.shard_map(
        partial(local, Grid(mesh)),
        mesh=mesh,
        in_specs=(
            whole,
            rows,
            sharded,
            sharded,
            rows,
            sharded,
            sharded,
            sharded,
            rows,
            sharded,
            rows,
            sharded,
            sharded,
            sharded,
            P(None, "blk", None),
            P("batch", None),
            P("batch"),
            P("batch", None, None),
        ),
        out_specs=(
            whole,
            whole,
            rows,
            sharded,
            sharded,
            rows,
            sharded,
            sharded,
            sharded,
            rows,
            sharded,
            rows,
            sharded,
            sharded,
            sharded,
        ),
        check_vma=False,
    )
```
